128 devices in a mesh: sp: 4 (over z_lo, core), fsdp: 32 (over z_hi, x, y).
Axes of the slice: x: 4, y: 4, z: 4 (z_hi: 2, z_lo: 2; z = z_hi * 2 + z_lo), core: 2. Of those that a mesh axis runs over, the one named last changes fastest.
Arguments:
- hidden_in: bfloat16 [16384, 768], P(('fsdp', 'sp')), may hold values from -6 to 6
- qkv_weight: bfloat16 [768, 2304], P('fsdp'), may hold values from -0.3125 to 0.3125
- query_bias: bfloat16 [768], P('fsdp'), may hold values from -3 to 3
- value_bias: bfloat16 [768], P('fsdp'), may hold values from -3 to 3
- output_weight: bfloat16 [768, 768], P('fsdp'), may hold values from -1.75 to 1.75
- output_bias: bfloat16 [768], P('fsdp'), may hold values from -3 to 3
- first_gain: bfloat16 [768], P('fsdp'), may hold values from 0.25 to 1.75
- first_shift: bfloat16 [768], P('fsdp'), may hold values from -3 to 3
- up_weight: bfloat16 [768, 3072], P('fsdp'), may hold values from -0.21875 to 0.21875
- up_bias: bfloat16 [3072], P('fsdp'), may hold values from -3 to 3
- down_weight: bfloat16 [3072, 768], P('fsdp'), may hold values from -0.109375 to 0.109375
- down_bias: bfloat16 [768], P('fsdp'), may hold values from -3 to 3
- second_gain: bfloat16 [768], P('fsdp'), may hold values from 0.25 to 1.75
- second_shift: bfloat16 [768], P('fsdp'), may hold values from -3 to 3
- valid_length: int32 [1], replicated, may hold values from 16128 to 16384
- out_cotangent: bfloat16 [16384, 768], P(('fsdp', 'sp')), may hold values from -6 to 6
Outputs:
- output: bfloat16 [16384, 768], P(('fsdp', 'sp'))
- input_grad: float32 [16384, 768], P(('fsdp', 'sp'))
- qkv_weight_grad: float32 [768, 2304], P('fsdp')
- query_bias_grad: float32 [768], P('fsdp')
- value_bias_grad: float32 [768], P('fsdp')
- output_weight_grad: float32 [768, 768], P('fsdp')
- output_bias_grad: float32 [768], P('fsdp')
- first_gain_grad: float32 [768], P('fsdp')
- first_shift_grad: float32 [768], P('fsdp')
- up_weight_grad: float32 [768, 3072], P('fsdp')
- up_bias_grad: float32 [3072], P('fsdp')
- down_weight_grad: float32 [3072, 768], P('fsdp')
- down_bias_grad: float32 [768], P('fsdp')
- second_gain_grad: float32 [768], P('fsdp')
- second_shift_grad: float32 [768], P('fsdp')
The draws below stay inside these ranges and needn't reach their ends.
All inputs are finite; a program needn't handle non-finite values.
Results may differ from the reference program's by a relative error of at most 0.028.
Values may be sent and summed in bfloat16 or wider, within the bound.
A program may use at most 128 MiB of HBM per device.

```python
import math
import jax
import jax.numpy as jnp
from jax import lax

HEADS = 12
HEAD_DIM = 64
D = 768
FF = 3072
SEQS = 1
TOKENS = 16384
SEQ_LEN = 16384
N_FSDP = 32


def level_of(stream_key, shape, shards, least, largest):
    factor_of = 1.0
    for axis_at, shards_of in shards:
        heights = jax.random.uniform(jax.random.fold_in(jax.random.fold_in(stream_key, 6), axis_at), (shards_of,), jnp.float32, least / len(shards), largest / len(shards))
        factor_of = factor_of * jnp.repeat(jnp.exp(heights), shape[axis_at] // shards_of).reshape((-1,) + (1,) * (len(shape) - 1 - axis_at))
    return factor_of


def noise(stream_key, dims, spread, reach, cuts=(), kind=jnp.bfloat16):
    values = spread * jax.random.normal(stream_key, dims, jnp.float32)
    if cuts:
        values = values * level_of(stream_key, dims, cuts, -0.22, 0.18)
    return jnp.clip(values, -reach, reach).astype(kind)


def setup_inputs(seed: int = 0) -> dict:
    key_list = jax.random.split(jax.random.key(seed), 17)
    return {
        "hidden_in": noise(key_list[0], (TOKENS, D), 1.0, 6.0, ((0, 128),)),
        "qkv_weight": noise(key_list[1], (D, 3 * D), (D // 2) ** -0.5, 0.3125, ((0, 32),)),
        "query_bias": noise(key_list[2], (D,), 0.5, 3.0, ((0, 32),)),
        "value_bias": noise(key_list[3], (D,), 0.5, 3.0, ((0, 32),)),
        "output_weight": noise(key_list[4], (D, D), (max(4, D * 256 // SEQ_LEN)) ** -0.5, 1.75, ((0, 32),)),
        "output_bias": noise(key_list[5], (D,), 0.5, 3.0, ((0, 32),)),
        "first_gain": jnp.clip(1.0 + 0.15 * jax.random.normal(key_list[6], (D,), jnp.float32), 0.25, 1.75).astype(jnp.bfloat16),
        "first_shift": noise(key_list[7], (D,), 0.5, 3.0, ((0, 32),)),
        "up_weight": noise(key_list[8], (D, FF), D ** -0.5, 0.21875, ((0, 32),)),
        "up_bias": noise(key_list[9], (FF,), 0.5, 3.0, ((0, 32),)),
        "down_weight": noise(key_list[10], (FF, D), FF ** -0.5, 0.109375, ((0, 32),)),
        "down_bias": noise(key_list[11], (D,), 0.5, 3.0, ((0, 32),)),
        "second_gain": jnp.clip(1.0 + 0.15 * jax.random.normal(key_list[12], (D,), jnp.float32), 0.25, 1.75).astype(jnp.bfloat16),
        "second_shift": noise(key_list[13], (D,), 0.5, 3.0, ((0, 32),)),
        "valid_length": jax.random.randint(key_list[14], (SEQS,), SEQ_LEN - SEQ_LEN // (2 * N_FSDP), SEQ_LEN + 1).astype(jnp.int32),
        "out_cotangent": noise(key_list[15], (TOKENS, D), 1.0, 6.0, ((0, 128),)),
    }


@jax.custom_vjp
def low(v):
    return lax.optimization_barrier(v.astype(jnp.bfloat16)).astype(jnp.float32)

@jax.custom_vjp
def low_back(v):
    return v

def low_keep(v):
    return (low(v), None)

def low_pass(kept, grad):
    return (grad,)

def back_keep(v):
    return (v, None)

def back_low(kept, grad):
    return (low(grad),)
low.defvjp(low_keep, low_pass)
low_back.defvjp(back_keep, back_low)
epsilon = 1e-05
masked = -1e+30

def matmul(left_side, right_side):
    return jnp.dot(left_side, right_side, precision=lax.Precision.HIGHEST, preferred_element_type=jnp.float32)

def layer_norm(incoming, norm_gain, norm_shift):
    row_mean = lax.optimization_barrier(jnp.mean(incoming, axis=-1, keepdims=True))
    centered = incoming - row_mean
    variance = lax.optimization_barrier(jnp.mean(centered * centered, axis=-1, keepdims=True))
    return centered * lax.rsqrt(variance + epsilon) * norm_gain + norm_shift

def forward(hidden, qkv_weight, query_bias, value_bias, output_weight, output_bias, first_gain, first_shift, up_weight, up_bias, down_weight, down_bias, second_gain, second_shift, valid_limits):
    total_rows = hidden.shape[0]
    projected = matmul(hidden, qkv_weight)
    query_rows = low_back(low(projected[:, :D] + query_bias)).reshape(total_rows, HEADS, HEAD_DIM)
    key_rows = low_back(low(projected[:, D:2 * D])).reshape(total_rows, HEADS, HEAD_DIM)
    value_rows = low_back(low(projected[:, 2 * D:] + value_bias)).reshape(total_rows, HEADS, HEAD_DIM)
    key_index = jnp.arange(total_rows, dtype=jnp.int32)
    key_seq = key_index // SEQ_LEN
    key_valid = key_index - key_seq * SEQ_LEN < valid_limits[key_seq]
    block_size = math.gcd(total_rows, 512)
    block_count = total_rows // block_size

    def attend(block_item):
        query_block, start = block_item
        query_seq = (start + jnp.arange(block_size, dtype=jnp.int32)) // SEQ_LEN
        allowed = (query_seq[:, None] == key_seq[None, :]) & key_valid[None, :]
        scores = jnp.einsum('rhd,khd->hrk', query_block, key_rows, precision=lax.Precision.HIGHEST) * 0.125
        scores = jnp.where(allowed[None, :, :], low_back(scores), masked)
        exponent = jnp.exp(scores - lax.optimization_barrier(jnp.max(scores, axis=-1, keepdims=True)))
        weights = low(exponent / lax.optimization_barrier(jnp.sum(exponent, axis=-1, keepdims=True)))
        return jnp.einsum('hrk,khd->rhd', weights, value_rows, precision=lax.Precision.HIGHEST)
    blocks = query_rows.reshape(block_count, block_size, HEADS, HEAD_DIM)
    starts = jnp.arange(block_count, dtype=jnp.int32) * block_size
    attended = lax.map(jax.checkpoint(attend), (blocks, starts))
    attended = low_back(low(attended.reshape(total_rows, D)))
    branch_one = low_back(matmul(attended, output_weight) + output_bias)
    first = layer_norm(hidden + branch_one, first_gain, first_shift)
    pre_active = low_back(matmul(low(first), up_weight) + up_bias)
    active = low(jax.nn.gelu(pre_active, approximate=False))
    branch_two = low_back(matmul(active, down_weight) + down_bias)
    return layer_norm(first + branch_two, second_gain, second_shift)

def reference(hidden_in, qkv_weight, query_bias, value_bias, output_weight, output_bias, first_gain, first_shift, up_weight, up_bias, down_weight, down_bias, second_gain, second_shift, valid_length, out_cotangent):
    params = (hidden_in, qkv_weight, query_bias, value_bias, output_weight, output_bias, first_gain, first_shift, up_weight, up_bias, down_weight, down_bias, second_gain, second_shift)
    floats = tuple((param.astype(jnp.float32) for param in params))
    valid_limits = valid_length.astype(jnp.int32)

    def forward_call(*inputs):
        return forward(*inputs, valid_limits)
    result, pullback = jax.vjp(forward_call, *floats)
    gradients = pullback(out_cotangent.astype(jnp.float32))
    return (result.astype(jnp.bfloat16), gradients[0], gradients[1], gradients[2], gradients[3], gradients[4], gradients[5], gradients[6], gradients[7], gradients[8], gradients[9], gradients[10], gradients[11], gradients[12], gradients[13])
```

```python
import functools

import jax
import jax.numpy as jnp
from jax import lax
from jax.experimental import pallas as pl
from jax.experimental.pallas import tpu as pltpu
from jax.sharding import PartitionSpec as P

HEADS = 12
HEAD_DIM = 64
SP = 4
FS = 32
YG = 4
XG = 8
LH = HEADS // SP

BF = jnp.bfloat16
F32 = jnp.float32
MESH = pl.DeviceIdType.MESH
epsilon = 1e-05
masked = -1e30
VMEM_LIMIT = 56 * 1024 * 1024


def dot_nn(a, b):
    return lax.dot_general(a, b, (((1,), (0,)), ((), ())), preferred_element_type=F32)


def dot_nt(a, b):
    return lax.dot_general(a, b, (((1,), (1,)), ((), ())), preferred_element_type=F32)


def dot_tn(a, b):
    return lax.dot_general(a, b, (((0,), (0,)), ((), ())), preferred_element_type=F32)


def norm_forward(incoming, norm_gain, norm_shift):
    row_mean = jnp.mean(incoming, axis=-1, keepdims=True)
    centered = incoming - row_mean
    inverse = lax.rsqrt(jnp.mean(centered * centered, axis=-1, keepdims=True) + epsilon)
    normed = centered * inverse
    return (normed * norm_gain + norm_shift, normed, inverse)


def norm_backward(incoming, normed, inverse, norm_gain):
    scaled = incoming * norm_gain
    adjusted = (
        scaled
        - jnp.mean(scaled, axis=-1, keepdims=True)
        - normed * jnp.mean(scaled * normed, axis=-1, keepdims=True)
    )
    return (
        adjusted * inverse,
        jnp.sum(incoming * normed, axis=0, keepdims=True),
        jnp.sum(incoming, axis=0, keepdims=True),
    )


def loop(low, high, body):
    def step(d, carried):
        body(d)
        return carried

    lax.fori_loop(low, high, step, 0)


def remote(src, dst, send, recv, **device):
    return pltpu.make_async_remote_copy(
        src_ref=src,
        dst_ref=dst,
        send_sem=send,
        recv_sem=recv,
        device_id=device,
        device_id_type=MESH,
    )


def greet(barrier, **device):
    pl.semaphore_signal(barrier, inc=1, device_id=device, device_id_type=MESH)


def greet_all(f, s):
    barrier = pltpu.get_barrier_semaphore()
    loop(1, FS, lambda d: greet(barrier, fsdp=lax.rem(f + d, FS)))
    loop(1, SP, lambda d: greet(barrier, sp=lax.rem(s + d, SP)))
    pl.semaphore_wait(barrier, FS - 1 + SP - 1)


def project_kernel(
    hid, wq, up, down, out, small,
    hid_all, wqkv, q_all, kv_all, up_g, down_g, out_g, vecs,
    wq_g, small_g, wf, q_st, kv_st, qvb,
    hid_s, hid_r, wq_s, wq_r, up_s, up_r, dn_s, dn_r, ou_s, ou_r, sm_s, sm_r,
    q_s, q_r, kv_s, kv_r, loc,
):
    s = lax.axis_index("sp")
    f = lax.axis_index("fsdp")
    i, j = f // YG, lax.rem(f, YG)
    owner = s == f // 8
    greet_all(f, s)
    rows = hid.shape[0]

    def hid_copy(d):
        dst = hid_all.at[pl.ds(s * rows, rows)]
        return remote(hid, dst, hid_s.at[d - 1], hid_r.at[d - 1], sp=lax.rem(s + d, SP))

    def fs_copy(src, buf, send, recv):
        return lambda d: remote(
            src, buf.at[f], send.at[d - 1], recv.at[d - 1], fsdp=lax.rem(f + d, FS)
        )

    wq_copy = fs_copy(wq, wq_g, wq_s, wq_r)
    small_copy = fs_copy(small, small_g, sm_s, sm_r)
    up_copy = fs_copy(up, up_g, up_s, up_r)

    def down_copy(d):
        k = lax.rem(f, 8)
        return remote(down, down_g.at[k], dn_s.at[d - 1], dn_r.at[k], fsdp=lax.rem(f + d, FS))

    def out_copy(d):
        k = lax.rem(f, 8)
        return remote(out, out_g.at[k], ou_s.at[d - 1], ou_r.at[k], fsdp=lax.rem(f + d, FS))

    loop(1, SP, lambda d: hid_copy(d).start())

    def first_sends(d):
        wq_copy(d).start()
        small_copy(d).start()

    loop(1, FS, first_sends)
    hid_all[pl.ds(pl.multiple_of(s * rows, rows), rows), :] = hid[...]
    wq_g[f] = wq[...]
    small_g[f] = small[...]
    up_own = pltpu.make_async_copy(up, up_g.at[f], loc.at[0])
    up_own.start()

    loop(1, SP, lambda d: hid_copy(d).wait())

    def first_waits(d):
        wq_copy(d).wait()
        small_copy(d).wait()

    loop(1, FS, first_waits)

    width = vecs.shape[1]
    total = jnp.zeros((8, width), F32)
    pad = jnp.zeros((8, width - 128), F32)
    for n in range(FS):
        piece = small_g[n][0:8].astype(F32)
        wide = jnp.concatenate((piece, pad), axis=1)
        total = total + (wide if n == 0 else pltpu.roll(wide, 24 * n, 1))
    vecs[0:8, :] = total
    ub = jnp.zeros((8, width), F32)
    qv = jnp.zeros((8, width), F32)
    for k in range(8):
        block = small_g[8 * s + k].astype(F32)
        ub_wide = jnp.concatenate((block[8:16], pad), axis=1)
        qv_wide = jnp.concatenate((block[0:8], pad), axis=1)
        ub = ub + (ub_wide if k == 0 else pltpu.roll(ub_wide, 96 * k, 1))
        qv = qv + (qv_wide if k == 0 else pltpu.roll(qv_wide, 24 * k, 1))
    vecs[8:16, :] = ub
    qvb[...] = qv
    lane = lax.broadcasted_iota(jnp.int32, (1, width), 1)
    qrow = qvb[0:1, :]
    vrow = qvb[1:2, :]
    bias = jnp.zeros((1, width), F32)
    wide_q = jnp.broadcast_to(qrow, (8, width))
    wide_v = jnp.broadcast_to(vrow, (8, width))
    bias = jnp.where((lane >= 384) & (lane < 576), pltpu.roll(wide_q, 384, 1)[0:1], 0.0)
    for h in range(LH):
        here = (lane >= 128 * h + 64) & (lane < 128 * h + 128)
        bias = bias + jnp.where(here, pltpu.roll(wide_v, 64 * h + 64, 1)[0:1], 0.0)

    def assemble(n):
        wf[pl.ds(pl.multiple_of(24 * n, 8), 24), :] = wq_g[n].astype(F32)

    loop(0, FS, assemble)
    wqkv[...] = wf[...].astype(BF)

    low_lane = lax.broadcasted_iota(jnp.int32, (rows, 128), 1) < HEAD_DIM

    def project(b):
        at = pl.ds(pl.multiple_of(b * rows, rows), rows)
        p = dot_nn(hid_all[at, :], wqkv[...]) + bias[:, :576]
        for h in range(LH):
            kv_st[h, at, :] = p[:, 128 * h : 128 * h + 128].astype(BF)
        q01 = p[:, 384:512] * 0.125
        q2 = jnp.concatenate((p[:, 512:576], jnp.zeros((rows, 64), F32)), axis=1) * 0.125
        q_st[0, at, :] = jnp.where(low_lane, q01, 0.0).astype(BF)
        q_st[1, at, :] = jnp.where(low_lane, pltpu.roll(q01, 64, 1), 0.0).astype(BF)
        q_st[2, at, :] = q2.astype(BF)

    loop(0, SP, project)

    def kv_copy(d):
        to = lax.rem(i + d, XG) * YG + j
        return remote(kv_st, kv_all.at[i], kv_s.at[d - 1], kv_r.at[d - 1], fsdp=to)

    def q_copy(d):
        to = i * YG + lax.rem(j + d, YG)
        return remote(q_st, q_all.at[j], q_s.at[d - 1], q_r.at[d - 1], fsdp=to)

    loop(1, XG, lambda d: kv_copy(d).start())
    loop(1, YG, lambda d: q_copy(d).start())
    kv_own = pltpu.make_async_copy(kv_st, kv_all.at[i], loc.at[1])
    q_own = pltpu.make_async_copy(q_st, q_all.at[j], loc.at[2])
    kv_own.start()
    q_own.start()
    loop(1, FS, lambda d: up_copy(d).start())

    @pl.when(owner)
    def _():
        def both(d):
            down_copy(d).start()
            out_copy(d).start()

        loop(1, FS, both)
        dn_own = pltpu.make_async_copy(down, down_g.at[lax.rem(f, 8)], loc.at[3])
        ou_own = pltpu.make_async_copy(out, out_g.at[lax.rem(f, 8)], loc.at[4])
        dn_own.start()
        ou_own.start()
        dn_own.wait()
        ou_own.wait()

    kv_own.wait()
    q_own.wait()
    up_own.wait()
    loop(1, XG, lambda d: kv_copy(d).wait())
    loop(1, YG, lambda d: q_copy(d).wait())
    loop(1, FS, lambda d: up_copy(d).wait())

    @pl.when(owner)
    def _():
        def both(d):
            down_copy(d).wait_send()
            out_copy(d).wait_send()

        loop(1, FS, both)

    def arrivals(k):
        @pl.when(8 * s + k != f)
        def _():
            other = lax.rem(f + 1, FS)
            remote(down, down_g.at[k], dn_s.at[0], dn_r.at[k], fsdp=other).wait_recv()
            remote(out, out_g.at[k], ou_s.at[0], ou_r.at[k], fsdp=other).wait_recv()

    loop(0, 8, arrivals)


def attend_kernel(valid, q, kv, o):
    rows = q.shape[2]
    keys = kv.shape[2]
    f = lax.axis_index("fsdp")
    first_key = ((XG - 1) * YG + lax.rem(f, YG)) * keys
    query = q[0, 0]
    m = l = acc = None
    for c in range(XG):
        block = kv[c, 0]
        scores = dot_nt(query, block)
        if c == XG - 1:
            place = first_key + lax.broadcasted_iota(jnp.int32, (1, keys), 1)
            scores = jnp.where(place < valid[0], scores, masked)
        top = jnp.max(scores, axis=1, keepdims=True)
        new = top if c == 0 else jnp.maximum(m, top)
        p = jnp.exp(scores - new)
        part = jnp.sum(p, axis=1, keepdims=True)
        weighted = dot_nn(p.astype(BF), block)
        if c == 0:
            l, acc = part, weighted
        else:
            decay = jnp.exp(m - new)
            l = l * decay + part
            acc = acc * decay + weighted
        m = new
    log_sum = m + jnp.log(l)
    high = log_sum.astype(BF).astype(F32)
    lane = lax.broadcasted_iota(jnp.int32, (rows, 128), 1)
    result = jnp.where(lane >= 64, acc / l, jnp.where(lane < 32, high, log_sum - high))
    o[0, 0] = result.astype(BF)


def middle_kernel(
    o_part, wo, wup, wdn, vecs, hid, cot,
    result, gfs, d_all, ld_all, dup, ddn, dwo, vp,
    o_rb, att, ld, st, own, first, n1, inv1, x_all, act, deriv, gd, gp, gb, gsec, rb, dbuf, ldrow, vg,
    o_s, o_r, ag_s, ag_r, rs_s, rs_r, d_s, d_r, l_s, l_r, loc,
):
    s = lax.axis_index("sp")
    f = lax.axis_index("fsdp")
    i, j = f // YG, lax.rem(f, YG)
    rows = hid.shape[0]
    tall = SP * rows
    barrier = pltpu.get_barrier_semaphore()
    loop(1, YG, lambda d: greet(barrier, fsdp=i * YG + lax.rem(j + d, YG)))
    loop(1, SP, lambda d: greet(barrier, sp=lax.rem(s + d, SP)))
    pl.semaphore_wait(barrier, YG - 1 + SP - 1)

    def y_peer(d):
        return i * YG + lax.rem(j + d, YG)

    def o_copy(d):
        src = o_part.at[lax.rem(j + d, YG)]
        return remote(src, o_rb.at[d - 1], o_s.at[d - 1], o_r.at[d - 1], fsdp=y_peer(d))

    loop(1, YG, lambda d: o_copy(d).start())
    loop(1, YG, lambda d: o_copy(d).wait())

    def span(b):
        return pl.ds(pl.multiple_of(b * rows, rows), rows)

    lane = lax.broadcasted_iota(jnp.int32, (rows, 128), 1)

    def merge(b):
        at = span(b)
        sums = jnp.zeros((rows, 128), F32)
        for h in range(LH):
            parts = [o_part[j, h, at, :].astype(F32)]
            parts += [o_rb[d, h, at, :].astype(F32) for d in range(YG - 1)]
            logs = [p[:, 0:1] + p[:, 32:33] for p in parts]
            top = functools.reduce(jnp.maximum, logs)
            weights = [jnp.exp(g - top) for g in logs]
            total = functools.reduce(jnp.add, weights)
            merged = functools.reduce(jnp.add, [p * w for p, w in zip(parts, weights)]) / total
            att[at, 128 * h : 128 * h + 128] = jnp.where(lane >= 64, merged, 0.0).astype(BF)
            sums = jnp.where(lane == 2 * h, top + jnp.log(total), sums)
        ld[at, :] = sums

    loop(0, SP, merge)

    def gather(e, buf):
        def copy(d):
            at = buf.at[pl.ds(s * rows, rows)]
            return remote(at, at, ag_s.at[e, d - 1], ag_r.at[e, d - 1], sp=lax.rem(s + d, SP))

        return copy

    def scatter(e):
        def copy(d):
            src = st.at[e, pl.ds(lax.rem(s + d, SP) * rows, rows)]
            sems = (rs_s.at[e, d - 1], rs_r.at[e, d - 1])
            return remote(src, rb.at[e, d - 1], *sems, sp=lax.rem(s + d, SP))

        return copy

    def collect(e):
        loop(1, SP, lambda d: scatter(e)(d).wait())
        total = own[...]
        for d in range(SP - 1):
            total = total + rb[e, d].astype(F32)
        return total

    def out_part(d):
        b = lax.rem(s + d, SP)
        value = dot_nn(att[span(b), :], wo[...])

        @pl.when(d < SP)
        def _():
            st[0, span(b), :] = value.astype(BF)
            scatter(0)(d).start()

        @pl.when(d == SP)
        def _():
            own[...] = value

    loop(1, SP + 1, out_part)
    summed = hid[...].astype(F32) + collect(0) + vecs[2:3, :]
    value, normed, inverse = norm_forward(summed, vecs[3:4, :], vecs[4:5, :])
    first[...] = value
    n1[...] = normed
    inv1[...] = jnp.broadcast_to(inverse, inv1.shape)
    x_all[span(s), :] = value.astype(BF)
    loop(1, SP, lambda d: gather(0, x_all)(d).start())

    def pipeline(e, buf, work):
        def step(d):
            b = lax.rem(s + SP - d, SP)

            @pl.when(d > 0)
            def _():
                gather(e, buf)(d).wait_recv()

            value = work(b)

            @pl.when(d > 0)
            def _():
                st[e + 1, span(b), :] = value.astype(BF)
                scatter(e + 1)(SP - d).start()

            @pl.when(d == 0)
            def _():
                own[...] = value

        loop(0, SP, step)
        loop(1, SP, lambda d: gather(e, buf)(d).wait_send())

    def feed(b):
        at = span(b)
        pre = dot_nn(x_all[at, :], wup[...]) + vecs[8:9, :]
        cdf = 0.5 * (1.0 + lax.erf(pre * 0.7071067811865476))
        density = jnp.exp(-0.5 * pre * pre) * 0.3989422804014327
        active = (pre * cdf).astype(BF)
        act[at, :] = active
        deriv[at, :] = cdf + pre * density
        return dot_nn(active, wdn[...])

    pipeline(0, x_all, feed)
    summed = first[...] + collect(1) + vecs[5:6, :]
    value, normed, inverse = norm_forward(summed, vecs[6:7, :], vecs[7:8, :])
    result[...] = value.astype(BF)
    grad, ggain, gshift = norm_backward(cot[...].astype(F32), normed, inverse, vecs[6:7, :])
    gsec[...] = grad
    low = grad.astype(BF)
    gd[span(s), :] = low
    loop(1, SP, lambda d: gather(1, gd)(d).start())
    vg[...] = jnp.zeros(vg.shape, F32)
    vg[3:4, :] = jnp.sum(low.astype(F32), axis=0, keepdims=True)
    vg[4:5, :] = ggain
    vg[5:6, :] = gshift

    def back(b):
        at = span(b)
        grad_pre = (dot_nt(gd[at, :], wdn[...]) * deriv[at, :]).astype(BF)
        gp[at, :] = grad_pre
        return dot_nt(grad_pre, wup[...])

    pipeline(1, gd, back)

    def weight_terms(c):
        at = pl.ds(pl.multiple_of(128 * c, 128), 128)
        ddn[at, :] = dot_tn(act[:, at], gd[...]).astype(BF)
        dup[at, :] = dot_tn(x_all[:, at], gp[...]).astype(BF)

    loop(0, act.shape[1] // 128, weight_terms)
    ub = jnp.sum(gp[...].astype(F32), axis=0, keepdims=True)
    grad_first = gsec[...] + collect(2)
    grad, ggain, gshift = norm_backward(grad_first, n1[...], inv1[:, 0:1], vecs[3:4, :])
    gfs[...] = grad
    low = grad.astype(BF)
    gb[span(s), :] = low
    loop(1, SP, lambda d: gather(2, gb)(d).start())
    vg[0:1, :] = jnp.sum(low.astype(F32), axis=0, keepdims=True)
    vg[1:2, :] = ggain
    vg[2:3, :] = gshift

    def branch(d):
        b = lax.rem(s + SP - d, SP)
        at = span(b)

        @pl.when(d > 0)
        def _():
            gather(2, gb)(d).wait_recv()

        value = dot_nt(gb[at, :], wo[...]).astype(BF)
        sums = ld[at, :]
        for h in range(LH):
            part = value[:, 128 * h : 128 * h + 128]
            dbuf[h, at, :] = part
            product = part.astype(F32) * att[at, 128 * h : 128 * h + 128].astype(F32)
            sums = jnp.where(lane == 2 * h + 1, jnp.sum(product, axis=1, keepdims=True), sums)
        ld[at, :] = sums

    loop(0, SP, branch)
    loop(1, SP, lambda d: gather(2, gb)(d).wait_send())
    ldrow[...] = jnp.transpose(ld[...], (1, 0))[0:8, :]

    def d_copy(d):
        return remote(dbuf, d_all.at[j], d_s.at[d - 1], d_r.at[d - 1], fsdp=y_peer(d))

    def l_copy(d):
        return remote(ldrow, ld_all.at[j], l_s.at[d - 1], l_r.at[d - 1], fsdp=y_peer(d))

    loop(1, YG, lambda d: d_copy(d).start())
    loop(1, YG, lambda d: l_copy(d).start())
    d_own = pltpu.make_async_copy(dbuf, d_all.at[j], loc.at[0])
    l_own = pltpu.make_async_copy(ldrow, ld_all.at[j], loc.at[1])
    d_own.start()
    l_own.start()
    for h in range(LH):
        value = dot_tn(att[:, 128 * h : 128 * h + 128], gb[...])
        dwo[64 * h : 64 * h + 64, :] = value[64:128].astype(BF)
    lane8 = lax.broadcasted_iota(jnp.int32, (8, 128), 1)
    wide = vg[...]
    width = wide.shape[1]
    ub_wide = jnp.broadcast_to(ub, (8, width))
    for n in range(FS):
        piece = wide if n == 0 else pltpu.roll(wide, width - 24 * n, 1)
        vp[n, 0:8, :] = jnp.where(lane8 < 24, piece[:, 0:128], 0.0)
        vp[n, 8:16, :] = jnp.zeros((8, 128), F32)
    for k in range(8):
        piece = ub_wide if k == 0 else pltpu.roll(ub_wide, width - 96 * k, 1)
        vp[8 * s + k, 8:16, :] = jnp.where(lane8 < 96, piece[:, 0:128], 0.0)
    d_own.wait()
    l_own.wait()
    loop(1, YG, lambda d: d_copy(d).wait())
    loop(1, YG, lambda d: l_copy(d).wait())


def attend_back_kernel(valid, q, dout, ld, kv, dkv, dq, acc):
    h = pl.program_id(0)
    step = pl.program_id(1)
    keys = kv.shape[2]
    f = lax.axis_index("fsdp")
    first_key = (step * YG + lax.rem(f, YG)) * keys

    @pl.when(step == 0)
    def _():
        acc[...] = jnp.zeros(acc.shape, F32)

    def work(last):
        block = kv[0, 0]
        flipped = jnp.transpose(block.astype(F32), (1, 0))[0:HEAD_DIM].astype(BF)
        total = None
        for n in range(YG):
            query = q[n, 0]
            grad = dout[n, 0]
            log_sum = ld[n, pl.ds(2 * h, 1), :]
            delta = ld[n, pl.ds(2 * h + 1, 1), :]
            scores = dot_nt(block, query)
            if last:
                place = first_key + lax.broadcasted_iota(jnp.int32, (keys, 1), 0)
                scores = jnp.where(place < valid[0], scores, masked)
            p = jnp.exp(scores - log_sum)
            grad_p = dot_nt(block, grad)
            grad_s = (p * (grad_p - delta)).astype(BF)
            terms = dot_nn(grad_s, query) + dot_nn(p.astype(BF), grad)
            total = terms if n == 0 else total + terms
            acc[n] = acc[n] + dot_nn(flipped, grad_s)
        dkv[0, 0] = total.astype(BF)

    @pl.when(step < XG - 1)
    def _():
        work(False)

    @pl.when(step == XG - 1)
    def _():
        work(True)
        dq[:, 0] = acc[...].astype(BF)


def finish_kernel(
    dkv, dq, hid_all, wqkv, gfs, dup, ddn, dwo, vp,
    input_grad, qkvg, upg, dng, outg, vecg, qvg,
    kv_rb, q_rb, g, wf, wp, bp, st, own, rb, wq_rb, up_rb, dn_rb, ou_rb, vp_rb, bp_rb,
    up_fin, dn_fin, ou_fin, v_fin, qv_fin,
    kv_s, kv_r, q_s, q_r, wq_s, wq_r, up_s, up_r, dn_s, dn_r, ou_s, ou_r, vp_s, vp_r, bp_s, bp_r,
    rs_s, rs_r, fin_s, fin_r, b_s, b_r,
):
    s = lax.axis_index("sp")
    f = lax.axis_index("fsdp")
    i, j = f // YG, lax.rem(f, YG)
    rows = gfs.shape[0]
    tall = SP * rows
    owner = s == f // 8
    greet_all(f, s)

    def kv_copy(d):
        to = lax.rem(i + d, XG)
        return remote(dkv.at[to], kv_rb.at[d - 1], kv_s.at[d - 1], kv_r.at[d - 1], fsdp=to * YG + j)

    def q_copy(d):
        to = lax.rem(j + d, YG)
        return remote(dq.at[to], q_rb.at[d - 1], q_s.at[d - 1], q_r.at[d - 1], fsdp=i * YG + to)

    def fs_copy(src, buf, send, recv):
        def copy(d):
            to = lax.rem(f + d, FS)
            return remote(src.at[to], buf.at[d - 1], send.at[d - 1], recv.at[d - 1], fsdp=to)

        return copy

    up_copy = fs_copy(dup, up_rb, up_s, up_r)
    vp_copy = fs_copy(vp, vp_rb, vp_s, vp_r)
    wq_copy = fs_copy(wp, wq_rb, wq_s, wq_r)
    bp_copy = fs_copy(bp, bp_rb, bp_s, bp_r)

    def owner_copies(k):
        to = 8 * s + k
        return (
            remote(ddn.at[k], dn_rb.at[f], dn_s.at[k], dn_r.at[f], fsdp=to),
            remote(dwo.at[k], ou_rb.at[f], ou_s.at[k], ou_r.at[f], fsdp=to),
        )

    loop(1, XG, lambda d: kv_copy(d).start())
    loop(1, YG, lambda d: q_copy(d).start())

    def early(d):
        up_copy(d).start()
        vp_copy(d).start()

    loop(1, FS, early)

    def to_owner(k):
        @pl.when(8 * s + k != f)
        def _():
            for copy in owner_copies(k):
                copy.start()

    loop(0, 8, to_owner)

    loop(1, XG, lambda d: kv_copy(d).wait())
    loop(1, YG, lambda d: q_copy(d).wait())

    def span(b):
        return pl.ds(pl.multiple_of(b * rows, rows), rows)

    def sum_keys(b):
        at = span(b)
        for h in range(LH):
            total = dkv[i, h, at, :].astype(F32)
            for d in range(XG - 1):
                total = total + kv_rb[d, h, at, :].astype(F32)
            g[at, 128 * h : 128 * h + 128] = total.astype(BF)

    loop(0, SP, sum_keys)
    total = dq[j].astype(F32)
    for d in range(YG - 1):
        total = total + q_rb[d].astype(F32)
    g[:, 384:576] = (jnp.transpose(total, (1, 0)) * 0.125).astype(BF)

    def weight_terms(c):
        at = pl.ds(pl.multiple_of(128 * c, 128), 128)
        wf[at, :] = dot_tn(hid_all[:, at], g[...])

    loop(0, wf.shape[0] // 128, weight_terms)

    def cut(n):
        wp[n] = wf[pl.ds(pl.multiple_of(24 * n, 8), 24), :].astype(BF)

    loop(0, FS, cut)
    loop(1, FS, lambda d: wq_copy(d).start())

    def input_part(d):
        b = lax.rem(s + d, SP)
        value = dot_nt(g[span(b), :], wqkv[...])

        @pl.when(d < SP)
        def _():
            st[span(b), :] = value.astype(BF)
            rs_copy(d).start()

        @pl.when(d == SP)
        def _():
            own[...] = value

    def rs_copy(d):
        to = lax.rem(s + d, SP)
        src = st.at[pl.ds(to * rows, rows)]
        return remote(src, rb.at[d - 1], rs_s.at[d - 1], rs_r.at[d - 1], sp=to)

    loop(1, SP + 1, input_part)

    sums = jnp.sum(g[...].astype(F32), axis=0, keepdims=True)
    lane = lax.broadcasted_iota(jnp.int32, (8, 128), 1)
    row = lax.broadcasted_iota(jnp.int32, (8, 256), 0)
    low = lax.broadcasted_iota(jnp.int32, (8, 128), 1) < 64
    wide = jnp.broadcast_to(jnp.concatenate((sums, jnp.zeros((1, 64), F32)), axis=1), (8, 640))
    heads = [pltpu.roll(wide[:, 128 * h : 128 * h + 128], 64, 1) for h in range(LH)]
    vrow = jnp.concatenate(
        (
            jnp.where(low, heads[0], wide[:, 128:256]),
            jnp.where(low, heads[2], 0.0),
        ),
        axis=1,
    )
    both = jnp.where(row == 0, wide[:, 384:640], jnp.where(row == 1, vrow, 0.0))
    bp[...] = jnp.zeros(bp.shape, F32)
    for k in range(8):
        piece = both if k == 0 else pltpu.roll(both, 256 - 24 * k, 1)
        bp[8 * s + k] = jnp.where(lane < 24, piece[:, 0:128], 0.0)
    loop(1, FS, lambda d: bp_copy(d).start())

    def late(d):
        up_copy(d).wait()
        vp_copy(d).wait()

    loop(1, FS, late)

    def add_up(src, buf, start):
        def step(d, total):
            return total + buf[d].astype(F32)

        return lax.fori_loop(0, FS - 1, step, start)

    up_fin[s] = add_up(dup, up_rb, dup[f].astype(F32)).astype(BF)
    v_fin[s] = add_up(vp, vp_rb, vp[f])

    def sp_copy(e, buf):
        def copy(d):
            at = buf.at[s]
            return remote(at, at, fin_s.at[e, d - 1], fin_r.at[e, d - 1], sp=lax.rem(s + d, SP))

        return copy

    loop(1, SP, lambda d: sp_copy(0, up_fin)(d).start())
    loop(1, SP, lambda d: sp_copy(1, v_fin)(d).start())

    def own_copies(d):
        to = lax.rem(s + d, SP)
        return (
            remote(dn_fin, dn_fin, b_s.at[0, d - 1], b_r.at[0], sp=to),
            remote(ou_fin, ou_fin, b_s.at[1, d - 1], b_r.at[1], sp=to),
        )

    @pl.when(owner)
    def _():
        def arrived(d):
            frm = lax.rem(f + d, FS)
            remote(ddn.at[0], dn_rb.at[frm], dn_s.at[0], dn_r.at[frm], fsdp=frm).wait_recv()
            remote(dwo.at[0], ou_rb.at[frm], ou_s.at[0], ou_r.at[frm], fsdp=frm).wait_recv()

        loop(1, FS, arrived)
        k = lax.rem(f, 8)
        dn_rb[f] = ddn[k]
        ou_rb[f] = dwo[k]

        def down_rows(c):
            at = pl.ds(pl.multiple_of(c * 32, 32), 32)

            def step(n, total):
                return total + dn_rb[n, at, :].astype(F32)

            start = jnp.zeros((32, dn_fin.shape[1]), F32)
            dn_fin[at, :] = lax.fori_loop(0, FS, step, start).astype(BF)

        loop(0, dn_fin.shape[0] // 32, down_rows)

        def step(n, total):
            return total + ou_rb[n].astype(F32)

        ou_fin[...] = lax.fori_loop(0, FS, step, jnp.zeros(ou_fin.shape, F32)).astype(BF)

        def send(d):
            for copy in own_copies(d):
                copy.start()

        loop(1, SP, send)

    def later(d):
        wq_copy(d).wait()
        bp_copy(d).wait()

    loop(1, FS, later)
    qkvg[s] = add_up(wp, wq_rb, wp[f].astype(F32)).astype(BF)
    qv_fin[s] = add_up(bp, bp_rb, bp[f])
    loop(1, SP, lambda d: sp_copy(2, qkvg)(d).start())
    loop(1, SP, lambda d: sp_copy(3, qv_fin)(d).start())

    loop(1, SP, lambda d: rs_copy(d).wait())
    total = gfs[...] + own[...]
    for d in range(SP - 1):
        total = total + rb[d].astype(F32)
    input_grad[...] = total

    loop(1, SP, lambda d: sp_copy(0, up_fin)(d).wait())
    loop(1, SP, lambda d: sp_copy(1, v_fin)(d).wait())
    for n in range(SP):
        upg[:, 768 * n : 768 * n + 768] = up_fin[n].astype(F32)
    vecg[...] = v_fin[0] + v_fin[1] + v_fin[2] + v_fin[3]

    @pl.when(owner)
    def _():
        def sent(d):
            for copy in own_copies(d):
                copy.wait_send()

        loop(1, SP, sent)

    @pl.when(jnp.logical_not(owner))
    def _():
        for copy in own_copies(1):
            copy.wait_recv()

    dng[...] = dn_fin[...].astype(F32)
    outg[...] = ou_fin[...].astype(F32)

    loop(1, SP, lambda d: sp_copy(2, qkvg)(d).wait())
    loop(1, SP, lambda d: sp_copy(3, qv_fin)(d).wait())
    qvg[...] = qv_fin[0] + qv_fin[1] + qv_fin[2] + qv_fin[3]

    def sent_all(k):
        @pl.when(8 * s + k != f)
        def _():
            for copy in owner_copies(k):
                copy.wait_send()

    loop(0, 8, sent_all)


def on_device(
    hidden_in,
    qkv_weight,
    query_bias,
    value_bias,
    output_weight,
    output_bias,
    first_gain,
    first_shift,
    up_weight,
    up_bias,
    down_weight,
    down_bias,
    second_gain,
    second_shift,
    valid_length,
    out_cotangent,
):
    s = lax.axis_index("sp")
    rows, width = hidden_in.shape
    tall = SP * rows
    slim = qkv_weight.shape[0]
    deep = down_weight.shape[0]
    share = up_weight.shape[1] // SP
    cols = LH * HEAD_DIM * 3
    vmem = pl.BlockSpec(memory_space=pltpu.VMEM)
    hbm = pl.BlockSpec(memory_space=pl.ANY)
    dma = pltpu.SemaphoreType.DMA
    shape = jax.ShapeDtypeStruct

    parts = qkv_weight.reshape(slim, 3, SP, LH, HEAD_DIM)
    parts = lax.dynamic_index_in_dim(parts, s, 2, keepdims=False)
    kv_cols = jnp.stack((parts[:, 1], parts[:, 2]), axis=2).reshape(slim, -1)
    wq = jnp.concatenate((kv_cols, parts[:, 0].reshape(slim, -1)), axis=1)
    up = lax.dynamic_slice_in_dim(up_weight, s * share, share, 1)
    small = jnp.stack(
        (
            query_bias, value_bias, output_bias, first_gain, first_shift, down_bias,
            second_gain, second_shift,
        )
    )
    small = jnp.pad(small, ((0, 8), (0, 128 - slim)))
    small = lax.dynamic_update_slice(small, up_bias[None, :], (8, 0))

    hid_all, wqkv, q_all, kv_all, up_g, down_g, out_g, vecs = pl.pallas_call(
        project_kernel,
        out_shape=(
            shape((tall, width), BF),
            shape((width, cols), BF),
            shape((YG, LH, tall, 128), BF),
            shape((XG, LH, tall, 128), BF),
            shape((FS, slim, share), BF),
            shape((8, deep, width), BF),
            shape((8, slim, width), BF),
            shape((16, width), F32),
        ),
        in_specs=[vmem] * 6,
        out_specs=(vmem, vmem, hbm, hbm, hbm, hbm, hbm, vmem),
        scratch_shapes=[
            pltpu.VMEM((FS, slim, cols), BF),
            pltpu.VMEM((FS, 16, 128), BF),
            pltpu.VMEM((width, cols), F32),
            pltpu.VMEM((LH, tall, 128), BF),
            pltpu.VMEM((LH, tall, 128), BF),
            pltpu.VMEM((8, width), F32),
        ]
        + [dma((n,)) for n in (3, 3, 31, 31, 31, 31, 31, 8, 31, 8, 31, 31, 3, 3, 7, 7, 5)],
        compiler_params=pltpu.CompilerParams(
            collective_id=0, has_side_effects=True, vmem_limit_bytes=VMEM_LIMIT
        ),
        name="project",
    )(hidden_in, wq, up, down_weight, output_weight, small)

    flops = 4 * LH * YG * XG * tall * tall * HEAD_DIM
    o_part = pl.pallas_call(
        attend_kernel,
        grid=(LH, YG),
        out_shape=shape((YG, LH, tall, 128), BF),
        in_specs=[
            pl.BlockSpec(memory_space=pltpu.SMEM),
            pl.BlockSpec((1, 1, tall, 128), lambda h, n: (n, h, 0, 0)),
            pl.BlockSpec((XG, 1, tall, 128), lambda h, n: (0, h, 0, 0)),
        ],
        out_specs=pl.BlockSpec((1, 1, tall, 128), lambda h, n: (n, h, 0, 0)),
        compiler_params=pltpu.CompilerParams(vmem_limit_bytes=VMEM_LIMIT),
        name="attend",
    )(valid_length, q_all, kv_all)

    wo = jnp.pad(out_g.reshape(LH, HEAD_DIM, width), ((0, 0), (HEAD_DIM, 0), (0, 0)))
    wo = wo.reshape(LH * 128, width)
    result, gfs, d_all, ld_all, dup, ddn, dwo, vp = pl.pallas_call(
        middle_kernel,
        out_shape=(
            shape((rows, width), BF),
            shape((rows, width), F32),
            shape((YG, LH, tall, 128), BF),
            shape((YG, 8, tall), F32),
            shape((width, share), BF),
            shape((share, width), BF),
            shape((LH * HEAD_DIM, width), BF),
            shape((FS, 16, 128), F32),
        ),
        in_specs=[vmem] * 7,
        out_specs=(vmem, vmem, hbm, hbm, vmem, vmem, vmem, vmem),
        scratch_shapes=[
            pltpu.VMEM((YG - 1, LH, tall, 128), BF),
            pltpu.VMEM((tall, LH * 128), BF),
            pltpu.VMEM((tall, 128), F32),
            pltpu.VMEM((3, tall, width), BF),
            pltpu.VMEM((rows, width), F32),
            pltpu.VMEM((rows, width), F32),
            pltpu.VMEM((rows, width), F32),
            pltpu.VMEM((rows, 128), F32),
            pltpu.VMEM((tall, width), BF),
            pltpu.VMEM((tall, share), BF),
            pltpu.VMEM((tall, share), F32),
            pltpu.VMEM((tall, width), BF),
            pltpu.VMEM((tall, share), BF),
            pltpu.VMEM((tall, width), BF),
            pltpu.VMEM((rows, width), F32),
            pltpu.VMEM((3, SP - 1, rows, width), BF),
            pltpu.VMEM((LH, tall, 128), BF),
            pltpu.VMEM((8, tall), F32),
            pltpu.VMEM((8, width), F32),
        ]
        + [dma((3,)), dma((3,))]
        + [dma((3, 3)) for _ in range(4)]
        + [dma((n,)) for n in (3, 3, 3, 3, 2)],
        compiler_params=pltpu.CompilerParams(
            collective_id=1, has_side_effects=True, vmem_limit_bytes=VMEM_LIMIT
        ),
        name="middle",
    )(
        o_part, wo, up_g.reshape(width, share), down_g.reshape(share, width), vecs,
        hidden_in, out_cotangent,
    )

    dkv, dq = pl.pallas_call(
        attend_back_kernel,
        grid=(LH, XG),
        out_shape=(shape((XG, LH, tall, 128), BF), shape((YG, LH, HEAD_DIM, tall), BF)),
        in_specs=[
            pl.BlockSpec(memory_space=pltpu.SMEM),
            pl.BlockSpec((YG, 1, tall, 128), lambda h, n: (0, h, 0, 0)),
            pl.BlockSpec((YG, 1, tall, 128), lambda h, n: (0, h, 0, 0)),
            pl.BlockSpec((YG, 8, tall), lambda h, n: (0, 0, 0)),
            pl.BlockSpec((1, 1, tall, 128), lambda h, n: (n, h, 0, 0)),
        ],
        out_specs=(
            pl.BlockSpec((1, 1, tall, 128), lambda h, n: (n, h, 0, 0)),
            pl.BlockSpec((YG, 1, HEAD_DIM, tall), lambda h, n: (0, h, 0, 0)),
        ),
        scratch_shapes=[pltpu.VMEM((YG, HEAD_DIM, tall), F32)],
        compiler_params=pltpu.CompilerParams(vmem_limit_bytes=VMEM_LIMIT),
        name="attend_back",
    )(valid_length, q_all, d_all, ld_all, kv_all)

    input_grad, qkvg, upg, dng, outg, vecg, qvg = pl.pallas_call(
        finish_kernel,
        out_shape=(
            shape((rows, width), F32),
            shape((SP, slim, cols), BF),
            shape((slim, SP * share), F32),
            shape((deep, width), F32),
            shape((slim, width), F32),
            shape((16, 128), F32),
            shape((8, 128), F32),
        ),
        in_specs=[vmem] * 9,
        out_specs=(vmem,) * 7,
        scratch_shapes=[
            pltpu.VMEM((XG - 1, LH, tall, 128), BF),
            pltpu.VMEM((YG - 1, LH * HEAD_DIM, tall), BF),
            pltpu.VMEM((tall, cols), BF),
            pltpu.VMEM((width, cols), F32),
            pltpu.VMEM((FS, slim, cols), BF),
            pltpu.VMEM((FS, 8, 128), F32),
            pltpu.VMEM((tall, width), BF),
            pltpu.VMEM((rows, width), F32),
            pltpu.VMEM((SP - 1, rows, width), BF),
            pltpu.VMEM((FS - 1, slim, cols), BF),
            pltpu.VMEM((FS - 1, slim, share), BF),
            pltpu.VMEM((FS, deep, width), BF),
            pltpu.VMEM((FS, slim, width), BF),
            pltpu.VMEM((FS - 1, 16, 128), F32),
            pltpu.VMEM((FS - 1, 8, 128), F32),
            pltpu.VMEM((SP, slim, share), BF),
            pltpu.VMEM((deep, width), BF),
            pltpu.VMEM((slim, width), BF),
            pltpu.VMEM((SP, 16, 128), F32),
            pltpu.VMEM((SP, 8, 128), F32),
        ]
        + [dma((n,)) for n in (7, 7, 3, 3, 31, 31, 31, 31, 8, 32, 8, 32, 31, 31, 31, 31, 3, 3)]
        + [dma((4, 3)), dma((4, 3)), dma((2, 3)), dma((2,))],
        compiler_params=pltpu.CompilerParams(
            collective_id=2, has_side_effects=True, vmem_limit_bytes=VMEM_LIMIT
        ),
        name="finish",
    )(
        dkv, dq.reshape(YG, LH * HEAD_DIM, tall), hid_all, wqkv, gfs,
        dup.reshape(FS, slim, share), ddn.reshape(8, deep, width), dwo.reshape(8, slim, width), vp,
    )

    kv_grad = qkvg[:, :, : LH * 128].reshape(SP, slim, LH, 2, HEAD_DIM)
    q_grad = qkvg[:, :, LH * 128 :].reshape(SP, slim, LH, 1, HEAD_DIM)
    qkv_grad = jnp.concatenate((q_grad, kv_grad), axis=3)
    qkv_grad = jnp.transpose(qkv_grad, (1, 3, 0, 2, 4)).reshape(slim, -1).astype(F32)
    return (
        result,
        input_grad,
        qkv_grad,
        qvg[0, :slim],
        qvg[1, :slim],
        outg,
        vecg[0, :slim],
        vecg[1, :slim],
        vecg[2, :slim],
        upg,
        vecg[8, :deep],
        dng,
        vecg[3, :slim],
        vecg[4, :slim],
        vecg[5, :slim],
    )


def solution(mesh):
    placed = (
        P(("fsdp", "sp"), None),
        P("fsdp", None),
        P("fsdp"),
        P("fsdp"),
        P("fsdp", None),
        P("fsdp"),
        P("fsdp"),
        P("fsdp"),
        P("fsdp", None),
        P("fsdp"),
        P("fsdp", None),
        P("fsdp"),
        P("fsdp"),
        P("fsdp"),
        P(),
        P(("fsdp", "sp"), None),
    )
    return jax.shard_map(
        on_device,
        mesh=mesh,
        in_specs=placed,
        out_specs=(
            P(("fsdp", "sp"), None),
            P(("fsdp", "sp"), None),
            P("fsdp", None),
            P("fsdp"),
            P("fsdp"),
            P("fsdp", None),
            P("fsdp"),
            P("fsdp"),
            P("fsdp"),
            P("fsdp", None),
            P("fsdp"),
            P("fsdp", None),
            P("fsdp"),
            P("fsdp"),
            P("fsdp"),
        ),
        check_vma=False,
    )
```

```python
import functools

import jax
import jax.numpy as jnp
from jax import lax
from jax.experimental import pallas as pl
from jax.experimental.pallas import tpu as pltpu
from jax.sharding import PartitionSpec as P

HEADS = 12
HEAD_DIM = 64
SP = 4
FS = 32
YG = 4
XG = 8
LH = HEADS // SP

BF = jnp.bfloat16
F32 = jnp.float32
MESH = pl.DeviceIdType.MESH
epsilon = 1e-05
masked = -1e30
VMEM_LIMIT = 56 * 1024 * 1024


def dot_nn(a, b):
    return lax.dot_general(a, b, (((1,), (0,)), ((), ())), preferred_element_type=F32)


def dot_nt(a, b):
    return lax.dot_general(a, b, (((1,), (1,)), ((), ())), preferred_element_type=F32)


def dot_tn(a, b):
    return lax.dot_general(a, b, (((0,), (0,)), ((), ())), preferred_element_type=F32)


def norm_forward(incoming, norm_gain, norm_shift):
    row_mean = jnp.mean(incoming, axis=-1, keepdims=True)
    centered = incoming - row_mean
    inverse = lax.rsqrt(jnp.mean(centered * centered, axis=-1, keepdims=True) + epsilon)
    normed = centered * inverse
    return (normed * norm_gain + norm_shift, normed, inverse)


def norm_backward(incoming, normed, inverse, norm_gain):
    scaled = incoming * norm_gain
    adjusted = (
        scaled
        - jnp.mean(scaled, axis=-1, keepdims=True)
        - normed * jnp.mean(scaled * normed, axis=-1, keepdims=True)
    )
    return (
        adjusted * inverse,
        jnp.sum(incoming * normed, axis=0, keepdims=True),
        jnp.sum(incoming, axis=0, keepdims=True),
    )


def loop(low, high, body):
    def step(d, carried):
        body(d)
        return carried

    lax.fori_loop(low, high, step, 0)


def remote(src, dst, send, recv, **device):
    return pltpu.make_async_remote_copy(
        src_ref=src,
        dst_ref=dst,
        send_sem=send,
        recv_sem=recv,
        device_id=device,
        device_id_type=MESH,
    )


def greet(barrier, **device):
    pl.semaphore_signal(barrier, inc=1, device_id=device, device_id_type=MESH)


def greet_all(f, s):
    barrier = pltpu.get_barrier_semaphore()
    loop(1, FS, lambda d: greet(barrier, fsdp=lax.rem(f + d, FS)))
    loop(1, SP, lambda d: greet(barrier, sp=lax.rem(s + d, SP)))

    @pl.when(s != f // 8)
    def _():
        loop(0, 8, lambda t: greet(barrier, fsdp=8 * s + t, sp=f // 8))

    pl.semaphore_wait(barrier, FS - 1 + SP - 1 + jnp.where(s != f // 8, 8, 0))


def forward_kernel(
    valid, hid, wq, up, down, out, small,
    hid_all, wqkv, q_all, kv_all, o_all, up_g, down_g, out_g, vecs,
    wq_g, small_g, wf, q_st, kv_st, qvb, state, o_st,
    hid_s, hid_r, wq_s, wq_r, up_s, up_r, dn_s, dn_r, ou_s, ou_r, sm_s, sm_r,
    q_s, q_r, kv_s, kv_r, o_s, o_r, loc,
):
    s = lax.axis_index("sp")
    f = lax.axis_index("fsdp")
    i, j = f // YG, lax.rem(f, YG)
    greet_all(f, s)
    rows = hid.shape[0]

    def hid_copy(d):
        dst = hid_all.at[pl.ds(s * rows, rows)]
        return remote(hid, dst, hid_s.at[d - 1], hid_r.at[d - 1], sp=lax.rem(s + d, SP))

    def fs_copy(src, buf, send, recv):
        return lambda d: remote(
            src, buf.at[f], send.at[d - 1], recv.at[d - 1], fsdp=lax.rem(f + d, FS)
        )

    wq_copy = fs_copy(wq, wq_g, wq_s, wq_r)
    small_copy = fs_copy(small, small_g, sm_s, sm_r)
    up_copy = fs_copy(up, up_g, up_s, up_r)

    def owned_copies(t):
        k = lax.rem(f, 8)
        to = {"fsdp": 8 * s + t, "sp": f // 8}
        return (
            remote(down, down_g.at[k], dn_s.at[t], dn_r.at[k], **to),
            remote(out, out_g.at[k], ou_s.at[t], ou_r.at[k], **to),
        )

    def owned_arrivals(k):
        to = {"fsdp": 8 * s + k, "sp": f // 8}
        return (
            remote(down, down_g.at[k], dn_s.at[k], dn_r.at[k], **to),
            remote(out, out_g.at[k], ou_s.at[k], ou_r.at[k], **to),
        )

    def is_self(t):
        return (s == f // 8) & (8 * s + t == f)

    loop(1, SP, lambda d: hid_copy(d).start())

    def first_sends(d):
        wq_copy(d).start()
        small_copy(d).start()

    loop(1, FS, first_sends)
    hid_all[pl.ds(pl.multiple_of(s * rows, rows), rows), :] = hid[...]
    wq_g[f] = wq[...]
    small_g[f] = small[...]
    up_own = pltpu.make_async_copy(up, up_g.at[f], loc.at[0])
    up_own.start()

    loop(1, SP, lambda d: hid_copy(d).wait())

    def first_waits(d):
        wq_copy(d).wait()
        small_copy(d).wait()

    loop(1, FS, first_waits)

    width = vecs.shape[1]
    total = jnp.zeros((8, width), F32)
    pad = jnp.zeros((8, width - 128), F32)
    for n in range(FS):
        piece = small_g[n][0:8].astype(F32)
        wide = jnp.concatenate((piece, pad), axis=1)
        total = total + (wide if n == 0 else pltpu.roll(wide, 24 * n, 1))
    vecs[0:8, :] = total
    ub = jnp.zeros((8, width), F32)
    qv = jnp.zeros((8, width), F32)
    for k in range(8):
        block = small_g[8 * s + k].astype(F32)
        ub_wide = jnp.concatenate((block[8:16], pad), axis=1)
        qv_wide = jnp.concatenate((block[0:8], pad), axis=1)
        ub = ub + (ub_wide if k == 0 else pltpu.roll(ub_wide, 96 * k, 1))
        qv = qv + (qv_wide if k == 0 else pltpu.roll(qv_wide, 24 * k, 1))
    vecs[8:16, :] = ub
    qvb[...] = qv
    lane = lax.broadcasted_iota(jnp.int32, (1, width), 1)
    qrow = qvb[0:1, :]
    vrow = qvb[1:2, :]
    bias = jnp.zeros((1, width), F32)
    wide_q = jnp.broadcast_to(qrow, (8, width))
    wide_v = jnp.broadcast_to(vrow, (8, width))
    bias = jnp.where((lane >= 384) & (lane < 576), pltpu.roll(wide_q, 384, 1)[0:1], 0.0)
    for h in range(LH):
        here = (lane >= 128 * h + 64) & (lane < 128 * h + 128)
        bias = bias + jnp.where(here, pltpu.roll(wide_v, 64 * h + 64, 1)[0:1], 0.0)

    def assemble(n):
        wf[pl.ds(pl.multiple_of(24 * n, 8), 24), :] = wq_g[n].astype(F32)

    loop(0, FS, assemble)
    wqkv[...] = wf[...].astype(BF)

    low_lane = lax.broadcasted_iota(jnp.int32, (rows, 128), 1) < HEAD_DIM

    def project(b):
        at = pl.ds(pl.multiple_of(b * rows, rows), rows)
        p = dot_nn(hid_all[at, :], wqkv[...]) + bias[:, :576]
        for h in range(LH):
            kv_st[h, at, :] = p[:, 128 * h : 128 * h + 128].astype(BF)
        q01 = p[:, 384:512] * 0.125
        q2 = jnp.concatenate((p[:, 512:576], jnp.zeros((rows, 64), F32)), axis=1) * 0.125
        q_st[0, at, :] = jnp.where(low_lane, q01, 0.0).astype(BF)
        q_st[1, at, :] = jnp.where(low_lane, pltpu.roll(q01, 64, 1), 0.0).astype(BF)
        q_st[2, at, :] = q2.astype(BF)

    loop(0, SP, project)

    def kv_copy(d):
        to = lax.rem(i + d, XG) * YG + j
        return remote(kv_st, kv_all.at[i], kv_s.at[d - 1], kv_r.at[d - 1], fsdp=to)

    def q_copy(d):
        to = i * YG + lax.rem(j + d, YG)
        return remote(q_st, q_all.at[j], q_s.at[d - 1], q_r.at[d - 1], fsdp=to)

    loop(1, XG, lambda d: kv_copy(d).start())
    loop(1, YG, lambda d: q_copy(d).start())
    kv_all[i] = kv_st[...]
    q_all[j] = q_st[...]

    tall = SP * rows
    half = tall // 2
    key_place = lax.broadcasted_iota(jnp.int32, (1, tall), 1)
    lanes = lax.broadcasted_iota(jnp.int32, (half, 128), 1)

    def o_copy(d, h):
        to = lax.rem(j + YG - d, YG)
        src = o_st.at[to, h]
        return remote(src, o_all.at[j, h], o_s.at[d - 1, h], o_r.at[d - 1, h], fsdp=i * YG + to)

    def attend(step, is_first, is_last):
        places = [lax.rem(i + XG - 2 * step - c, XG) for c in range(2)]
        limits = [
            jnp.where((at * YG + j) * tall + key_place < valid[0], 0.0, masked) for at in places
        ]

        def tile(t):
            d = t // LH
            h = lax.rem(t, LH)
            n = lax.rem(j + YG - d, YG)
            if is_first:

                @pl.when((d > 0) & (h == 0))
                def _():
                    q_copy(d).wait_recv()

            for r in range(2):
                at = pl.ds(r * half, half)
                query = q_all[n, h, at, :]
                blocks = [kv_all[p, h] for p in places]
                scores = [dot_nt(query, block) + limit for block, limit in zip(blocks, limits)]
                tops = [jnp.max(score, axis=1, keepdims=True) for score in scores]
                top = jnp.maximum(tops[0], tops[1])
                if not is_first:
                    old = state[n, h, at, :]
                    before = old[:, 0:1]
                    top = jnp.maximum(top, before)
                probs = [jnp.exp(score - top) for score in scores]
                total = functools.reduce(
                    jnp.add, [jnp.sum(p, axis=1, keepdims=True) for p in probs]
                )
                weighted = functools.reduce(
                    jnp.add, [dot_nn(p.astype(BF), block) for p, block in zip(probs, blocks)]
                )
                if not is_first:
                    decay = jnp.exp(before - top)
                    total = total + decay * old[:, 32:33]
                    weighted = weighted + decay * old
                if is_last:
                    log_sum = top + jnp.log(total)
                    high = log_sum.astype(BF).astype(F32)
                    logs = jnp.where(lanes < 32, high, log_sum - high)
                    o_st[n, h, at, :] = jnp.where(lanes >= 64, weighted / total, logs).astype(BF)
                else:
                    logs = jnp.where(lanes < 32, top, total)
                    state[n, h, at, :] = jnp.where(lanes >= 64, weighted, logs)
            if is_last:

                @pl.when(d > 0)
                def _():
                    o_copy(d, h).start()

                @pl.when(d == 0)
                def _():
                    o_all[j, h] = o_st[j, h]

        if is_last:
            loop(LH, LH * YG, tile)
            loop(0, LH, tile)
        else:
            loop(0, LH * YG, tile)

    kv_copy(1).wait_recv()
    attend(0, True, False)
    loop(1, FS, lambda d: up_copy(d).start())

    def send_owned(t):
        @pl.when(jnp.logical_not(is_self(t)))
        def _():
            for copy in owned_copies(t):
                copy.start()

    loop(0, 8, send_owned)

    @pl.when(s == f // 8)
    def _():
        dn_own = pltpu.make_async_copy(down, down_g.at[lax.rem(f, 8)], loc.at[1])
        ou_own = pltpu.make_async_copy(out, out_g.at[lax.rem(f, 8)], loc.at[2])
        dn_own.start()
        ou_own.start()
        dn_own.wait()
        ou_own.wait()

    def middle_pass(step):
        kv_copy(2 * step).wait_recv()
        kv_copy(2 * step + 1).wait_recv()
        attend(step, False, False)

    loop(1, XG // 2 - 1, middle_pass)
    kv_copy(XG - 2).wait_recv()
    kv_copy(XG - 1).wait_recv()
    attend(XG // 2 - 1, False, True)

    up_own.wait()
    loop(1, XG, lambda d: kv_copy(d).wait_send())
    loop(1, YG, lambda d: q_copy(d).wait_send())
    loop(1, FS, lambda d: up_copy(d).wait())

    def owned_wait(t):
        @pl.when(jnp.logical_not(is_self(t)))
        def _():
            for copy in owned_copies(t):
                copy.wait_send()
            for copy in owned_arrivals(t):
                copy.wait_recv()

    loop(0, 8, owned_wait)
    loop(1, YG, lambda d: loop(0, LH, lambda h: o_copy(d, h).wait()))


def middle_kernel(
    o_all, wo, wup, wdn, vecs, hid, cot,
    result, gfs, d_all, ld_all, dup, ddn, dwo, vp,
    att, ld, st, own, first, n1, inv1, x_all, act, deriv, gd, gp, gb, gsec, rb, dbuf, ldrow, vg,
    ag_s, ag_r, rs_s, rs_r, d_s, d_r, l_s, l_r, loc,
):
    s = lax.axis_index("sp")
    f = lax.axis_index("fsdp")
    i, j = f // YG, lax.rem(f, YG)
    rows = hid.shape[0]
    tall = SP * rows
    barrier = pltpu.get_barrier_semaphore()
    loop(1, YG, lambda d: greet(barrier, fsdp=i * YG + lax.rem(j + d, YG)))
    loop(1, SP, lambda d: greet(barrier, sp=lax.rem(s + d, SP)))
    pl.semaphore_wait(barrier, YG - 1 + SP - 1)

    def y_peer(d):
        return i * YG + lax.rem(j + d, YG)

    def span(b):
        return pl.ds(pl.multiple_of(b * rows, rows), rows)

    lane = lax.broadcasted_iota(jnp.int32, (rows, 128), 1)

    def merge(b):
        at = span(b)
        sums = jnp.zeros((rows, 128), F32)
        for h in range(LH):
            parts = [o_all[d, h, at, :].astype(F32) for d in range(YG)]
            logs = [p[:, 0:1] + p[:, 32:33] for p in parts]
            top = functools.reduce(jnp.maximum, logs)
            weights = [jnp.exp(g - top) for g in logs]
            total = functools.reduce(jnp.add, weights)
            merged = functools.reduce(jnp.add, [p * w for p, w in zip(parts, weights)]) / total
            att[at, 128 * h : 128 * h + 128] = jnp.where(lane >= 64, merged, 0.0).astype(BF)
            sums = jnp.where(lane == 2 * h, top + jnp.log(total), sums)
        ld[at, :] = sums

    loop(0, SP, merge)

    def gather(e, buf):
        def copy(d):
            at = buf.at[pl.ds(s * rows, rows)]
            return remote(at, at, ag_s.at[e, d - 1], ag_r.at[e, d - 1], sp=lax.rem(s + d, SP))

        return copy

    def scatter(e):
        def copy(d):
            src = st.at[e, pl.ds(lax.rem(s + d, SP) * rows, rows)]
            sems = (rs_s.at[e, d - 1], rs_r.at[e, d - 1])
            return remote(src, rb.at[e, d - 1], *sems, sp=lax.rem(s + d, SP))

        return copy

    def collect(e):
        loop(1, SP, lambda d: scatter(e)(d).wait())
        total = own[...]
        for d in range(SP - 1):
            total = total + rb[e, d].astype(F32)
        return total

    def out_part(d):
        b = lax.rem(s + d, SP)
        value = dot_nn(att[span(b), :], wo[...])

        @pl.when(d < SP)
        def _():
            st[0, span(b), :] = value.astype(BF)
            scatter(0)(d).start()

        @pl.when(d == SP)
        def _():
            own[...] = value

    loop(1, SP + 1, out_part)
    summed = hid[...].astype(F32) + collect(0) + vecs[2:3, :]
    value, normed, inverse = norm_forward(summed, vecs[3:4, :], vecs[4:5, :])
    first[...] = value
    n1[...] = normed
    inv1[...] = jnp.broadcast_to(inverse, inv1.shape)
    x_all[span(s), :] = value.astype(BF)
    loop(1, SP, lambda d: gather(0, x_all)(d).start())

    def pipeline(e, buf, work):
        def step(d):
            b = lax.rem(s + SP - d, SP)

            @pl.when(d > 0)
            def _():
                gather(e, buf)(d).wait_recv()

            value = work(b)

            @pl.when(d > 0)
            def _():
                st[e + 1, span(b), :] = value.astype(BF)
                scatter(e + 1)(SP - d).start()

            @pl.when(d == 0)
            def _():
                own[...] = value

        loop(0, SP, step)
        loop(1, SP, lambda d: gather(e, buf)(d).wait_send())

    def feed(b):
        at = span(b)
        pre = dot_nn(x_all[at, :], wup[...]) + vecs[8:9, :]
        cdf = 0.5 * (1.0 + lax.erf(pre * 0.7071067811865476))
        density = jnp.exp(-0.5 * pre * pre) * 0.3989422804014327
        active = (pre * cdf).astype(BF)
        act[at, :] = active
        deriv[at, :] = cdf + pre * density
        return dot_nn(active, wdn[...])

    pipeline(0, x_all, feed)
    summed = first[...] + collect(1) + vecs[5:6, :]
    value, normed, inverse = norm_forward(summed, vecs[6:7, :], vecs[7:8, :])
    result[...] = value.astype(BF)
    grad, ggain, gshift = norm_backward(cot[...].astype(F32), normed, inverse, vecs[6:7, :])
    gsec[...] = grad
    low = grad.astype(BF)
    gd[span(s), :] = low
    loop(1, SP, lambda d: gather(1, gd)(d).start())
    vg[...] = jnp.zeros(vg.shape, F32)
    vg[3:4, :] = jnp.sum(low.astype(F32), axis=0, keepdims=True)
    vg[4:5, :] = ggain
    vg[5:6, :] = gshift

    def back(b):
        at = span(b)
        grad_pre = (dot_nt(gd[at, :], wdn[...]) * deriv[at, :]).astype(BF)
        gp[at, :] = grad_pre
        return dot_nt(grad_pre, wup[...])

    pipeline(1, gd, back)

    def weight_terms(c):
        at = pl.ds(pl.multiple_of(128 * c, 128), 128)
        ddn[at, :] = dot_tn(act[:, at], gd[...]).astype(BF)
        dup[at, :] = dot_tn(x_all[:, at], gp[...]).astype(BF)

    loop(0, act.shape[1] // 128, weight_terms)
    ub = jnp.sum(gp[...].astype(F32), axis=0, keepdims=True)
    grad_first = gsec[...] + collect(2)
    grad, ggain, gshift = norm_backward(grad_first, n1[...], inv1[:, 0:1], vecs[3:4, :])
    gfs[...] = grad
    low = grad.astype(BF)
    gb[span(s), :] = low
    loop(1, SP, lambda d: gather(2, gb)(d).start())
    vg[0:1, :] = jnp.sum(low.astype(F32), axis=0, keepdims=True)
    vg[1:2, :] = ggain
    vg[2:3, :] = gshift

    def branch(d):
        b = lax.rem(s + SP - d, SP)
        at = span(b)

        @pl.when(d > 0)
        def _():
            gather(2, gb)(d).wait_recv()

        value = dot_nt(gb[at, :], wo[...]).astype(BF)
        sums = ld[at, :]
        for h in range(LH):
            part = value[:, 128 * h : 128 * h + 128]
            dbuf[h, at, :] = part
            product = part.astype(F32) * att[at, 128 * h : 128 * h + 128].astype(F32)
            sums = jnp.where(lane == 2 * h + 1, jnp.sum(product, axis=1, keepdims=True), sums)
        ld[at, :] = sums
        loop(1, YG, lambda n: d_copy(n, d).start())

    def d_copy(n, d):
        at = span(lax.rem(s + SP - d, SP))
        sems = (d_s.at[n - 1, d], d_r.at[n - 1, d])
        return remote(dbuf.at[:, at], d_all.at[j, :, at], *sems, fsdp=y_peer(n))

    loop(0, SP, branch)
    loop(1, SP, lambda d: gather(2, gb)(d).wait_send())
    ldrow[...] = jnp.transpose(ld[...], (1, 0))[0:8, :]

    def l_copy(d):
        return remote(ldrow, ld_all.at[j], l_s.at[d - 1], l_r.at[d - 1], fsdp=y_peer(d))

    loop(1, YG, lambda d: l_copy(d).start())
    d_own = pltpu.make_async_copy(dbuf, d_all.at[j], loc.at[0])
    l_own = pltpu.make_async_copy(ldrow, ld_all.at[j], loc.at[1])
    d_own.start()
    l_own.start()
    for h in range(LH):
        value = dot_tn(att[:, 128 * h : 128 * h + 128], gb[...])
        dwo[64 * h : 64 * h + 64, :] = value[64:128].astype(BF)
    lane8 = lax.broadcasted_iota(jnp.int32, (8, 128), 1)
    wide = vg[...]
    width = wide.shape[1]
    ub_wide = jnp.broadcast_to(ub, (8, width))
    for n in range(FS):
        piece = wide if n == 0 else pltpu.roll(wide, width - 24 * n, 1)
        vp[n, 0:8, :] = jnp.where(lane8 < 24, piece[:, 0:128], 0.0)
        vp[n, 8:16, :] = jnp.zeros((8, 128), F32)
    for k in range(8):
        piece = ub_wide if k == 0 else pltpu.roll(ub_wide, width - 96 * k, 1)
        vp[8 * s + k, 8:16, :] = jnp.where(lane8 < 96, piece[:, 0:128], 0.0)
    d_own.wait()
    l_own.wait()
    loop(1, YG, lambda n: loop(0, SP, lambda d: d_copy(n, d).wait()))
    loop(1, YG, lambda d: l_copy(d).wait())


def backward_kernel(
    valid, q_all, d_all, ld, kv_all, hid_all, wqkv, gfs, dup, ddn, dwo, vp,
    input_grad, qkvg, upg, dng, outg, vecg, qvg,
    acc, dq, dkv, kv_rb, q_rb, g, wf, wp, bp, st, own, rb, wq_rb, up_rb, dn_rb, ou_rb, vp_rb, bp_rb,
    up_fin, dn_fin, ou_fin, v_fin, qv_fin,
    kv_s, kv_r, q_s, q_r, wq_s, wq_r, up_s, up_r, dn_s, dn_r, ou_s, ou_r, vp_s, vp_r, bp_s, bp_r,
    rs_s, rs_r, fin_s, fin_r,
):
    s = lax.axis_index("sp")
    f = lax.axis_index("fsdp")
    i, j = f // YG, lax.rem(f, YG)
    rows = gfs.shape[0]
    tall = SP * rows
    greet_all(f, s)

    def kv_copy(d):
        to = lax.rem(i + d, XG)
        return remote(dkv.at[d - 1], kv_rb.at[d - 1], kv_s.at[d - 1], kv_r.at[d - 1], fsdp=to * YG + j)

    def q_copy(d):
        to = lax.rem(j + d, YG)
        return remote(dq.at[to], q_rb.at[d - 1], q_s.at[d - 1], q_r.at[d - 1], fsdp=i * YG + to)

    def fs_copy(src, buf, send, recv):
        def copy(d):
            to = lax.rem(f + d, FS)
            return remote(src.at[to], buf.at[d - 1], send.at[d - 1], recv.at[d - 1], fsdp=to)

        return copy

    up_copy = fs_copy(dup, up_rb, up_s, up_r)
    vp_copy = fs_copy(vp, vp_rb, vp_s, vp_r)
    wq_copy = fs_copy(wp, wq_rb, wq_s, wq_r)
    bp_copy = fs_copy(bp, bp_rb, bp_s, bp_r)

    def owner_copies(k):
        to = {"fsdp": 8 * s + k, "sp": f // 8}
        n = lax.rem(f, 8)
        return (
            remote(ddn.at[k], dn_rb.at[n], dn_s.at[k], dn_r.at[n], **to),
            remote(dwo.at[k], ou_rb.at[n], ou_s.at[k], ou_r.at[n], **to),
        )

    def owner_arrivals(n):
        to = {"fsdp": 8 * s + n, "sp": f // 8}
        return (
            remote(ddn.at[n], dn_rb.at[n], dn_s.at[n], dn_r.at[n], **to),
            remote(dwo.at[n], ou_rb.at[n], ou_s.at[n], ou_r.at[n], **to),
        )

    def is_self(t):
        return (s == f // 8) & (8 * s + t == f)

    def early(d):
        up_copy(d).start()
        vp_copy(d).start()

    loop(1, FS, early)

    def to_owner(k):
        @pl.when(jnp.logical_not(is_self(k)))
        def _():
            for copy in owner_copies(k):
                copy.start()

        @pl.when(is_self(k))
        def _():
            dn_rb[k] = ddn[k]
            ou_rb[k] = dwo[k]

    loop(0, 8, to_owner)

    acc[...] = jnp.zeros(acc.shape, F32)

    def key_step(d):
        at = lax.rem(i + d, XG)
        first_key = (at * YG + j) * tall

        def head(h):
            def work(last):
                block = kv_all[at, h]
                flipped = jnp.transpose(block.astype(F32), (1, 0))[0:HEAD_DIM].astype(BF)
                total = None
                for n in range(YG):
                    query = q_all[n, h]
                    grad = d_all[n, h]
                    log_sum = ld[n, pl.ds(2 * h, 1), :]
                    delta = ld[n, pl.ds(2 * h + 1, 1), :]
                    scores = dot_nt(block, query)
                    if last:
                        place = first_key + lax.broadcasted_iota(jnp.int32, (tall, 1), 0)
                        scores = jnp.where(place < valid[0], scores, masked)
                    p = jnp.exp(scores - log_sum)
                    grad_p = dot_nt(block, grad)
                    grad_s = (p * (grad_p - delta)).astype(BF)
                    terms = dot_nn(grad_s, query) + dot_nn(p.astype(BF), grad)
                    total = terms if n == 0 else total + terms
                    acc[n, h] = acc[n, h] + dot_nn(flipped, grad_s)
                dkv[d - 1, h] = total.astype(BF)

            @pl.when(at < XG - 1)
            def _():
                work(False)

            @pl.when(at == XG - 1)
            def _():
                work(True)

        loop(0, LH, head)

        @pl.when(d < XG)
        def _():
            kv_copy(d).start()

    loop(1, XG + 1, key_step)
    for n in range(YG):
        for h in range(LH):
            dq[n, 64 * h : 64 * h + 64, :] = acc[n, h].astype(BF)
    loop(1, YG, lambda d: q_copy(d).start())

    def late(d):
        up_copy(d).wait()
        vp_copy(d).wait()

    loop(1, FS, late)

    def add_up(buf, start):
        def step(d, total):
            return total + buf[d].astype(F32)

        return lax.fori_loop(0, buf.shape[0], step, start)

    up_fin[s] = add_up(up_rb, dup[f].astype(F32)).astype(BF)
    v_fin[s] = add_up(vp_rb, vp[f])

    def owner_wait(t):
        @pl.when(jnp.logical_not(is_self(t)))
        def _():
            for copy in owner_copies(t):
                copy.wait_send()
            for copy in owner_arrivals(t):
                copy.wait_recv()

    loop(0, 8, owner_wait)

    def down_rows(c):
        at = pl.ds(pl.multiple_of(c * 32, 32), 32)
        total = dn_rb[0, at, :].astype(F32)
        for n in range(1, 8):
            total = total + dn_rb[n, at, :].astype(F32)
        dn_fin[s, at, :] = total.astype(BF)

    loop(0, dn_fin.shape[1] // 32, down_rows)
    ou_fin[s] = add_up(ou_rb, jnp.zeros(ou_fin.shape[1:], F32)).astype(BF)

    def sp_copy(e, buf):
        def copy(d):
            at = buf.at[s]
            return remote(at, at, fin_s.at[e, d - 1], fin_r.at[e, d - 1], sp=lax.rem(s + d, SP))

        return copy

    early_bufs = ((0, up_fin), (1, v_fin), (4, dn_fin), (5, ou_fin))
    for e, buf in early_bufs:
        loop(1, SP, lambda d: sp_copy(e, buf)(d).start())

    loop(1, XG, lambda d: kv_copy(d).wait())
    loop(1, YG, lambda d: q_copy(d).wait())

    def span(b):
        return pl.ds(pl.multiple_of(b * rows, rows), rows)

    def sum_keys(b):
        at = span(b)
        for h in range(LH):
            total = dkv[XG - 1, h, at, :].astype(F32)
            for d in range(XG - 1):
                total = total + kv_rb[d, h, at, :].astype(F32)
            g[at, 128 * h : 128 * h + 128] = total.astype(BF)

    loop(0, SP, sum_keys)
    total = dq[j].astype(F32)
    for d in range(YG - 1):
        total = total + q_rb[d].astype(F32)
    g[:, 384:576] = (jnp.transpose(total, (1, 0)) * 0.125).astype(BF)

    def weight_terms(c):
        at = pl.ds(pl.multiple_of(128 * c, 128), 128)
        wf[at, :] = dot_tn(hid_all[:, at], g[...])

    loop(0, wf.shape[0] // 128, weight_terms)

    def cut(n):
        wp[n] = wf[pl.ds(pl.multiple_of(24 * n, 8), 24), :].astype(BF)

    loop(0, FS, cut)
    loop(1, FS, lambda d: wq_copy(d).start())

    def input_part(d):
        b = lax.rem(s + d, SP)
        value = dot_nt(g[span(b), :], wqkv[...])

        @pl.when(d < SP)
        def _():
            st[span(b), :] = value.astype(BF)
            rs_copy(d).start()

        @pl.when(d == SP)
        def _():
            own[...] = value

    def rs_copy(d):
        to = lax.rem(s + d, SP)
        src = st.at[pl.ds(to * rows, rows)]
        return remote(src, rb.at[d - 1], rs_s.at[d - 1], rs_r.at[d - 1], sp=to)

    loop(1, SP + 1, input_part)

    sums = jnp.sum(g[...].astype(F32), axis=0, keepdims=True)
    lane = lax.broadcasted_iota(jnp.int32, (8, 128), 1)
    row = lax.broadcasted_iota(jnp.int32, (8, 256), 0)
    low = lax.broadcasted_iota(jnp.int32, (8, 128), 1) < 64
    wide = jnp.broadcast_to(jnp.concatenate((sums, jnp.zeros((1, 64), F32)), axis=1), (8, 640))
    heads = [pltpu.roll(wide[:, 128 * h : 128 * h + 128], 64, 1) for h in range(LH)]
    vrow = jnp.concatenate(
        (
            jnp.where(low, heads[0], wide[:, 128:256]),
            jnp.where(low, heads[2], 0.0),
        ),
        axis=1,
    )
    both = jnp.where(row == 0, wide[:, 384:640], jnp.where(row == 1, vrow, 0.0))
    bp[...] = jnp.zeros(bp.shape, F32)
    for k in range(8):
        piece = both if k == 0 else pltpu.roll(both, 256 - 24 * k, 1)
        bp[8 * s + k] = jnp.where(lane < 24, piece[:, 0:128], 0.0)
    loop(1, FS, lambda d: bp_copy(d).start())

    def later(d):
        wq_copy(d).wait()
        bp_copy(d).wait()

    loop(1, FS, later)
    qkvg[s] = add_up(wq_rb, wp[f].astype(F32)).astype(BF)
    qv_fin[s] = add_up(bp_rb, bp[f])
    loop(1, SP, lambda d: sp_copy(2, qkvg)(d).start())
    loop(1, SP, lambda d: sp_copy(3, qv_fin)(d).start())

    loop(1, SP, lambda d: rs_copy(d).wait())
    total = gfs[...] + own[...]
    for d in range(SP - 1):
        total = total + rb[d].astype(F32)
    input_grad[...] = total

    for e, buf in early_bufs:
        loop(1, SP, lambda d: sp_copy(e, buf)(d).wait())
    for n in range(SP):
        upg[:, 768 * n : 768 * n + 768] = up_fin[n].astype(F32)
    vecg[...] = v_fin[0] + v_fin[1] + v_fin[2] + v_fin[3]
    down_sum = dn_fin[0].astype(F32)
    out_sum = ou_fin[0].astype(F32)
    for n in range(1, SP):
        down_sum = down_sum + dn_fin[n].astype(F32)
        out_sum = out_sum + ou_fin[n].astype(F32)
    dng[...] = down_sum
    outg[...] = out_sum

    loop(1, SP, lambda d: sp_copy(2, qkvg)(d).wait())
    loop(1, SP, lambda d: sp_copy(3, qv_fin)(d).wait())
    qvg[...] = qv_fin[0] + qv_fin[1] + qv_fin[2] + qv_fin[3]


def on_device(
    hidden_in,
    qkv_weight,
    query_bias,
    value_bias,
    output_weight,
    output_bias,
    first_gain,
    first_shift,
    up_weight,
    up_bias,
    down_weight,
    down_bias,
    second_gain,
    second_shift,
    valid_length,
    out_cotangent,
):
    s = lax.axis_index("sp")
    rows, width = hidden_in.shape
    tall = SP * rows
    slim = qkv_weight.shape[0]
    deep = down_weight.shape[0]
    share = up_weight.shape[1] // SP
    cols = LH * HEAD_DIM * 3
    vmem = pl.BlockSpec(memory_space=pltpu.VMEM)
    hbm = pl.BlockSpec(memory_space=pl.ANY)
    dma = pltpu.SemaphoreType.DMA
    shape = jax.ShapeDtypeStruct

    parts = qkv_weight.reshape(slim, 3, SP, LH, HEAD_DIM)
    parts = lax.dynamic_index_in_dim(parts, s, 2, keepdims=False)
    kv_cols = jnp.stack((parts[:, 1], parts[:, 2]), axis=2).reshape(slim, -1)
    wq = jnp.concatenate((kv_cols, parts[:, 0].reshape(slim, -1)), axis=1)
    up = lax.dynamic_slice_in_dim(up_weight, s * share, share, 1)
    small = jnp.stack(
        (
            query_bias, value_bias, output_bias, first_gain, first_shift, down_bias,
            second_gain, second_shift,
        )
    )
    small = jnp.pad(small, ((0, 8), (0, 128 - slim)))
    small = lax.dynamic_update_slice(small, up_bias[None, :], (8, 0))

    smem = pl.BlockSpec(memory_space=pltpu.SMEM)
    hid_all, wqkv, q_all, kv_all, o_all, up_g, down_g, out_g, vecs = pl.pallas_call(
        forward_kernel,
        out_shape=(
            shape((tall, width), BF),
            shape((width, cols), BF),
            shape((YG, LH, tall, 128), BF),
            shape((XG, LH, tall, 128), BF),
            shape((YG, LH, tall, 128), BF),
            shape((FS, slim, share), BF),
            shape((8, deep, width), BF),
            shape((8, slim, width), BF),
            shape((16, width), F32),
        ),
        in_specs=[smem] + [vmem] * 6,
        out_specs=(vmem, vmem, vmem, vmem, vmem, hbm, hbm, hbm, vmem),
        scratch_shapes=[
            pltpu.VMEM((FS, slim, cols), BF),
            pltpu.VMEM((FS, 16, 128), BF),
            pltpu.VMEM((width, cols), F32),
            pltpu.VMEM((LH, tall, 128), BF),
            pltpu.VMEM((LH, tall, 128), BF),
            pltpu.VMEM((8, width), F32),
            pltpu.VMEM((YG, LH, tall, 128), F32),
            pltpu.VMEM((YG, LH, tall, 128), BF),
        ]
        + [dma((n,)) for n in (3, 3, 31, 31, 31, 31, 8, 8, 8, 8, 31, 31, 3, 3, 7, 7)]
        + [dma((3, 3)), dma((3, 3)), dma((3,))],
        compiler_params=pltpu.CompilerParams(
            collective_id=0, has_side_effects=True, vmem_limit_bytes=VMEM_LIMIT
        ),
        name="forward",
    )(valid_length, hidden_in, wq, up, down_weight, output_weight, small)

    wo = jnp.pad(out_g.reshape(LH, HEAD_DIM, width), ((0, 0), (HEAD_DIM, 0), (0, 0)))
    wo = wo.reshape(LH * 128, width)
    result, gfs, d_all, ld_all, dup, ddn, dwo, vp = pl.pallas_call(
        middle_kernel,
        out_shape=(
            shape((rows, width), BF),
            shape((rows, width), F32),
            shape((YG, LH, tall, 128), BF),
            shape((YG, 8, tall), F32),
            shape((width, share), BF),
            shape((share, width), BF),
            shape((LH * HEAD_DIM, width), BF),
            shape((FS, 16, 128), F32),
        ),
        in_specs=[vmem] * 7,
        out_specs=(vmem, vmem, hbm, hbm, vmem, vmem, vmem, vmem),
        scratch_shapes=[
            pltpu.VMEM((tall, LH * 128), BF),
            pltpu.VMEM((tall, 128), F32),
            pltpu.VMEM((3, tall, width), BF),
            pltpu.VMEM((rows, width), F32),
            pltpu.VMEM((rows, width), F32),
            pltpu.VMEM((rows, width), F32),
            pltpu.VMEM((rows, 128), F32),
            pltpu.VMEM((tall, width), BF),
            pltpu.VMEM((tall, share), BF),
            pltpu.VMEM((tall, share), F32),
            pltpu.VMEM((tall, width), BF),
            pltpu.VMEM((tall, share), BF),
            pltpu.VMEM((tall, width), BF),
            pltpu.VMEM((rows, width), F32),
            pltpu.VMEM((3, SP - 1, rows, width), BF),
            pltpu.VMEM((LH, tall, 128), BF),
            pltpu.VMEM((8, tall), F32),
            pltpu.VMEM((8, width), F32),
        ]
        + [dma((3, 3)) for _ in range(4)]
        + [dma((3, 4)), dma((3, 4)), dma((3,)), dma((3,)), dma((2,))],
        compiler_params=pltpu.CompilerParams(
            collective_id=1, has_side_effects=True, vmem_limit_bytes=VMEM_LIMIT
        ),
        name="middle",
    )(
        o_all, wo, up_g.reshape(width, share), down_g.reshape(share, width), vecs,
        hidden_in, out_cotangent,
    )

    input_grad, qkvg, upg, dng, outg, vecg, qvg = pl.pallas_call(
        backward_kernel,
        out_shape=(
            shape((rows, width), F32),
            shape((SP, slim, cols), BF),
            shape((slim, SP * share), F32),
            shape((deep, width), F32),
            shape((slim, width), F32),
            shape((16, 128), F32),
            shape((8, 128), F32),
        ),
        in_specs=[smem] + [vmem] * 11,
        out_specs=(vmem,) * 7,
        scratch_shapes=[
            pltpu.VMEM((YG, LH, HEAD_DIM, tall), F32),
            pltpu.VMEM((YG, LH * HEAD_DIM, tall), BF),
            pltpu.VMEM((XG, LH, tall, 128), BF),
            pltpu.VMEM((XG - 1, LH, tall, 128), BF),
            pltpu.VMEM((YG - 1, LH * HEAD_DIM, tall), BF),
            pltpu.VMEM((tall, cols), BF),
            pltpu.VMEM((width, cols), F32),
            pltpu.VMEM((FS, slim, cols), BF),
            pltpu.VMEM((FS, 8, 128), F32),
            pltpu.VMEM((tall, width), BF),
            pltpu.VMEM((rows, width), F32),
            pltpu.VMEM((SP - 1, rows, width), BF),
            pltpu.VMEM((FS - 1, slim, cols), BF),
            pltpu.VMEM((FS - 1, slim, share), BF),
            pltpu.VMEM((8, deep, width), BF),
            pltpu.VMEM((8, slim, width), BF),
            pltpu.VMEM((FS - 1, 16, 128), F32),
            pltpu.VMEM((FS - 1, 8, 128), F32),
            pltpu.VMEM((SP, slim, share), BF),
            pltpu.VMEM((SP, deep, width), BF),
            pltpu.VMEM((SP, slim, width), BF),
            pltpu.VMEM((SP, 16, 128), F32),
            pltpu.VMEM((SP, 8, 128), F32),
        ]
        + [dma((n,)) for n in (7, 7, 3, 3, 31, 31, 31, 31, 8, 8, 8, 8, 31, 31, 31, 31, 3, 3)]
        + [dma((6, 3)), dma((6, 3))],
        compiler_params=pltpu.CompilerParams(
            collective_id=2, has_side_effects=True, vmem_limit_bytes=VMEM_LIMIT
        ),
        name="backward",
    )(
        valid_length, q_all, d_all, ld_all, kv_all, hid_all, wqkv, gfs,
        dup.reshape(FS, slim, share), ddn.reshape(8, deep, width), dwo.reshape(8, slim, width), vp,
    )

    kv_grad = qkvg[:, :, : LH * 128].reshape(SP, slim, LH, 2, HEAD_DIM)
    q_grad = qkvg[:, :, LH * 128 :].reshape(SP, slim, LH, 1, HEAD_DIM)
    qkv_grad = jnp.concatenate((q_grad, kv_grad), axis=3)
    qkv_grad = jnp.transpose(qkv_grad, (1, 3, 0, 2, 4)).reshape(slim, -1).astype(F32)
    return (
        result,
        input_grad,
        qkv_grad,
        qvg[0, :slim],
        qvg[1, :slim],
        outg,
        vecg[0, :slim],
        vecg[1, :slim],
        vecg[2, :slim],
        upg,
        vecg[8, :deep],
        dng,
        vecg[3, :slim],
        vecg[4, :slim],
        vecg[5, :slim],
    )


def solution(mesh):
    placed = (
        P(("fsdp", "sp"), None),
        P("fsdp", None),
        P("fsdp"),
        P("fsdp"),
        P("fsdp", None),
        P("fsdp"),
        P("fsdp"),
        P("fsdp"),
        P("fsdp", None),
        P("fsdp"),
        P("fsdp", None),
        P("fsdp"),
        P("fsdp"),
        P("fsdp"),
        P(),
        P(("fsdp", "sp"), None),
    )
    return jax.shard_map(
        on_device,
        mesh=mesh,
        in_specs=placed,
        out_specs=(
            P(("fsdp", "sp"), None),
            P(("fsdp", "sp"), None),
            P("fsdp", None),
            P("fsdp"),
            P("fsdp"),
            P("fsdp", None),
            P("fsdp"),
            P("fsdp"),
            P("fsdp"),
            P("fsdp", None),
            P("fsdp"),
            P("fsdp", None),
            P("fsdp"),
            P("fsdp"),
            P("fsdp"),
        ),
        check_vma=False,
    )
```

```python
import functools

import jax
import jax.numpy as jnp
from jax import lax
from jax.experimental import pallas as pl
from jax.experimental.pallas import tpu as pltpu
from jax.sharding import PartitionSpec as P

HEADS = 12
HEAD_DIM = 64
SP = 4
FS = 32
YG = 4
XG = 8
LH = HEADS // SP

KEY_STEPS = ((0, 1), (0, 3), (1, 0), (0, 2), (1, 1), (1, 3), (1, 2))
PASSES = ((0, 1, 2), (3, 4, 5, 6))

BF = jnp.bfloat16
F32 = jnp.float32
MESH = pl.DeviceIdType.MESH
epsilon = 1e-05
masked = -1e30
VMEM_LIMIT = 56 * 1024 * 1024


def dot_nn(a, b):
    return lax.dot_general(a, b, (((1,), (0,)), ((), ())), preferred_element_type=F32)


def dot_nt(a, b):
    return lax.dot_general(a, b, (((1,), (1,)), ((), ())), preferred_element_type=F32)


def dot_tn(a, b):
    return lax.dot_general(a, b, (((0,), (0,)), ((), ())), preferred_element_type=F32)


def norm_forward(incoming, norm_gain, norm_shift):
    row_mean = jnp.mean(incoming, axis=-1, keepdims=True)
    centered = incoming - row_mean
    inverse = lax.rsqrt(jnp.mean(centered * centered, axis=-1, keepdims=True) + epsilon)
    normed = centered * inverse
    return (normed * norm_gain + norm_shift, normed, inverse)


def norm_backward(incoming, normed, inverse, norm_gain):
    scaled = incoming * norm_gain
    adjusted = (
        scaled
        - jnp.mean(scaled, axis=-1, keepdims=True)
        - normed * jnp.mean(scaled * normed, axis=-1, keepdims=True)
    )
    return (
        adjusted * inverse,
        jnp.sum(incoming * normed, axis=0, keepdims=True),
        jnp.sum(incoming, axis=0, keepdims=True),
    )


def loop(low, high, body):
    def step(d, carried):
        body(d)
        return carried

    lax.fori_loop(low, high, step, 0)


def remote(src, dst, send, recv, **device):
    return pltpu.make_async_remote_copy(
        src_ref=src,
        dst_ref=dst,
        send_sem=send,
        recv_sem=recv,
        device_id=device,
        device_id_type=MESH,
    )


def greet(barrier, **device):
    pl.semaphore_signal(barrier, inc=1, device_id=device, device_id_type=MESH)


def greet_all(f, s):
    barrier = pltpu.get_barrier_semaphore()
    loop(1, FS, lambda d: greet(barrier, fsdp=lax.rem(f + d, FS)))
    loop(1, SP, lambda d: greet(barrier, sp=lax.rem(s + d, SP)))

    @pl.when(s != f // 8)
    def _():
        loop(0, 8, lambda t: greet(barrier, fsdp=8 * s + t, sp=f // 8))

    pl.semaphore_wait(barrier, FS - 1 + SP - 1 + jnp.where(s != f // 8, 8, 0))


def forward_kernel(
    valid, hid, wq, out,
    hid_all, wqkv, q_all, kv_all, o_all, out_g, vecs,
    wq_g, wf, q_st, kv_st, qvb, state, o_st,
    hid_s, hid_r, wq_s, wq_r, ou_s, ou_r,
    q_s, q_r, kv_s, kv_r, o_s, o_r, loc,
):
    s = lax.axis_index("sp")
    f = lax.axis_index("fsdp")
    i, j = f // YG, lax.rem(f, YG)
    greet_all(f, s)
    rows = hid.shape[0]

    def hid_copy(d):
        dst = hid_all.at[pl.ds(s * rows, rows)]
        return remote(hid, dst, hid_s.at[d - 1], hid_r.at[d - 1], sp=lax.rem(s + d, SP))

    def fs_copy(src, buf, send, recv):
        return lambda d: remote(
            src, buf.at[f], send.at[d - 1], recv.at[d - 1], fsdp=lax.rem(f + d, FS)
        )

    wq_copy = fs_copy(wq, wq_g, wq_s, wq_r)

    def out_copy(t):
        k = lax.rem(f, 8)
        return remote(out, out_g.at[k], ou_s.at[t], ou_r.at[k], fsdp=8 * s + t, sp=f // 8)

    def out_arrival(k):
        return remote(out, out_g.at[k], ou_s.at[k], ou_r.at[k], fsdp=8 * s + k, sp=f // 8)

    def is_self(t):
        return (s == f // 8) & (8 * s + t == f)

    loop(1, SP, lambda d: hid_copy(d).start())

    loop(1, FS, lambda d: wq_copy(d).start())
    hid_all[pl.ds(pl.multiple_of(s * rows, rows), rows), :] = hid[...]
    wq_g[f] = wq[...]
    loop(1, SP, lambda d: hid_copy(d).wait())

    loop(1, FS, lambda d: wq_copy(d).wait())

    width = vecs.shape[1]
    pad = jnp.zeros((8, width - 64), F32)

    def riders(n, low):
        block = wq_g[n, low : low + 8, 512:640].astype(F32)
        wide = jnp.concatenate((block[:, 64:128], pad), axis=1)
        return wide

    def shifted(wide, amount):
        return wide if amount == 0 else pltpu.roll(wide, amount, 1)

    qv = jnp.zeros((8, width), F32)
    for n in range(8):
        qv = qv + shifted(riders(8 * s + n, 0), 24 * n)
    qvb[...] = qv
    lane = lax.broadcasted_iota(jnp.int32, (1, width), 1)
    qrow = qvb[0:1, :]
    vrow = qvb[1:2, :]
    bias = jnp.zeros((1, width), F32)
    wide_q = jnp.broadcast_to(qrow, (8, width))
    wide_v = jnp.broadcast_to(vrow, (8, width))
    bias = jnp.where((lane >= 384) & (lane < 576), pltpu.roll(wide_q, 384, 1)[0:1], 0.0)
    for h in range(LH):
        here = (lane >= 128 * h + 64) & (lane < 128 * h + 128)
        bias = bias + jnp.where(here, pltpu.roll(wide_v, 64 * h + 64, 1)[0:1], 0.0)

    def assemble(n):
        wf[pl.ds(pl.multiple_of(24 * n, 8), 24), :] = wq_g[n, :, 0:576].astype(F32)

    loop(0, FS, assemble)
    wqkv[...] = wf[...].astype(BF)

    low_lane = lax.broadcasted_iota(jnp.int32, (rows, 128), 1) < HEAD_DIM

    def project(b):
        at = pl.ds(pl.multiple_of(b * rows, rows), rows)
        p = dot_nn(hid_all[at, :], wqkv[...]) + bias[:, :576]
        for h in range(LH):
            kv_st[h, at, :] = p[:, 128 * h : 128 * h + 128].astype(BF)
        q01 = p[:, 384:512] * 0.125
        q2 = jnp.concatenate((p[:, 512:576], jnp.zeros((rows, 64), F32)), axis=1) * 0.125
        q_st[0, at, :] = jnp.where(low_lane, q01, 0.0).astype(BF)
        q_st[1, at, :] = jnp.where(low_lane, pltpu.roll(q01, 64, 1), 0.0).astype(BF)
        q_st[2, at, :] = q2.astype(BF)

    loop(0, SP, project)

    def kv_copy(n):
        dz, dx = KEY_STEPS[n]
        to = lax.rem(i // YG + dz, 2) * YG + lax.rem(i + dx, YG)
        return remote(kv_st, kv_all.at[i], kv_s.at[n], kv_r.at[n], fsdp=to * YG + j)

    def kv_from(n):
        dz, dx = KEY_STEPS[n]
        return lax.rem(i // YG + dz, 2) * YG + lax.rem(i + YG - dx, YG)

    def q_copy(d):
        to = i * YG + lax.rem(j + d, YG)
        return remote(q_st, q_all.at[j], q_s.at[d - 1], q_r.at[d - 1], fsdp=to)

    loop(1, YG, lambda d: q_copy(d).start())
    for n in range(XG - 1):
        kv_copy(n).start()
    kv_all[i] = kv_st[...]
    q_all[j] = q_st[...]

    total = jnp.zeros((8, width), F32)
    for n in range(FS):
        total = total + shifted(riders(n, 0), 24 * n)
    vecs[0:8, :] = total
    ub = jnp.zeros((8, width), F32)
    for n in range(8):
        rider = riders(8 * s + n, 8)
        for c in range(4):
            row = jnp.broadcast_to(rider[c : c + 1], (8, width))
            ub = ub + shifted(row, 96 * n + 24 * c)
    vecs[8:16, :] = ub

    def send_out(t):
        @pl.when(jnp.logical_not(is_self(t)))
        def _():
            out_copy(t).start()

    loop(0, 8, send_out)

    @pl.when(s == f // 8)
    def _():
        out_own = pltpu.make_async_copy(out, out_g.at[lax.rem(f, 8)], loc.at[0])
        out_own.start()
        out_own.wait()

    tall = SP * rows
    key_place = lax.broadcasted_iota(jnp.int32, (1, tall), 1)
    lanes = lax.broadcasted_iota(jnp.int32, (tall, 128), 1)

    def o_copy(d, h):
        to = lax.rem(j + YG - d, YG)
        src = o_st.at[to, h]
        return remote(src, o_all.at[j, h], o_s.at[d - 1, h], o_r.at[d - 1, h], fsdp=i * YG + to)

    def attend(places, is_first, is_last):
        limits = [
            jnp.where((at * YG + j) * tall + key_place < valid[0], 0.0, masked) for at in places
        ]

        def tile(t):
            d = t // LH
            h = lax.rem(t, LH)
            n = lax.rem(j + YG - d, YG)
            if is_first:

                @pl.when((d > 0) & (h == 0))
                def _():
                    q_copy(d).wait_recv()

            query = q_all[n, h]
            m = l = acc = None
            if not is_first:
                acc = state[n, h]
                m, l = acc[:, 0:1], acc[:, 32:33]
            for at, limit in zip(places, limits):
                block = kv_all[at, h]
                scores = dot_nt(query, block) + limit
                top = jnp.max(scores, axis=1, keepdims=True)
                new = top if m is None else jnp.maximum(m, top)
                p = jnp.exp(scores - new)
                part = jnp.sum(p, axis=1, keepdims=True)
                weighted = dot_nn(p.astype(BF), block)
                if m is None:
                    l, acc = part, weighted
                else:
                    decay = jnp.exp(m - new)
                    l = l * decay + part
                    acc = acc * decay + weighted
                m = new
            if is_last:
                log_sum = m + jnp.log(l)
                high = log_sum.astype(BF).astype(F32)
                logs = jnp.where(lanes < 32, high, log_sum - high)
                o_st[n, h] = jnp.where(lanes >= 64, acc / l, logs).astype(BF)
            else:
                state[n, h] = jnp.where(lanes >= 64, acc, jnp.where(lanes < 32, m, l))
            if is_last:

                @pl.when(d > 0)
                def _():
                    o_copy(d, h).start()

                @pl.when(d == 0)
                def _():
                    o_all[j, h] = o_st[j, h]

        if is_last:
            loop(LH, LH * YG, tile)
            loop(0, LH, tile)
        else:
            loop(0, LH * YG, tile)

    for step, members in enumerate(PASSES):
        for n in members:
            kv_copy(n).wait_recv()
        places = [kv_from(n) for n in members]
        attend(places if step else [i] + places, step == 0, step == len(PASSES) - 1)

    for n in range(XG - 1):
        kv_copy(n).wait_send()
    loop(1, YG, lambda d: q_copy(d).wait_send())

    def owned_wait(t):
        @pl.when(jnp.logical_not(is_self(t)))
        def _():
            out_copy(t).wait_send()
            out_arrival(t).wait_recv()

    loop(0, 8, owned_wait)
    loop(1, YG, lambda d: loop(0, LH, lambda h: o_copy(d, h).wait()))


def middle_kernel(
    o_all, out_g, up, down, vecs, hid, cot,
    result, gfs, d_all, ld_all, up_own, up_rb, dn_rb, dwo, vp,
    up_g, wf, wo, wup, wdn, dup, ddn,
    att, ld, st, own, first, n1, inv1, x_all, act, deriv, gd, gp, gb, gsec, rb, dbuf, ldrow, vg,
    ag_s, ag_r, rs_s, rs_r, d_s, d_r, l_s, l_r, loc,
    ua_s, ua_r, ub_s, ub_r, dn_s, dn_r, us_s, us_r, ds_s, ds_r,
):
    s = lax.axis_index("sp")
    f = lax.axis_index("fsdp")
    i, j = f // YG, lax.rem(f, YG)
    rows = hid.shape[0]
    tall = SP * rows
    z, x = f // 16, lax.rem(i, YG)
    greet_all(f, s)

    def zy_copy(n):
        to = (lax.rem(z + (n + 1) // YG, 2) * YG + x) * YG + lax.rem(j + n + 1, YG)
        return remote(up, up_g.at[f], ua_s.at[n], ua_r.at[n], fsdp=to)

    def x_copy(d):
        to = (z * YG + lax.rem(x + d, YG)) * YG + j
        copies = []
        for n in range(2):
            at = up_g.at[pl.ds((n * YG + x) * YG, YG)]
            copies.append(remote(at, at, ub_s.at[d - 1, n], ub_r.at[d - 1, n], fsdp=to))
        return copies

    def down_copy(t):
        k = lax.rem(f, 8)
        dst = wdn.at[pl.ds(k * 96, 96)]
        return remote(down, dst, dn_s.at[t], dn_r.at[k], fsdp=8 * s + t, sp=f // 8)

    def down_arrival(k):
        dst = wdn.at[pl.ds(k * 96, 96)]
        return remote(down, dst, dn_s.at[k], dn_r.at[k], fsdp=8 * s + k, sp=f // 8)

    def is_self(t):
        return (s == f // 8) & (8 * s + t == f)

    def unless_self(work):
        def step(t):
            @pl.when(jnp.logical_not(is_self(t)))
            def _():
                work(t)

        loop(0, 8, step)

    for n in range(XG - 1):
        zy_copy(n).start()
    unless_self(lambda t: down_copy(t).start())
    up_g[f] = up[...]

    @pl.when(s == f // 8)
    def _():
        wdn[pl.ds(pl.multiple_of(lax.rem(f, 8) * 96, 32), 96), :] = down[...]

    wf[0:192, :] = out_g[...].astype(F32).reshape(192, wf.shape[1])
    for h in range(LH):
        wo[128 * h : 128 * h + 64, :] = jnp.zeros((64, wo.shape[1]), BF)
        wo[128 * h + 64 : 128 * h + 128, :] = wf[64 * h : 64 * h + 64, :].astype(BF)

    def y_peer(d):
        return i * YG + lax.rem(j + d, YG)

    def span(b):
        return pl.ds(pl.multiple_of(b * rows, rows), rows)

    lane = lax.broadcasted_iota(jnp.int32, (rows, 128), 1)

    def merge(b):
        at = span(b)
        sums = jnp.zeros((rows, 128), F32)
        for h in range(LH):
            parts = [o_all[d, h, at, :].astype(F32) for d in range(YG)]
            logs = [p[:, 0:1] + p[:, 32:33] for p in parts]
            top = functools.reduce(jnp.maximum, logs)
            weights = [jnp.exp(g - top) for g in logs]
            total = functools.reduce(jnp.add, weights)
            merged = functools.reduce(jnp.add, [p * w for p, w in zip(parts, weights)]) / total
            att[at, 128 * h : 128 * h + 128] = jnp.where(lane >= 64, merged, 0.0).astype(BF)
            sums = jnp.where(lane == 2 * h, top + jnp.log(total), sums)
        ld[at, :] = sums

    loop(0, SP, merge)

    def gather(e, buf):
        def copy(d):
            at = buf.at[pl.ds(s * rows, rows)]
            return remote(at, at, ag_s.at[e, d - 1], ag_r.at[e, d - 1], sp=lax.rem(s + d, SP))

        return copy

    def scatter(e):
        def copy(d):
            src = st.at[e, pl.ds(lax.rem(s + d, SP) * rows, rows)]
            sems = (rs_s.at[e, d - 1], rs_r.at[e, d - 1])
            return remote(src, rb.at[e, d - 1], *sems, sp=lax.rem(s + d, SP))

        return copy

    def collect(e):
        loop(1, SP, lambda d: scatter(e)(d).wait())
        total = own[...]
        for d in range(SP - 1):
            total = total + rb[e, d].astype(F32)
        return total

    def out_part(d):
        b = lax.rem(s + d, SP)
        value = dot_nn(att[span(b), :], wo[...])

        @pl.when(d < SP)
        def _():
            st[0, span(b), :] = value.astype(BF)
            scatter(0)(d).start()

        @pl.when(d == SP)
        def _():
            own[...] = value

    loop(1, SP + 1, out_part)
    for n in range(XG - 1):
        zy_copy(n).wait()
    for d in range(1, YG):
        for copy in x_copy(d):
            copy.start()
    summed = hid[...].astype(F32) + collect(0) + vecs[2:3, :]
    value, normed, inverse = norm_forward(summed, vecs[3:4, :], vecs[4:5, :])
    first[...] = value
    n1[...] = normed
    inv1[...] = jnp.broadcast_to(inverse, inv1.shape)
    x_all[span(s), :] = value.astype(BF)
    loop(1, SP, lambda d: gather(0, x_all)(d).start())

    for d in range(1, YG):
        for copy in x_copy(d):
            copy.wait()

    def assemble(n):
        wf[pl.ds(pl.multiple_of(24 * n, 8), 24), :] = up_g[n].astype(F32)

    loop(0, FS, assemble)
    wup[...] = wf[...].astype(BF)
    unless_self(lambda t: (down_copy(t).wait_send(), down_arrival(t).wait_recv()))

    def pipeline(e, buf, work):
        def step(d):
            b = lax.rem(s + SP - d, SP)

            @pl.when(d > 0)
            def _():
                gather(e, buf)(d).wait_recv()

            value = work(b)

            @pl.when(d > 0)
            def _():
                st[e + 1, span(b), :] = value.astype(BF)
                scatter(e + 1)(SP - d).start()

            @pl.when(d == 0)
            def _():
                own[...] = value

        loop(0, SP, step)
        loop(1, SP, lambda d: gather(e, buf)(d).wait_send())

    def feed(b):
        at = span(b)
        pre = dot_nn(x_all[at, :], wup[...]) + vecs[8:9, :]
        cdf = 0.5 * (1.0 + lax.erf(pre * 0.7071067811865476))
        density = jnp.exp(-0.5 * pre * pre) * 0.3989422804014327
        active = (pre * cdf).astype(BF)
        act[at, :] = active
        deriv[at, :] = cdf + pre * density
        return dot_nn(active, wdn[...])

    pipeline(0, x_all, feed)
    summed = first[...] + collect(1) + vecs[5:6, :]
    value, normed, inverse = norm_forward(summed, vecs[6:7, :], vecs[7:8, :])
    result[...] = value.astype(BF)
    grad, ggain, gshift = norm_backward(cot[...].astype(F32), normed, inverse, vecs[6:7, :])
    gsec[...] = grad
    low = grad.astype(BF)
    gd[span(s), :] = low
    loop(1, SP, lambda d: gather(1, gd)(d).start())
    vg[...] = jnp.zeros(vg.shape, F32)
    vg[3:4, :] = jnp.sum(low.astype(F32), axis=0, keepdims=True)
    vg[4:5, :] = ggain
    vg[5:6, :] = gshift

    def back(b):
        at = span(b)
        grad_pre = (dot_nt(gd[at, :], wdn[...]) * deriv[at, :]).astype(BF)
        gp[at, :] = grad_pre
        return dot_nt(grad_pre, wup[...])

    pipeline(1, gd, back)

    def weight_terms(c):
        at = pl.ds(pl.multiple_of(128 * c, 128), 128)
        wf[at, :] = dot_tn(x_all[:, at], gp[...])
        ddn[at, :] = dot_tn(act[:, at], gd[...]).astype(BF)

    loop(0, act.shape[1] // 128, weight_terms)

    def cut(n):
        dup[n] = wf[pl.ds(pl.multiple_of(24 * n, 8), 24), :].astype(BF)

    loop(0, FS, cut)

    def up_sum(d):
        to = lax.rem(x + d, YG)
        copies = []
        for n in range(2):
            src = dup.at[pl.ds((n * YG + to) * YG, YG)]
            sems = (us_s.at[d - 1, n], us_r.at[d - 1, n])
            copies.append(remote(src, up_rb.at[d - 1, n], *sems, fsdp=(z * YG + to) * YG + j))
        return copies

    def down_sum(t):
        k = lax.rem(f, 8)
        src = ddn.at[pl.ds(t * 96, 96)]
        return remote(src, dn_rb.at[k], ds_s.at[t], ds_r.at[k], fsdp=8 * s + t, sp=f // 8)

    def down_sum_arrival(k):
        src = ddn.at[pl.ds(k * 96, 96)]
        return remote(src, dn_rb.at[k], ds_s.at[k], ds_r.at[k], fsdp=8 * s + k, sp=f // 8)

    for d in range(1, YG):
        for copy in up_sum(d):
            copy.start()
    unless_self(lambda t: down_sum(t).start())
    for n in range(2):
        up_own[n] = dup[pl.ds((n * YG + x) * YG, YG)]

    @pl.when(s == f // 8)
    def _():
        k = lax.rem(f, 8)
        dn_rb[k] = ddn[pl.ds(pl.multiple_of(k * 96, 32), 96), :]

    ub = jnp.sum(gp[...].astype(F32), axis=0, keepdims=True)
    grad_first = gsec[...] + collect(2)
    grad, ggain, gshift = norm_backward(grad_first, n1[...], inv1[:, 0:1], vecs[3:4, :])
    gfs[...] = grad
    low = grad.astype(BF)
    gb[span(s), :] = low
    loop(1, SP, lambda d: gather(2, gb)(d).start())
    vg[0:1, :] = jnp.sum(low.astype(F32), axis=0, keepdims=True)
    vg[1:2, :] = ggain
    vg[2:3, :] = gshift

    def branch(d):
        b = lax.rem(s + SP - d, SP)
        at = span(b)

        @pl.when(d > 0)
        def _():
            gather(2, gb)(d).wait_recv()

        value = dot_nt(gb[at, :], wo[...]).astype(BF)
        sums = ld[at, :]
        for h in range(LH):
            part = value[:, 128 * h : 128 * h + 128]
            dbuf[h, at, :] = part
            product = part.astype(F32) * att[at, 128 * h : 128 * h + 128].astype(F32)
            sums = jnp.where(lane == 2 * h + 1, jnp.sum(product, axis=1, keepdims=True), sums)
        ld[at, :] = sums
        loop(1, YG, lambda n: d_copy(n, d).start())

    def d_copy(n, d):
        at = span(lax.rem(s + SP - d, SP))
        sems = (d_s.at[n - 1, d], d_r.at[n - 1, d])
        return remote(dbuf.at[:, at], d_all.at[j, :, at], *sems, fsdp=y_peer(n))

    loop(0, SP, branch)
    loop(1, SP, lambda d: gather(2, gb)(d).wait_send())
    ldrow[...] = jnp.transpose(ld[...], (1, 0))[0:8, :]

    def l_copy(d):
        return remote(ldrow, ld_all.at[j], l_s.at[d - 1], l_r.at[d - 1], fsdp=y_peer(d))

    loop(1, YG, lambda d: l_copy(d).start())
    d_own = pltpu.make_async_copy(dbuf, d_all.at[j], loc.at[0])
    l_own = pltpu.make_async_copy(ldrow, ld_all.at[j], loc.at[1])
    d_own.start()
    l_own.start()
    for h in range(LH):
        value = dot_tn(att[:, 128 * h : 128 * h + 128], gb[...])
        dwo[64 * h : 64 * h + 64, :] = value[64:128].astype(BF)
    lane8 = lax.broadcasted_iota(jnp.int32, (8, 128), 1)
    wide = vg[...]
    width = wide.shape[1]
    ub_wide = jnp.broadcast_to(ub, (8, width))
    for n in range(FS):
        piece = wide if n == 0 else pltpu.roll(wide, width - 24 * n, 1)
        vp[n, 0:8, :] = jnp.where(lane8 < 24, piece[:, 0:128], 0.0)
        vp[n, 8:16, :] = jnp.zeros((8, 128), F32)
    for k in range(8):
        piece = ub_wide if k == 0 else pltpu.roll(ub_wide, width - 96 * k, 1)
        vp[8 * s + k, 8:16, :] = jnp.where(lane8 < 96, piece[:, 0:128], 0.0)
    d_own.wait()
    l_own.wait()
    loop(1, YG, lambda n: loop(0, SP, lambda d: d_copy(n, d).wait()))
    loop(1, YG, lambda d: l_copy(d).wait())
    for d in range(1, YG):
        for copy in up_sum(d):
            copy.wait()
    unless_self(lambda t: (down_sum(t).wait_send(), down_sum_arrival(t).wait_recv()))


def backward_kernel(
    valid, q_all, d_all, ld, kv_all, hid_all, wqkv, gfs, up_own, up_rb, dn_rb, dwo, vp,
    input_grad, wkg, wqg, upg, dng, outg, vecg,
    acc, dq, dkv, kv_rb, q_rb, g, wf, wk, wp, st, own, rb, wk_rb, wq_rb, up_st, up_rc, ou_rb, vp_rb,
    up_fin, dn_fin, ou_fin, v_fin, wk_fin, wq_fin,
    kv_s, kv_r, q_s, q_r, wk_s, wk_r, wq_s, wq_r, up_s, up_r, ou_s, ou_r, vp_s, vp_r,
    rs_s, rs_r, fin_s, fin_r,
):
    s = lax.axis_index("sp")
    f = lax.axis_index("fsdp")
    i, j = f // YG, lax.rem(f, YG)
    rows = gfs.shape[0]
    tall = SP * rows
    greet_all(f, s)

    def kv_copy(d):
        to = lax.rem(i + d, XG)
        return remote(dkv.at[d - 1], kv_rb.at[d - 1], kv_s.at[d - 1], kv_r.at[d - 1], fsdp=to * YG + j)

    def q_copy(d):
        to = lax.rem(j + d, YG)
        return remote(dq.at[to], q_rb.at[d - 1], q_s.at[d - 1], q_r.at[d - 1], fsdp=i * YG + to)

    def fs_copy(src, buf, send, recv):
        def copy(d):
            to = lax.rem(f + d, FS)
            return remote(src.at[to], buf.at[d - 1], send.at[d - 1], recv.at[d - 1], fsdp=to)

        return copy

    vp_copy = fs_copy(vp, vp_rb, vp_s, vp_r)
    wq_copy = fs_copy(wp, wq_rb, wq_s, wq_r)
    wk_copy = fs_copy(wk, wk_rb, wk_s, wk_r)
    z, x = f // 16, lax.rem(i, YG)

    def up_copy(n):
        zn, yn = lax.rem(z + (n + 1) // YG, 2), lax.rem(j + n + 1, YG)
        to = (zn * YG + x) * YG + yn
        return remote(up_st.at[zn * YG + yn], up_rc.at[n], up_s.at[n], up_r.at[n], fsdp=to)

    def out_copy(k):
        n = lax.rem(f, 8)
        return remote(dwo.at[k], ou_rb.at[n], ou_s.at[k], ou_r.at[n], fsdp=8 * s + k, sp=f // 8)

    def out_arrival(n):
        return remote(dwo.at[n], ou_rb.at[n], ou_s.at[n], ou_r.at[n], fsdp=8 * s + n, sp=f // 8)

    def is_self(t):
        return (s == f // 8) & (8 * s + t == f)

    for n in range(2):
        for c in range(YG):
            total = up_own[n, c].astype(F32)
            for d in range(YG - 1):
                total = total + up_rb[d, n, c].astype(F32)
            up_st[n * YG + c] = total.astype(BF)
    for n in range(XG - 1):
        up_copy(n).start()
    loop(1, FS, lambda d: vp_copy(d).start())

    def to_owner(k):
        @pl.when(jnp.logical_not(is_self(k)))
        def _():
            out_copy(k).start()

        @pl.when(is_self(k))
        def _():
            ou_rb[k] = dwo[k]

    loop(0, 8, to_owner)

    def down_rows(c):
        at = pl.ds(pl.multiple_of(c * 32, 32), 32)
        total = dn_rb[0, at, :].astype(F32)
        for n in range(1, 8):
            total = total + dn_rb[n, at, :].astype(F32)
        dn_fin[s, at, :] = total.astype(BF)

    loop(0, dn_fin.shape[1] // 32, down_rows)

    acc[...] = jnp.zeros(acc.shape, F32)

    def key_step(d):
        at = lax.rem(i + d, XG)
        first_key = (at * YG + j) * tall

        def head(h):
            def work(last):
                block = kv_all[at, h]
                flipped = jnp.transpose(block.astype(F32), (1, 0))[0:HEAD_DIM].astype(BF)
                total = None
                for n in range(YG):
                    query = q_all[n, h]
                    grad = d_all[n, h]
                    log_sum = ld[n, pl.ds(2 * h, 1), :]
                    delta = ld[n, pl.ds(2 * h + 1, 1), :]
                    scores = dot_nt(block, query)
                    if last:
                        place = first_key + lax.broadcasted_iota(jnp.int32, (tall, 1), 0)
                        scores = jnp.where(place < valid[0], scores, masked)
                    p = jnp.exp(scores - log_sum)
                    grad_p = dot_nt(block, grad)
                    grad_s = (p * (grad_p - delta)).astype(BF)
                    terms = dot_nn(grad_s, query) + dot_nn(p.astype(BF), grad)
                    total = terms if n == 0 else total + terms
                    acc[n, h] = acc[n, h] + dot_nn(flipped, grad_s)
                dkv[d - 1, h] = total.astype(BF)

            @pl.when(at < XG - 1)
            def _():
                work(False)

            @pl.when(at == XG - 1)
            def _():
                work(True)

        loop(0, LH, head)

        @pl.when(d < XG)
        def _():
            kv_copy(d).start()

    loop(1, XG + 1, key_step)
    for n in range(YG):
        for h in range(LH):
            dq[n, 64 * h : 64 * h + 64, :] = acc[n, h].astype(BF)
    loop(1, YG, lambda d: q_copy(d).start())

    def span(b):
        return pl.ds(pl.multiple_of(b * rows, rows), rows)

    def sum_keys(b):
        at = span(b)
        for h in range(LH):
            total = dkv[XG - 1, h, at, :].astype(F32)
            for d in range(XG - 1):
                total = total + kv_rb[d, h, at, :].astype(F32)
            g[at, 128 * h : 128 * h + 128] = total.astype(BF)

    loop(1, XG, lambda d: kv_copy(d).wait())
    loop(0, SP, sum_keys)

    def key_terms(c):
        at = pl.ds(pl.multiple_of(128 * c, 128), 128)
        wf[at, 0:384] = dot_tn(hid_all[:, at], g[:, 0:384])

    loop(0, wf.shape[0] // 128, key_terms)

    def cut_keys(n):
        wk[n] = wf[pl.ds(pl.multiple_of(24 * n, 8), 24), 0:384].astype(BF)

    loop(0, FS, cut_keys)
    loop(1, FS, lambda d: wk_copy(d).start())

    def add_up(buf, start):
        def step(d, total):
            return total + buf[d].astype(F32)

        return lax.fori_loop(0, buf.shape[0], step, start)

    for n in range(XG - 1):
        up_copy(n).wait()
    loop(1, FS, lambda d: vp_copy(d).wait())
    up_fin[s] = add_up(up_rc, up_st[z * YG + j].astype(F32)).astype(BF)
    v_fin[s] = add_up(vp_rb, vp[f])

    def owner_wait(t):
        @pl.when(jnp.logical_not(is_self(t)))
        def _():
            out_copy(t).wait_send()
            out_arrival(t).wait_recv()

    loop(0, 8, owner_wait)
    ou_fin[s] = add_up(ou_rb, jnp.zeros(ou_fin.shape[1:], F32)).astype(BF)

    def sp_copy(e, buf):
        def copy(d):
            at = buf.at[s]
            return remote(at, at, fin_s.at[e, d - 1], fin_r.at[e, d - 1], sp=lax.rem(s + d, SP))

        return copy

    early_bufs = ((0, up_fin), (1, v_fin), (4, dn_fin), (5, ou_fin))
    for e, buf in early_bufs:
        loop(1, SP, lambda d: sp_copy(e, buf)(d).start())

    loop(1, YG, lambda d: q_copy(d).wait())
    total = dq[j].astype(F32)
    for d in range(YG - 1):
        total = total + q_rb[d].astype(F32)
    g[:, 384:576] = (jnp.transpose(total, (1, 0)) * 0.125).astype(BF)

    def query_terms(c):
        at = pl.ds(pl.multiple_of(128 * c, 128), 128)
        value = dot_tn(hid_all[:, at], g[:, 384:576])
        wf[at, 384:640] = jnp.concatenate((value, jnp.zeros((128, 64), F32)), axis=1)

    loop(0, wf.shape[0] // 128, query_terms)

    sums = jnp.sum(g[...].astype(F32), axis=0, keepdims=True)
    row = lax.broadcasted_iota(jnp.int32, (8, 256), 0)
    low = lax.broadcasted_iota(jnp.int32, (8, 128), 1) < 64
    wide = jnp.broadcast_to(jnp.concatenate((sums, jnp.zeros((1, 64), F32)), axis=1), (8, 640))
    heads = [pltpu.roll(wide[:, 128 * h : 128 * h + 128], 64, 1) for h in range(LH)]
    vrow = jnp.concatenate(
        (jnp.where(low, heads[0], wide[:, 128:256]), jnp.where(low, heads[2], 0.0)), axis=1
    )
    both = jnp.where(row == 0, wide[:, 384:640], jnp.where(row == 1, vrow, 0.0))

    def cut_queries(n):
        wp[n] = wf[pl.ds(pl.multiple_of(24 * n, 8), 24), 384:640].astype(BF)

    loop(0, FS, cut_queries)
    lane = lax.broadcasted_iota(jnp.int32, (8, 128), 1)
    for n in range(8):
        piece = both if n == 0 else pltpu.roll(both, 256 - 24 * n, 1)
        piece = pltpu.roll(piece[:, 0:128], 64, 1)
        piece = jnp.where((lane >= 64) & (lane < 88), piece, 0.0)
        rest = jnp.concatenate((piece, jnp.zeros((16, 128), F32)), axis=0)
        kept = wp[8 * s + n, :, 128:256].astype(F32)
        lanes = lax.broadcasted_iota(jnp.int32, (24, 128), 1)
        wp[8 * s + n, :, 128:256] = jnp.where(lanes < 64, kept, rest).astype(BF)
    loop(1, FS, lambda d: wq_copy(d).start())

    def input_part(d):
        b = lax.rem(s + d, SP)
        value = dot_nt(g[span(b), :], wqkv[...])

        @pl.when(d < SP)
        def _():
            st[span(b), :] = value.astype(BF)
            rs_copy(d).start()

        @pl.when(d == SP)
        def _():
            own[...] = value

    def rs_copy(d):
        to = lax.rem(s + d, SP)
        src = st.at[pl.ds(to * rows, rows)]
        return remote(src, rb.at[d - 1], rs_s.at[d - 1], rs_r.at[d - 1], sp=to)

    loop(1, SP + 1, input_part)

    loop(1, FS, lambda d: wk_copy(d).wait())
    wk_fin[s] = add_up(wk_rb, wk[f].astype(F32)).astype(BF)
    loop(1, SP, lambda d: sp_copy(2, wk_fin)(d).start())
    for e, buf in early_bufs:
        loop(1, SP, lambda d: sp_copy(e, buf)(d).wait())
    for n in range(SP):
        upg[:, 768 * n : 768 * n + 768] = up_fin[n].astype(F32)
    vecg[...] = v_fin[0] + v_fin[1] + v_fin[2] + v_fin[3]
    down_total = dn_fin[0].astype(F32)
    out_total = ou_fin[0].astype(F32)
    for n in range(1, SP):
        down_total = down_total + dn_fin[n].astype(F32)
        out_total = out_total + ou_fin[n].astype(F32)
    dng[...] = down_total
    outg[...] = out_total

    loop(1, SP, lambda d: rs_copy(d).wait())
    total = gfs[...] + own[...]
    for d in range(SP - 1):
        total = total + rb[d].astype(F32)
    input_grad[...] = total

    loop(1, FS, lambda d: wq_copy(d).wait())
    wq_fin[s] = add_up(wq_rb, wp[f].astype(F32)).astype(BF)
    loop(1, SP, lambda d: sp_copy(3, wq_fin)(d).start())
    loop(1, SP, lambda d: sp_copy(2, wk_fin)(d).wait())
    wkg[...] = wk_fin[...].astype(F32)
    loop(1, SP, lambda d: sp_copy(3, wq_fin)(d).wait())
    wqg[...] = wq_fin[...].astype(F32)


def on_device(
    hidden_in,
    qkv_weight,
    query_bias,
    value_bias,
    output_weight,
    output_bias,
    first_gain,
    first_shift,
    up_weight,
    up_bias,
    down_weight,
    down_bias,
    second_gain,
    second_shift,
    valid_length,
    out_cotangent,
):
    s = lax.axis_index("sp")
    rows, width = hidden_in.shape
    tall = SP * rows
    slim = qkv_weight.shape[0]
    deep = down_weight.shape[0]
    share = up_weight.shape[1] // SP
    cols = LH * HEAD_DIM * 3
    vmem = pl.BlockSpec(memory_space=pltpu.VMEM)
    hbm = pl.BlockSpec(memory_space=pl.ANY)
    dma = pltpu.SemaphoreType.DMA
    shape = jax.ShapeDtypeStruct

    parts = qkv_weight.reshape(slim, 3, SP, LH, HEAD_DIM)
    parts = lax.dynamic_index_in_dim(parts, s, 2, keepdims=False)
    kv_cols = jnp.stack((parts[:, 1], parts[:, 2]), axis=2).reshape(slim, -1)
    wq = jnp.concatenate((kv_cols, parts[:, 0].reshape(slim, -1)), axis=1)
    up = lax.dynamic_slice_in_dim(up_weight, s * share, share, 1)
    riders = jnp.stack(
        (
            query_bias, value_bias, output_bias, first_gain, first_shift, down_bias,
            second_gain, second_shift,
        )
    )
    riders = jnp.pad(riders, ((0, slim - 8), (0, 64 - slim)))
    riders = lax.dynamic_update_slice(riders, up_bias.reshape(4, slim), (8, 0))
    wq = jnp.concatenate((wq, riders), axis=1)
    smem = pl.BlockSpec(memory_space=pltpu.SMEM)
    hid_all, wqkv, q_all, kv_all, o_all, out_g, vecs = pl.pallas_call(
        forward_kernel,
        out_shape=(
            shape((tall, width), BF),
            shape((width, cols), BF),
            shape((YG, LH, tall, 128), BF),
            shape((XG, LH, tall, 128), BF),
            shape((YG, LH, tall, 128), BF),
            shape((8, slim, width), BF),
            shape((16, width), F32),
        ),
        in_specs=[smem] + [vmem] * 3,
        out_specs=(vmem, vmem, vmem, vmem, vmem, hbm, vmem),
        scratch_shapes=[
            pltpu.VMEM((FS, slim, cols + 64), BF),
            pltpu.VMEM((width, cols), F32),
            pltpu.VMEM((LH, tall, 128), BF),
            pltpu.VMEM((LH, tall, 128), BF),
            pltpu.VMEM((8, width), F32),
            pltpu.VMEM((YG, LH, tall, 128), F32),
            pltpu.VMEM((YG, LH, tall, 128), BF),
        ]
        + [dma((n,)) for n in (3, 3, 31, 31, 8, 8, 3, 3, 7, 7)]
        + [dma((3, 3)), dma((3, 3)), dma((1,))],
        compiler_params=pltpu.CompilerParams(
            collective_id=0, has_side_effects=True, vmem_limit_bytes=VMEM_LIMIT
        ),
        name="forward",
    )(valid_length, hidden_in, wq, output_weight)

    result, gfs, d_all, ld_all, up_own, up_rb, dn_rb, dwo, vp = pl.pallas_call(
        middle_kernel,
        out_shape=(
            shape((rows, width), BF),
            shape((rows, width), F32),
            shape((YG, LH, tall, 128), BF),
            shape((YG, 8, tall), F32),
            shape((2, YG, slim, share), BF),
            shape((YG - 1, 2, YG, slim, share), BF),
            shape((8, deep, width), BF),
            shape((LH * HEAD_DIM, width), BF),
            shape((FS, 16, 128), F32),
        ),
        in_specs=[vmem] * 7,
        out_specs=(vmem, vmem, hbm, hbm, vmem, vmem, vmem, vmem, vmem),
        scratch_shapes=[
            pltpu.VMEM((FS, slim, share), BF),
            pltpu.VMEM((width, share), F32),
            pltpu.VMEM((LH * 128, width), BF),
            pltpu.VMEM((width, share), BF),
            pltpu.VMEM((share, width), BF),
            pltpu.VMEM((FS, slim, share), BF),
            pltpu.VMEM((share, width), BF),
            pltpu.VMEM((tall, LH * 128), BF),
            pltpu.VMEM((tall, 128), F32),
            pltpu.VMEM((3, tall, width), BF),
            pltpu.VMEM((rows, width), F32),
            pltpu.VMEM((rows, width), F32),
            pltpu.VMEM((rows, width), F32),
            pltpu.VMEM((rows, 128), F32),
            pltpu.VMEM((tall, width), BF),
            pltpu.VMEM((tall, share), BF),
            pltpu.VMEM((tall, share), F32),
            pltpu.VMEM((tall, width), BF),
            pltpu.VMEM((tall, share), BF),
            pltpu.VMEM((tall, width), BF),
            pltpu.VMEM((rows, width), F32),
            pltpu.VMEM((3, SP - 1, rows, width), BF),
            pltpu.VMEM((LH, tall, 128), BF),
            pltpu.VMEM((8, tall), F32),
            pltpu.VMEM((8, width), F32),
        ]
        + [dma((3, 3)) for _ in range(4)]
        + [dma((3, 4)), dma((3, 4)), dma((3,)), dma((3,)), dma((2,))]
        + [dma((7,)), dma((7,)), dma((3, 2)), dma((3, 2)), dma((8,)), dma((8,))]
        + [dma((3, 2)), dma((3, 2)), dma((8,)), dma((8,))],
        compiler_params=pltpu.CompilerParams(
            collective_id=1, has_side_effects=True, vmem_limit_bytes=VMEM_LIMIT
        ),
        name="middle",
    )(
        o_all, out_g, up, down_weight, vecs,
        hidden_in, out_cotangent,
    )

    input_grad, wkg, wqg, upg, dng, outg, vecg = pl.pallas_call(
        backward_kernel,
        out_shape=(
            shape((rows, width), F32),
            shape((SP, slim, 2 * LH * HEAD_DIM), F32),
            shape((SP, slim, 256), F32),
            shape((slim, SP * share), F32),
            shape((deep, width), F32),
            shape((slim, width), F32),
            shape((16, 128), F32),
        ),
        in_specs=[smem] + [vmem] * 12,
        out_specs=(vmem,) * 7,
        scratch_shapes=[
            pltpu.VMEM((YG, LH, HEAD_DIM, tall), F32),
            pltpu.VMEM((YG, LH * HEAD_DIM, tall), BF),
            pltpu.VMEM((XG, LH, tall, 128), BF),
            pltpu.VMEM((XG - 1, LH, tall, 128), BF),
            pltpu.VMEM((YG - 1, LH * HEAD_DIM, tall), BF),
            pltpu.VMEM((tall, cols), BF),
            pltpu.VMEM((width, 640), F32),
            pltpu.VMEM((FS, slim, 384), BF),
            pltpu.VMEM((FS, slim, 256), BF),
            pltpu.VMEM((tall, width), BF),
            pltpu.VMEM((rows, width), F32),
            pltpu.VMEM((SP - 1, rows, width), BF),
            pltpu.VMEM((FS - 1, slim, 384), BF),
            pltpu.VMEM((FS - 1, slim, 256), BF),
            pltpu.VMEM((8, slim, share), BF),
            pltpu.VMEM((XG - 1, slim, share), BF),
            pltpu.VMEM((8, slim, width), BF),
            pltpu.VMEM((FS - 1, 16, 128), F32),
            pltpu.VMEM((SP, slim, share), BF),
            pltpu.VMEM((SP, deep, width), BF),
            pltpu.VMEM((SP, slim, width), BF),
            pltpu.VMEM((SP, 16, 128), F32),
            pltpu.VMEM((SP, slim, 384), BF),
            pltpu.VMEM((SP, slim, 256), BF),
        ]
        + [dma((n,)) for n in (7, 7, 3, 3, 31, 31, 31, 31, 7, 7, 8, 8, 31, 31, 3, 3)]
        + [dma((6, 3)), dma((6, 3))],
        compiler_params=pltpu.CompilerParams(
            collective_id=2, has_side_effects=True, vmem_limit_bytes=VMEM_LIMIT
        ),
        name="backward",
    )(
        valid_length, q_all, d_all, ld_all, kv_all, hid_all, wqkv, gfs,
        up_own, up_rb, dn_rb, dwo.reshape(8, slim, width), vp,
    )

    kv_grad = wkg.reshape(SP, slim, LH, 2, HEAD_DIM)
    q_grad = wqg[:, :, : LH * HEAD_DIM].reshape(SP, slim, LH, 1, HEAD_DIM)
    qkv_grad = jnp.concatenate((q_grad, kv_grad), axis=3)
    qkv_grad = jnp.transpose(qkv_grad, (1, 3, 0, 2, 4)).reshape(slim, -1)
    qv_grad = jnp.sum(wqg[:, 0:2, LH * HEAD_DIM : LH * HEAD_DIM + slim], axis=0)
    return (
        result,
        input_grad,
        qkv_grad,
        qv_grad[0],
        qv_grad[1],
        outg,
        vecg[0, :slim],
        vecg[1, :slim],
        vecg[2, :slim],
        upg,
        vecg[8, :deep],
        dng,
        vecg[3, :slim],
        vecg[4, :slim],
        vecg[5, :slim],
    )


def solution(mesh):
    placed = (
        P(("fsdp", "sp"), None),
        P("fsdp", None),
        P("fsdp"),
        P("fsdp"),
        P("fsdp", None),
        P("fsdp"),
        P("fsdp"),
        P("fsdp"),
        P("fsdp", None),
        P("fsdp"),
        P("fsdp", None),
        P("fsdp"),
        P("fsdp"),
        P("fsdp"),
        P(),
        P(("fsdp", "sp"), None),
    )
    return jax.shard_map(
        on_device,
        mesh=mesh,
        in_specs=placed,
        out_specs=(
            P(("fsdp", "sp"), None),
            P(("fsdp", "sp"), None),
            P("fsdp", None),
            P("fsdp"),
            P("fsdp"),
            P("fsdp", None),
            P("fsdp"),
            P("fsdp"),
            P("fsdp"),
            P("fsdp", None),
            P("fsdp"),
            P("fsdp", None),
            P("fsdp"),
            P("fsdp"),
            P("fsdp"),
        ),
        check_vma=False,
    )
```

```python
import functools

import jax
import jax.numpy as jnp
from jax import lax
from jax.experimental import pallas as pl
from jax.experimental.pallas import tpu as pltpu
from jax.sharding import PartitionSpec as P

HEADS = 12
HEAD_DIM = 64
SP = 4
FS = 32
YG = 4
XG = 8
LH = HEADS // SP

KEY_STEPS = ((0, 1), (0, 3), (1, 0), (0, 2), (1, 1), (1, 3), (1, 2))
PASSES = ((0, 1, 2), (3, 4, 5, 6))
UP_STEP = 1

BF = jnp.bfloat16
F32 = jnp.float32
MESH = pl.DeviceIdType.MESH
epsilon = 1e-05
masked = -1e30
VMEM_LIMIT = 56 * 1024 * 1024


def dot_nn(a, b):
    return lax.dot_general(a, b, (((1,), (0,)), ((), ())), preferred_element_type=F32)


def dot_nt(a, b):
    return lax.dot_general(a, b, (((1,), (1,)), ((), ())), preferred_element_type=F32)


def dot_tn(a, b):
    return lax.dot_general(a, b, (((0,), (0,)), ((), ())), preferred_element_type=F32)


def norm_forward(incoming, norm_gain, norm_shift):
    row_mean = jnp.mean(incoming, axis=-1, keepdims=True)
    centered = incoming - row_mean
    inverse = lax.rsqrt(jnp.mean(centered * centered, axis=-1, keepdims=True) + epsilon)
    normed = centered * inverse
    return (normed * norm_gain + norm_shift, normed, inverse)


def norm_backward(incoming, normed, inverse, norm_gain):
    scaled = incoming * norm_gain
    adjusted = (
        scaled
        - jnp.mean(scaled, axis=-1, keepdims=True)
        - normed * jnp.mean(scaled * normed, axis=-1, keepdims=True)
    )
    return (
        adjusted * inverse,
        jnp.sum(incoming * normed, axis=0, keepdims=True),
        jnp.sum(incoming, axis=0, keepdims=True),
    )


def loop(low, high, body):
    def step(d, carried):
        body(d)
        return carried

    lax.fori_loop(low, high, step, 0)


def remote(src, dst, send, recv, **device):
    return pltpu.make_async_remote_copy(
        src_ref=src,
        dst_ref=dst,
        send_sem=send,
        recv_sem=recv,
        device_id=device,
        device_id_type=MESH,
    )


def greet(barrier, **device):
    pl.semaphore_signal(barrier, inc=1, device_id=device, device_id_type=MESH)


def greet_all(f, s):
    barrier = pltpu.get_barrier_semaphore()
    loop(1, FS, lambda d: greet(barrier, fsdp=lax.rem(f + d, FS)))
    loop(1, SP, lambda d: greet(barrier, sp=lax.rem(s + d, SP)))

    @pl.when(s != f // 8)
    def _():
        loop(0, 8, lambda t: greet(barrier, fsdp=8 * s + t, sp=f // 8))

    pl.semaphore_wait(barrier, FS - 1 + SP - 1 + jnp.where(s != f // 8, 8, 0))


def forward_kernel(
    valid, hid, wq, out, up, down,
    hid_all, wqkv, q_all, kv_all, o_all, out_g, up_g, wdn, vecs,
    wq_g, wf, q_st, kv_st, qvb, state, o_st,
    hid_s, hid_r, wq_s, wq_r, ou_s, ou_r,
    q_s, q_r, kv_s, kv_r, o_s, o_r, loc,
    ua_s, ua_r, ub_s, ub_r, dn_s, dn_r,
):
    s = lax.axis_index("sp")
    f = lax.axis_index("fsdp")
    i, j = f // YG, lax.rem(f, YG)
    greet_all(f, s)
    rows = hid.shape[0]

    def hid_copy(d):
        dst = hid_all.at[pl.ds(s * rows, rows)]
        return remote(hid, dst, hid_s.at[d - 1], hid_r.at[d - 1], sp=lax.rem(s + d, SP))

    def fs_copy(src, buf, send, recv):
        return lambda d: remote(
            src, buf.at[f], send.at[d - 1], recv.at[d - 1], fsdp=lax.rem(f + d, FS)
        )

    wq_copy = fs_copy(wq, wq_g, wq_s, wq_r)

    def out_copy(t):
        k = lax.rem(f, 8)
        return remote(out, out_g.at[k], ou_s.at[t], ou_r.at[k], fsdp=8 * s + t, sp=f // 8)

    def out_arrival(k):
        return remote(out, out_g.at[k], ou_s.at[k], ou_r.at[k], fsdp=8 * s + k, sp=f // 8)

    z, x = f // 16, lax.rem(i, YG)

    def zy_copy(n):
        to = (lax.rem(z + (n + 1) // YG, 2) * YG + x) * YG + lax.rem(j + n + 1, YG)
        return remote(up, up_g.at[f], ua_s.at[n], ua_r.at[n], fsdp=to)

    def x_copy(d):
        to = (z * YG + lax.rem(x + d, YG)) * YG + j
        copies = []
        for n in range(2):
            at = up_g.at[pl.ds((n * YG + x) * YG, YG)]
            copies.append(remote(at, at, ub_s.at[d - 1, n], ub_r.at[d - 1, n], fsdp=to))
        return copies

    def down_copy(t):
        k = lax.rem(f, 8)
        dst = wdn.at[pl.ds(k * 96, 96)]
        return remote(down, dst, dn_s.at[t], dn_r.at[k], fsdp=8 * s + t, sp=f // 8)

    def down_arrival(k):
        dst = wdn.at[pl.ds(k * 96, 96)]
        return remote(down, dst, dn_s.at[k], dn_r.at[k], fsdp=8 * s + k, sp=f // 8)

    def is_self(t):
        return (s == f // 8) & (8 * s + t == f)

    def unless_self(work):
        def step(t):
            @pl.when(jnp.logical_not(is_self(t)))
            def _():
                work(t)

        loop(0, 8, step)

    loop(1, SP, lambda d: hid_copy(d).start())

    loop(1, FS, lambda d: wq_copy(d).start())
    hid_all[pl.ds(pl.multiple_of(s * rows, rows), rows), :] = hid[...]
    wq_g[f] = wq[...]
    loop(1, SP, lambda d: hid_copy(d).wait())

    loop(1, FS, lambda d: wq_copy(d).wait())

    width = vecs.shape[1]
    pad = jnp.zeros((8, width - 64), F32)

    def riders(n, low):
        block = wq_g[n, low : low + 8, 512:640].astype(F32)
        wide = jnp.concatenate((block[:, 64:128], pad), axis=1)
        return wide

    def shifted(wide, amount):
        return wide if amount == 0 else pltpu.roll(wide, amount, 1)

    qv = jnp.zeros((8, width), F32)
    for n in range(8):
        qv = qv + shifted(riders(8 * s + n, 0), 24 * n)
    qvb[...] = qv
    lane = lax.broadcasted_iota(jnp.int32, (1, width), 1)
    qrow = qvb[0:1, :]
    vrow = qvb[1:2, :]
    bias = jnp.zeros((1, width), F32)
    wide_q = jnp.broadcast_to(qrow, (8, width))
    wide_v = jnp.broadcast_to(vrow, (8, width))
    bias = jnp.where((lane >= 384) & (lane < 576), pltpu.roll(wide_q, 384, 1)[0:1], 0.0)
    for h in range(LH):
        here = (lane >= 128 * h + 64) & (lane < 128 * h + 128)
        bias = bias + jnp.where(here, pltpu.roll(wide_v, 64 * h + 64, 1)[0:1], 0.0)

    def assemble(n):
        wf[pl.ds(pl.multiple_of(24 * n, 8), 24), :] = wq_g[n, :, 0:576].astype(F32)

    loop(0, FS, assemble)
    wqkv[...] = wf[...].astype(BF)

    low_lane = lax.broadcasted_iota(jnp.int32, (rows, 128), 1) < HEAD_DIM

    def project(b):
        at = pl.ds(pl.multiple_of(b * rows, rows), rows)
        p = dot_nn(hid_all[at, :], wqkv[...]) + bias[:, :576]
        for h in range(LH):
            kv_st[h, at, :] = p[:, 128 * h : 128 * h + 128].astype(BF)
        q01 = p[:, 384:512] * 0.125
        q2 = jnp.concatenate((p[:, 512:576], jnp.zeros((rows, 64), F32)), axis=1) * 0.125
        q_st[0, at, :] = jnp.where(low_lane, q01, 0.0).astype(BF)
        q_st[1, at, :] = jnp.where(low_lane, pltpu.roll(q01, 64, 1), 0.0).astype(BF)
        q_st[2, at, :] = q2.astype(BF)

    loop(0, SP, project)

    def kv_copy(n):
        dz, dx = KEY_STEPS[n]
        to = lax.rem(i // YG + dz, 2) * YG + lax.rem(i + dx, YG)
        return remote(kv_st, kv_all.at[i], kv_s.at[n], kv_r.at[n], fsdp=to * YG + j)

    def kv_from(n):
        dz, dx = KEY_STEPS[n]
        return lax.rem(i // YG + dz, 2) * YG + lax.rem(i + YG - dx, YG)

    def q_copy(d):
        to = i * YG + lax.rem(j + d, YG)
        return remote(q_st, q_all.at[j], q_s.at[d - 1], q_r.at[d - 1], fsdp=to)

    loop(1, YG, lambda d: q_copy(d).start())
    for n in range(XG - 1):
        kv_copy(n).start()
    kv_all[i] = kv_st[...]
    q_all[j] = q_st[...]

    total = jnp.zeros((8, width), F32)
    for n in range(FS):
        total = total + shifted(riders(n, 0), 24 * n)
    vecs[0:8, :] = total
    ub = jnp.zeros((8, width), F32)
    for n in range(8):
        rider = riders(8 * s + n, 8)
        for c in range(4):
            row = jnp.broadcast_to(rider[c : c + 1], (8, width))
            ub = ub + shifted(row, 96 * n + 24 * c)
    vecs[8:16, :] = ub

    def send_out(t):
        @pl.when(jnp.logical_not(is_self(t)))
        def _():
            out_copy(t).start()

    loop(0, 8, send_out)

    @pl.when(s == f // 8)
    def _():
        out_own = pltpu.make_async_copy(out, out_g.at[lax.rem(f, 8)], loc.at[0])
        out_own.start()
        out_own.wait()

    for n in range(XG - 1):
        zy_copy(n).start()
    unless_self(lambda t: down_copy(t).start())
    up_g[f] = up[...]

    @pl.when(s == f // 8)
    def _():
        wdn[pl.ds(pl.multiple_of(lax.rem(f, 8) * 96, 32), 96), :] = down[...]

    tall = SP * rows
    key_place = lax.broadcasted_iota(jnp.int32, (1, tall), 1)
    half = tall // 2
    lanes = lax.broadcasted_iota(jnp.int32, (half, 128), 1)

    def o_copy(d, h):
        to = lax.rem(j + YG - d, YG)
        src = o_st.at[to, h]
        return remote(src, o_all.at[j, h], o_s.at[d - 1, h], o_r.at[d - 1, h], fsdp=i * YG + to)

    def attend(places, is_first, is_last):
        limits = [
            jnp.where((at * YG + j) * tall + key_place < valid[0], 0.0, masked) for at in places
        ]

        def tile(t):
            d = t // LH
            h = lax.rem(t, LH)
            n = lax.rem(j + YG - d, YG)
            if is_first:

                @pl.when((d > 0) & (h == 0))
                def _():
                    q_copy(d).wait_recv()

            for r in range(2):
                part_at = pl.ds(r * half, half)
                query = q_all[n, h, part_at, :]
                blocks = [kv_all[at, h] for at in places]
                scores = [dot_nt(query, block) + limit for block, limit in zip(blocks, limits)]
                tops = [jnp.max(score, axis=1, keepdims=True) for score in scores]
                top = functools.reduce(jnp.maximum, tops)
                if not is_first:
                    old = state[n, h, part_at, :]
                    before = old[:, 0:1]
                    top = jnp.maximum(top, before)
                probs = [jnp.exp(score - top) for score in scores]
                total = functools.reduce(
                    jnp.add, [jnp.sum(p, axis=1, keepdims=True) for p in probs]
                )
                weighted = functools.reduce(
                    jnp.add, [dot_nn(p.astype(BF), block) for p, block in zip(probs, blocks)]
                )
                if not is_first:
                    decay = jnp.exp(before - top)
                    total = total + decay * old[:, 32:33]
                    weighted = weighted + decay * old
                if is_last:
                    log_sum = top + jnp.log(total)
                    high = log_sum.astype(BF).astype(F32)
                    logs = jnp.where(lanes < 32, high, log_sum - high)
                    merged = jnp.where(lanes >= 64, weighted / total, logs)
                    o_st[n, h, part_at, :] = merged.astype(BF)
                else:
                    logs = jnp.where(lanes < 32, top, total)
                    state[n, h, part_at, :] = jnp.where(lanes >= 64, weighted, logs)
            if is_last:

                @pl.when(d > 0)
                def _():
                    o_copy(d, h).start()

                @pl.when(d == 0)
                def _():
                    o_all[j, h] = o_st[j, h]

        if is_last:
            loop(LH, LH * YG, tile)
            loop(0, LH, tile)
        else:
            loop(0, LH * YG, tile)

    attend([i], True, False)
    for step, members in enumerate(PASSES):
        for n in members:
            kv_copy(n).wait_recv()
        if step == UP_STEP:
            for n in range(XG - 1):
                zy_copy(n).wait()
            for d in range(1, YG):
                for copy in x_copy(d):
                    copy.start()
        places = [kv_from(n) for n in members]
        attend(places, False, step == len(PASSES) - 1)

    for d in range(1, YG):
        for copy in x_copy(d):
            copy.wait()
    unless_self(lambda t: (down_copy(t).wait_send(), down_arrival(t).wait_recv()))
    for n in range(XG - 1):
        kv_copy(n).wait_send()
    loop(1, YG, lambda d: q_copy(d).wait_send())

    def owned_wait(t):
        @pl.when(jnp.logical_not(is_self(t)))
        def _():
            out_copy(t).wait_send()
            out_arrival(t).wait_recv()

    loop(0, 8, owned_wait)
    loop(1, YG, lambda d: loop(0, LH, lambda h: o_copy(d, h).wait()))


def middle_kernel(
    o_all, out_g, up_g, wdn, vecs, hid, cot,
    result, gfs, d_all, ld_all, dup, ddn, dwo, vp,
    wf, wo, wup,
    att, ld, st, own, first, n1, inv1, x_all, act, deriv, gd, gp, gb, gsec, rb, dbuf, ldrow, vg,
    ag_s, ag_r, rs_s, rs_r, d_s, d_r, l_s, l_r, loc,
):
    s = lax.axis_index("sp")
    f = lax.axis_index("fsdp")
    i, j = f // YG, lax.rem(f, YG)
    rows = hid.shape[0]
    tall = SP * rows
    barrier = pltpu.get_barrier_semaphore()
    loop(1, YG, lambda d: greet(barrier, fsdp=i * YG + lax.rem(j + d, YG)))
    loop(1, SP, lambda d: greet(barrier, sp=lax.rem(s + d, SP)))
    pl.semaphore_wait(barrier, YG - 1 + SP - 1)

    wf[0:192, :] = out_g[...].astype(F32).reshape(192, wf.shape[1])
    for h in range(LH):
        wo[128 * h : 128 * h + 64, :] = jnp.zeros((64, wo.shape[1]), BF)
        wo[128 * h + 64 : 128 * h + 128, :] = wf[64 * h : 64 * h + 64, :].astype(BF)

    def y_peer(d):
        return i * YG + lax.rem(j + d, YG)

    def span(b):
        return pl.ds(pl.multiple_of(b * rows, rows), rows)

    lane = lax.broadcasted_iota(jnp.int32, (rows, 128), 1)

    def merge(b):
        at = span(b)
        sums = jnp.zeros((rows, 128), F32)
        for h in range(LH):
            parts = [o_all[d, h, at, :].astype(F32) for d in range(YG)]
            logs = [p[:, 0:1] + p[:, 32:33] for p in parts]
            top = functools.reduce(jnp.maximum, logs)
            weights = [jnp.exp(g - top) for g in logs]
            total = functools.reduce(jnp.add, weights)
            merged = functools.reduce(jnp.add, [p * w for p, w in zip(parts, weights)]) / total
            att[at, 128 * h : 128 * h + 128] = jnp.where(lane >= 64, merged, 0.0).astype(BF)
            sums = jnp.where(lane == 2 * h, top + jnp.log(total), sums)
        ld[at, :] = sums

    loop(0, SP, merge)

    def gather(e, buf):
        def copy(d):
            at = buf.at[pl.ds(s * rows, rows)]
            return remote(at, at, ag_s.at[e, d - 1], ag_r.at[e, d - 1], sp=lax.rem(s + d, SP))

        return copy

    def scatter(e):
        def copy(d):
            src = st.at[e, pl.ds(lax.rem(s + d, SP) * rows, rows)]
            sems = (rs_s.at[e, d - 1], rs_r.at[e, d - 1])
            return remote(src, rb.at[e, d - 1], *sems, sp=lax.rem(s + d, SP))

        return copy

    def collect(e):
        loop(1, SP, lambda d: scatter(e)(d).wait())
        total = own[...]
        for d in range(SP - 1):
            total = total + rb[e, d].astype(F32)
        return total

    def out_part(d):
        b = lax.rem(s + d, SP)
        value = dot_nn(att[span(b), :], wo[...])

        @pl.when(d < SP)
        def _():
            st[0, span(b), :] = value.astype(BF)
            scatter(0)(d).start()

        @pl.when(d == SP)
        def _():
            own[...] = value

    loop(1, SP + 1, out_part)
    summed = hid[...].astype(F32) + collect(0) + vecs[2:3, :]
    value, normed, inverse = norm_forward(summed, vecs[3:4, :], vecs[4:5, :])
    first[...] = value
    n1[...] = normed
    inv1[...] = jnp.broadcast_to(inverse, inv1.shape)
    x_all[span(s), :] = value.astype(BF)
    loop(1, SP, lambda d: gather(0, x_all)(d).start())

    def assemble(n):
        wf[pl.ds(pl.multiple_of(24 * n, 8), 24), :] = up_g[n].astype(F32)

    loop(0, FS, assemble)
    wup[...] = wf[...].astype(BF)

    def pipeline(e, buf, work):
        def step(d):
            b = lax.rem(s + SP - d, SP)

            @pl.when(d > 0)
            def _():
                gather(e, buf)(d).wait_recv()

            value = work(b)

            @pl.when(d > 0)
            def _():
                st[e + 1, span(b), :] = value.astype(BF)
                scatter(e + 1)(SP - d).start()

            @pl.when(d == 0)
            def _():
                own[...] = value

        loop(0, SP, step)
        loop(1, SP, lambda d: gather(e, buf)(d).wait_send())

    def feed(b):
        at = span(b)
        pre = dot_nn(x_all[at, :], wup[...]) + vecs[8:9, :]
        cdf = 0.5 * (1.0 + lax.erf(pre * 0.7071067811865476))
        density = jnp.exp(-0.5 * pre * pre) * 0.3989422804014327
        active = (pre * cdf).astype(BF)
        act[at, :] = active
        deriv[at, :] = cdf + pre * density
        return dot_nn(active, wdn[...])

    pipeline(0, x_all, feed)
    summed = first[...] + collect(1) + vecs[5:6, :]
    value, normed, inverse = norm_forward(summed, vecs[6:7, :], vecs[7:8, :])
    result[...] = value.astype(BF)
    grad, ggain, gshift = norm_backward(cot[...].astype(F32), normed, inverse, vecs[6:7, :])
    gsec[...] = grad
    low = grad.astype(BF)
    gd[span(s), :] = low
    loop(1, SP, lambda d: gather(1, gd)(d).start())
    vg[...] = jnp.zeros(vg.shape, F32)
    vg[3:4, :] = jnp.sum(low.astype(F32), axis=0, keepdims=True)
    vg[4:5, :] = ggain
    vg[5:6, :] = gshift

    def back(b):
        at = span(b)
        grad_pre = (dot_nt(gd[at, :], wdn[...]) * deriv[at, :]).astype(BF)
        gp[at, :] = grad_pre
        return dot_nt(grad_pre, wup[...])

    pipeline(1, gd, back)

    def weight_terms(c):
        at = pl.ds(pl.multiple_of(128 * c, 128), 128)
        wf[at, :] = dot_tn(x_all[:, at], gp[...])
        ddn[at, :] = dot_tn(act[:, at], gd[...]).astype(BF)

    loop(0, act.shape[1] // 128, weight_terms)

    def cut(n):
        dup[n] = wf[pl.ds(pl.multiple_of(24 * n, 8), 24), :].astype(BF)

    loop(0, FS, cut)

    ub = jnp.sum(gp[...].astype(F32), axis=0, keepdims=True)
    grad_first = gsec[...] + collect(2)
    grad, ggain, gshift = norm_backward(grad_first, n1[...], inv1[:, 0:1], vecs[3:4, :])
    gfs[...] = grad
    low = grad.astype(BF)
    gb[span(s), :] = low
    loop(1, SP, lambda d: gather(2, gb)(d).start())
    vg[0:1, :] = jnp.sum(low.astype(F32), axis=0, keepdims=True)
    vg[1:2, :] = ggain
    vg[2:3, :] = gshift

    def branch(d):
        b = lax.rem(s + SP - d, SP)
        at = span(b)

        @pl.when(d > 0)
        def _():
            gather(2, gb)(d).wait_recv()

        value = dot_nt(gb[at, :], wo[...]).astype(BF)
        sums = ld[at, :]
        for h in range(LH):
            part = value[:, 128 * h : 128 * h + 128]
            dbuf[h, at, :] = part
            product = part.astype(F32) * att[at, 128 * h : 128 * h + 128].astype(F32)
            sums = jnp.where(lane == 2 * h + 1, jnp.sum(product, axis=1, keepdims=True), sums)
        ld[at, :] = sums
        loop(1, YG, lambda n: d_copy(n, d).start())

    def d_copy(n, d):
        at = span(lax.rem(s + SP - d, SP))
        sems = (d_s.at[n - 1, d], d_r.at[n - 1, d])
        return remote(dbuf.at[:, at], d_all.at[j, :, at], *sems, fsdp=y_peer(n))

    loop(0, SP, branch)
    loop(1, SP, lambda d: gather(2, gb)(d).wait_send())
    ldrow[...] = jnp.transpose(ld[...], (1, 0))[0:8, :]

    def l_copy(d):
        return remote(ldrow, ld_all.at[j], l_s.at[d - 1], l_r.at[d - 1], fsdp=y_peer(d))

    loop(1, YG, lambda d: l_copy(d).start())
    d_own = pltpu.make_async_copy(dbuf, d_all.at[j], loc.at[0])
    l_own = pltpu.make_async_copy(ldrow, ld_all.at[j], loc.at[1])
    d_own.start()
    l_own.start()
    for h in range(LH):
        value = dot_tn(att[:, 128 * h : 128 * h + 128], gb[...])
        dwo[64 * h : 64 * h + 64, :] = value[64:128].astype(BF)
    lane8 = lax.broadcasted_iota(jnp.int32, (8, 128), 1)
    wide = vg[...]
    width = wide.shape[1]
    ub_wide = jnp.broadcast_to(ub, (8, width))
    for n in range(FS):
        piece = wide if n == 0 else pltpu.roll(wide, width - 24 * n, 1)
        vp[n, 0:8, :] = jnp.where(lane8 < 24, piece[:, 0:128], 0.0)
        vp[n, 8:16, :] = jnp.zeros((8, 128), F32)
    for k in range(8):
        piece = ub_wide if k == 0 else pltpu.roll(ub_wide, width - 96 * k, 1)
        vp[8 * s + k, 8:16, :] = jnp.where(lane8 < 96, piece[:, 0:128], 0.0)
    d_own.wait()
    l_own.wait()
    loop(1, YG, lambda n: loop(0, SP, lambda d: d_copy(n, d).wait()))
    loop(1, YG, lambda d: l_copy(d).wait())


def backward_kernel(
    valid, q_all, d_all, ld, kv_all, hid_all, wqkv, gfs, dup, ddn, dwo, vp,
    input_grad, wkg, wqg, upg, dng, outg, vecg,
    acc, dq, dkv, kv_rb, q_rb, g, wf, wk, wp, st, own, rb, wk_rb, wq_rb, up_rb, dn_rb, up_st, up_rc, ou_rb, vp_rb,
    up_fin, dn_fin, ou_fin, v_fin, wk_fin, wq_fin,
    kv_s, kv_r, q_s, q_r, wk_s, wk_r, wq_s, wq_r, up_s, up_r, ou_s, ou_r, vp_s, vp_r,
    rs_s, rs_r, fin_s, fin_r, us_s, us_r, ds_s, ds_r,
):
    s = lax.axis_index("sp")
    f = lax.axis_index("fsdp")
    i, j = f // YG, lax.rem(f, YG)
    rows = gfs.shape[0]
    tall = SP * rows
    greet_all(f, s)

    def kv_copy(d):
        to = lax.rem(i + d, XG)
        return remote(dkv.at[d - 1], kv_rb.at[d - 1], kv_s.at[d - 1], kv_r.at[d - 1], fsdp=to * YG + j)

    def q_copy(d):
        to = lax.rem(j + d, YG)
        return remote(dq.at[to], q_rb.at[d - 1], q_s.at[d - 1], q_r.at[d - 1], fsdp=i * YG + to)

    def fs_copy(src, buf, send, recv):
        def copy(d):
            to = lax.rem(f + d, FS)
            return remote(src.at[to], buf.at[d - 1], send.at[d - 1], recv.at[d - 1], fsdp=to)

        return copy

    vp_copy = fs_copy(vp, vp_rb, vp_s, vp_r)
    wq_copy = fs_copy(wp, wq_rb, wq_s, wq_r)
    wk_copy = fs_copy(wk, wk_rb, wk_s, wk_r)
    z, x = f // 16, lax.rem(i, YG)

    def up_copy(n):
        zn, yn = lax.rem(z + (n + 1) // YG, 2), lax.rem(j + n + 1, YG)
        to = (zn * YG + x) * YG + yn
        return remote(up_st.at[zn * YG + yn], up_rc.at[n], up_s.at[n], up_r.at[n], fsdp=to)

    def out_copy(k):
        n = lax.rem(f, 8)
        return remote(dwo.at[k], ou_rb.at[n], ou_s.at[k], ou_r.at[n], fsdp=8 * s + k, sp=f // 8)

    def out_arrival(n):
        return remote(dwo.at[n], ou_rb.at[n], ou_s.at[n], ou_r.at[n], fsdp=8 * s + n, sp=f // 8)

    def is_self(t):
        return (s == f // 8) & (8 * s + t == f)

    def unless_self(work):
        def step(t):
            @pl.when(jnp.logical_not(is_self(t)))
            def _():
                work(t)

        loop(0, 8, step)

    def up_sum(d):
        to = lax.rem(x + d, YG)
        copies = []
        for n in range(2):
            src = dup.at[pl.ds((n * YG + to) * YG, YG)]
            sems = (us_s.at[d - 1, n], us_r.at[d - 1, n])
            copies.append(remote(src, up_rb.at[d - 1, n], *sems, fsdp=(z * YG + to) * YG + j))
        return copies

    def down_sum(t):
        k = lax.rem(f, 8)
        src = ddn.at[pl.ds(t * 96, 96)]
        return remote(src, dn_rb.at[k], ds_s.at[t], ds_r.at[k], fsdp=8 * s + t, sp=f // 8)

    def down_sum_arrival(k):
        src = ddn.at[pl.ds(k * 96, 96)]
        return remote(src, dn_rb.at[k], ds_s.at[k], ds_r.at[k], fsdp=8 * s + k, sp=f // 8)

    for d in range(1, YG):
        for copy in up_sum(d):
            copy.start()
    unless_self(lambda t: down_sum(t).start())
    @pl.when(s == f // 8)
    def _():
        k = lax.rem(f, 8)
        dn_rb[k] = ddn[pl.ds(pl.multiple_of(k * 96, 32), 96), :]

    loop(1, FS, lambda d: vp_copy(d).start())

    def to_owner(k):
        @pl.when(jnp.logical_not(is_self(k)))
        def _():
            out_copy(k).start()

        @pl.when(is_self(k))
        def _():
            ou_rb[k] = dwo[k]

    loop(0, 8, to_owner)

    acc[...] = jnp.zeros(acc.shape, F32)

    def key_step(d):
        at = lax.rem(i + d, XG)
        first_key = (at * YG + j) * tall

        def head(h):
            def work(last):
                block = kv_all[at, h]
                flipped = jnp.transpose(block.astype(F32), (1, 0))[0:HEAD_DIM].astype(BF)
                total = None
                for n in range(YG):
                    query = q_all[n, h]
                    grad = d_all[n, h]
                    log_sum = ld[n, pl.ds(2 * h, 1), :]
                    delta = ld[n, pl.ds(2 * h + 1, 1), :]
                    scores = dot_nt(block, query)
                    if last:
                        place = first_key + lax.broadcasted_iota(jnp.int32, (tall, 1), 0)
                        scores = jnp.where(place < valid[0], scores, masked)
                    p = jnp.exp(scores - log_sum)
                    grad_p = dot_nt(block, grad)
                    grad_s = (p * (grad_p - delta)).astype(BF)
                    terms = dot_nn(grad_s, query) + dot_nn(p.astype(BF), grad)
                    total = terms if n == 0 else total + terms
                    acc[n, h] = acc[n, h] + dot_nn(flipped, grad_s)
                dkv[d - 1, h] = total.astype(BF)

            @pl.when(at < XG - 1)
            def _():
                work(False)

            @pl.when(at == XG - 1)
            def _():
                work(True)

        loop(0, LH, head)

        @pl.when(d < XG)
        def _():
            kv_copy(d).start()

    loop(1, 4, key_step)
    for d in range(1, YG):
        for copy in up_sum(d):
            copy.wait()
    for n in range(2):
        for c in range(YG):
            total = dup[(n * YG + x) * YG + c].astype(F32)
            for d in range(YG - 1):
                total = total + up_rb[d, n, c].astype(F32)
            up_st[n * YG + c] = total.astype(BF)
    for n in range(XG - 1):
        up_copy(n).start()
    loop(4, XG + 1, key_step)
    for n in range(YG):
        for h in range(LH):
            dq[n, 64 * h : 64 * h + 64, :] = acc[n, h].astype(BF)
    loop(1, YG, lambda d: q_copy(d).start())

    def span(b):
        return pl.ds(pl.multiple_of(b * rows, rows), rows)

    def sum_keys(b):
        at = span(b)
        for h in range(LH):
            total = dkv[XG - 1, h, at, :].astype(F32)
            for d in range(XG - 1):
                total = total + kv_rb[d, h, at, :].astype(F32)
            g[at, 128 * h : 128 * h + 128] = total.astype(BF)

    loop(1, XG, lambda d: kv_copy(d).wait())
    loop(0, SP, sum_keys)

    def key_terms(c):
        at = pl.ds(pl.multiple_of(128 * c, 128), 128)
        wf[at, 0:384] = dot_tn(hid_all[:, at], g[:, 0:384])

    loop(0, wf.shape[0] // 128, key_terms)

    def cut_keys(n):
        wk[n] = wf[pl.ds(pl.multiple_of(24 * n, 8), 24), 0:384].astype(BF)

    loop(0, FS, cut_keys)
    loop(1, FS, lambda d: wk_copy(d).start())

    def add_up(buf, start):
        def step(d, total):
            return total + buf[d].astype(F32)

        return lax.fori_loop(0, buf.shape[0], step, start)

    for n in range(XG - 1):
        up_copy(n).wait()
    loop(1, FS, lambda d: vp_copy(d).wait())
    up_fin[s] = add_up(up_rc, up_st[z * YG + j].astype(F32)).astype(BF)
    v_fin[s] = add_up(vp_rb, vp[f])

    def owner_wait(t):
        @pl.when(jnp.logical_not(is_self(t)))
        def _():
            out_copy(t).wait_send()
            out_arrival(t).wait_recv()

    loop(0, 8, owner_wait)
    unless_self(lambda t: (down_sum(t).wait_send(), down_sum_arrival(t).wait_recv()))

    def down_rows(c):
        at = pl.ds(pl.multiple_of(c * 32, 32), 32)
        total = dn_rb[0, at, :].astype(F32)
        for n in range(1, 8):
            total = total + dn_rb[n, at, :].astype(F32)
        dn_fin[s, at, :] = total.astype(BF)

    loop(0, dn_fin.shape[1] // 32, down_rows)

    ou_fin[s] = add_up(ou_rb, jnp.zeros(ou_fin.shape[1:], F32)).astype(BF)

    def sp_copy(e, buf):
        def copy(d):
            at = buf.at[s]
            return remote(at, at, fin_s.at[e, d - 1], fin_r.at[e, d - 1], sp=lax.rem(s + d, SP))

        return copy

    early_bufs = ((0, up_fin), (1, v_fin), (4, dn_fin), (5, ou_fin))
    for e, buf in early_bufs:
        loop(1, SP, lambda d: sp_copy(e, buf)(d).start())

    loop(1, YG, lambda d: q_copy(d).wait())
    total = dq[j].astype(F32)
    for d in range(YG - 1):
        total = total + q_rb[d].astype(F32)
    g[:, 384:576] = (jnp.transpose(total, (1, 0)) * 0.125).astype(BF)

    def query_terms(c):
        at = pl.ds(pl.multiple_of(128 * c, 128), 128)
        value = dot_tn(hid_all[:, at], g[:, 384:576])
        wf[at, 384:640] = jnp.concatenate((value, jnp.zeros((128, 64), F32)), axis=1)

    loop(0, wf.shape[0] // 128, query_terms)

    sums = jnp.sum(g[...].astype(F32), axis=0, keepdims=True)
    row = lax.broadcasted_iota(jnp.int32, (8, 256), 0)
    low = lax.broadcasted_iota(jnp.int32, (8, 128), 1) < 64
    wide = jnp.broadcast_to(jnp.concatenate((sums, jnp.zeros((1, 64), F32)), axis=1), (8, 640))
    heads = [pltpu.roll(wide[:, 128 * h : 128 * h + 128], 64, 1) for h in range(LH)]
    vrow = jnp.concatenate(
        (jnp.where(low, heads[0], wide[:, 128:256]), jnp.where(low, heads[2], 0.0)), axis=1
    )
    both = jnp.where(row == 0, wide[:, 384:640], jnp.where(row == 1, vrow, 0.0))

    def cut_queries(n):
        wp[n] = wf[pl.ds(pl.multiple_of(24 * n, 8), 24), 384:640].astype(BF)

    loop(0, FS, cut_queries)
    lane = lax.broadcasted_iota(jnp.int32, (8, 128), 1)
    for n in range(8):
        piece = both if n == 0 else pltpu.roll(both, 256 - 24 * n, 1)
        piece = pltpu.roll(piece[:, 0:128], 64, 1)
        piece = jnp.where((lane >= 64) & (lane < 88), piece, 0.0)
        rest = jnp.concatenate((piece, jnp.zeros((16, 128), F32)), axis=0)
        kept = wp[8 * s + n, :, 128:256].astype(F32)
        lanes = lax.broadcasted_iota(jnp.int32, (24, 128), 1)
        wp[8 * s + n, :, 128:256] = jnp.where(lanes < 64, kept, rest).astype(BF)
    loop(1, FS, lambda d: wq_copy(d).start())

    def input_part(d):
        b = lax.rem(s + d, SP)
        value = dot_nt(g[span(b), :], wqkv[...])

        @pl.when(d < SP)
        def _():
            st[span(b), :] = value.astype(BF)
            rs_copy(d).start()

        @pl.when(d == SP)
        def _():
            own[...] = value

    def rs_copy(d):
        to = lax.rem(s + d, SP)
        src = st.at[pl.ds(to * rows, rows)]
        return remote(src, rb.at[d - 1], rs_s.at[d - 1], rs_r.at[d - 1], sp=to)

    loop(1, SP + 1, input_part)

    loop(1, FS, lambda d: wk_copy(d).wait())
    wk_fin[s] = add_up(wk_rb, wk[f].astype(F32)).astype(BF)
    loop(1, SP, lambda d: sp_copy(2, wk_fin)(d).start())
    for e, buf in early_bufs:
        loop(1, SP, lambda d: sp_copy(e, buf)(d).wait())
    for n in range(SP):
        upg[:, 768 * n : 768 * n + 768] = up_fin[n].astype(F32)
    vecg[...] = v_fin[0] + v_fin[1] + v_fin[2] + v_fin[3]
    down_total = dn_fin[0].astype(F32)
    out_total = ou_fin[0].astype(F32)
    for n in range(1, SP):
        down_total = down_total + dn_fin[n].astype(F32)
        out_total = out_total + ou_fin[n].astype(F32)
    dng[...] = down_total
    outg[...] = out_total

    loop(1, SP, lambda d: rs_copy(d).wait())
    total = gfs[...] + own[...]
    for d in range(SP - 1):
        total = total + rb[d].astype(F32)
    input_grad[...] = total

    loop(1, FS, lambda d: wq_copy(d).wait())
    wq_fin[s] = add_up(wq_rb, wp[f].astype(F32)).astype(BF)
    loop(1, SP, lambda d: sp_copy(3, wq_fin)(d).start())
    loop(1, SP, lambda d: sp_copy(2, wk_fin)(d).wait())
    wkg[...] = wk_fin[...].astype(F32)
    loop(1, SP, lambda d: sp_copy(3, wq_fin)(d).wait())
    wqg[...] = wq_fin[...].astype(F32)


def on_device(
    hidden_in,
    qkv_weight,
    query_bias,
    value_bias,
    output_weight,
    output_bias,
    first_gain,
    first_shift,
    up_weight,
    up_bias,
    down_weight,
    down_bias,
    second_gain,
    second_shift,
    valid_length,
    out_cotangent,
):
    s = lax.axis_index("sp")
    rows, width = hidden_in.shape
    tall = SP * rows
    slim = qkv_weight.shape[0]
    deep = down_weight.shape[0]
    share = up_weight.shape[1] // SP
    cols = LH * HEAD_DIM * 3
    vmem = pl.BlockSpec(memory_space=pltpu.VMEM)
    hbm = pl.BlockSpec(memory_space=pl.ANY)
    dma = pltpu.SemaphoreType.DMA
    shape = jax.ShapeDtypeStruct

    parts = qkv_weight.reshape(slim, 3, SP, LH, HEAD_DIM)
    parts = lax.dynamic_index_in_dim(parts, s, 2, keepdims=False)
    kv_cols = jnp.stack((parts[:, 1], parts[:, 2]), axis=2).reshape(slim, -1)
    wq = jnp.concatenate((kv_cols, parts[:, 0].reshape(slim, -1)), axis=1)
    up = lax.dynamic_slice_in_dim(up_weight, s * share, share, 1)
    riders = jnp.stack(
        (
            query_bias, value_bias, output_bias, first_gain, first_shift, down_bias,
            second_gain, second_shift,
        )
    )
    riders = jnp.pad(riders, ((0, slim - 8), (0, 64 - slim)))
    riders = lax.dynamic_update_slice(riders, up_bias.reshape(4, slim), (8, 0))
    wq = jnp.concatenate((wq, riders), axis=1)
    smem = pl.BlockSpec(memory_space=pltpu.SMEM)
    hid_all, wqkv, q_all, kv_all, o_all, out_g, up_g, wdn, vecs = pl.pallas_call(
        forward_kernel,
        out_shape=(
            shape((tall, width), BF),
            shape((width, cols), BF),
            shape((YG, LH, tall, 128), BF),
            shape((XG, LH, tall, 128), BF),
            shape((YG, LH, tall, 128), BF),
            shape((8, slim, width), BF),
            shape((FS, slim, share), BF),
            shape((share, width), BF),
            shape((16, width), F32),
        ),
        in_specs=[smem] + [vmem] * 5,
        out_specs=(vmem, vmem, vmem, vmem, vmem, hbm, vmem, vmem, vmem),
        scratch_shapes=[
            pltpu.VMEM((FS, slim, cols + 64), BF),
            pltpu.VMEM((width, cols), F32),
            pltpu.VMEM((LH, tall, 128), BF),
            pltpu.VMEM((LH, tall, 128), BF),
            pltpu.VMEM((8, width), F32),
            pltpu.VMEM((YG, LH, tall, 128), F32),
            pltpu.VMEM((YG, LH, tall, 128), BF),
        ]
        + [dma((n,)) for n in (3, 3, 31, 31, 8, 8, 3, 3, 7, 7)]
        + [dma((3, 3)), dma((3, 3)), dma((1,))]
        + [dma((7,)), dma((7,)), dma((3, 2)), dma((3, 2)), dma((8,)), dma((8,))],
        compiler_params=pltpu.CompilerParams(
            collective_id=0, has_side_effects=True, vmem_limit_bytes=VMEM_LIMIT
        ),
        name="forward",
    )(valid_length, hidden_in, wq, output_weight, up, down_weight)

    result, gfs, d_all, ld_all, dup, ddn, dwo, vp = pl.pallas_call(
        middle_kernel,
        out_shape=(
            shape((rows, width), BF),
            shape((rows, width), F32),
            shape((YG, LH, tall, 128), BF),
            shape((YG, 8, tall), F32),
            shape((FS, slim, share), BF),
            shape((share, width), BF),
            shape((LH * HEAD_DIM, width), BF),
            shape((FS, 16, 128), F32),
        ),
        in_specs=[vmem] * 7,
        out_specs=(vmem, vmem, hbm, hbm, vmem, vmem, vmem, vmem),
        scratch_shapes=[
            pltpu.VMEM((width, share), F32),
            pltpu.VMEM((LH * 128, width), BF),
            pltpu.VMEM((width, share), BF),
            pltpu.VMEM((tall, LH * 128), BF),
            pltpu.VMEM((tall, 128), F32),
            pltpu.VMEM((3, tall, width), BF),
            pltpu.VMEM((rows, width), F32),
            pltpu.VMEM((rows, width), F32),
            pltpu.VMEM((rows, width), F32),
            pltpu.VMEM((rows, 128), F32),
            pltpu.VMEM((tall, width), BF),
            pltpu.VMEM((tall, share), BF),
            pltpu.VMEM((tall, share), F32),
            pltpu.VMEM((tall, width), BF),
            pltpu.VMEM((tall, share), BF),
            pltpu.VMEM((tall, width), BF),
            pltpu.VMEM((rows, width), F32),
            pltpu.VMEM((3, SP - 1, rows, width), BF),
            pltpu.VMEM((LH, tall, 128), BF),
            pltpu.VMEM((8, tall), F32),
            pltpu.VMEM((8, width), F32),
        ]
        + [dma((3, 3)) for _ in range(4)]
        + [dma((3, 4)), dma((3, 4)), dma((3,)), dma((3,)), dma((2,))],
        compiler_params=pltpu.CompilerParams(
            collective_id=1, has_side_effects=True, vmem_limit_bytes=VMEM_LIMIT
        ),
        name="middle",
    )(
        o_all, out_g, up_g, wdn, vecs,
        hidden_in, out_cotangent,
    )

    input_grad, wkg, wqg, upg, dng, outg, vecg = pl.pallas_call(
        backward_kernel,
        out_shape=(
            shape((rows, width), F32),
            shape((SP, slim, 2 * LH * HEAD_DIM), F32),
            shape((SP, slim, 256), F32),
            shape((slim, SP * share), F32),
            shape((deep, width), F32),
            shape((slim, width), F32),
            shape((16, 128), F32),
        ),
        in_specs=[smem] + [vmem] * 11,
        out_specs=(vmem,) * 7,
        scratch_shapes=[
            pltpu.VMEM((YG, LH, HEAD_DIM, tall), F32),
            pltpu.VMEM((YG, LH * HEAD_DIM, tall), BF),
            pltpu.VMEM((XG, LH, tall, 128), BF),
            pltpu.VMEM((XG - 1, LH, tall, 128), BF),
            pltpu.VMEM((YG - 1, LH * HEAD_DIM, tall), BF),
            pltpu.VMEM((tall, cols), BF),
            pltpu.VMEM((width, 640), F32),
            pltpu.VMEM((FS, slim, 384), BF),
            pltpu.VMEM((FS, slim, 256), BF),
            pltpu.VMEM((tall, width), BF),
            pltpu.VMEM((rows, width), F32),
            pltpu.VMEM((SP - 1, rows, width), BF),
            pltpu.VMEM((FS - 1, slim, 384), BF),
            pltpu.VMEM((FS - 1, slim, 256), BF),
            pltpu.VMEM((YG - 1, 2, YG, slim, share), BF),
            pltpu.VMEM((8, deep, width), BF),
            pltpu.VMEM((8, slim, share), BF),
            pltpu.VMEM((XG - 1, slim, share), BF),
            pltpu.VMEM((8, slim, width), BF),
            pltpu.VMEM((FS - 1, 16, 128), F32),
            pltpu.VMEM((SP, slim, share), BF),
            pltpu.VMEM((SP, deep, width), BF),
            pltpu.VMEM((SP, slim, width), BF),
            pltpu.VMEM((SP, 16, 128), F32),
            pltpu.VMEM((SP, slim, 384), BF),
            pltpu.VMEM((SP, slim, 256), BF),
        ]
        + [dma((n,)) for n in (7, 7, 3, 3, 31, 31, 31, 31, 7, 7, 8, 8, 31, 31, 3, 3)]
        + [dma((6, 3)), dma((6, 3)), dma((3, 2)), dma((3, 2)), dma((8,)), dma((8,))],
        compiler_params=pltpu.CompilerParams(
            collective_id=2, has_side_effects=True, vmem_limit_bytes=VMEM_LIMIT
        ),
        name="backward",
    )(
        valid_length, q_all, d_all, ld_all, kv_all, hid_all, wqkv, gfs,
        dup, ddn, dwo.reshape(8, slim, width), vp,
    )

    kv_grad = wkg.reshape(SP, slim, LH, 2, HEAD_DIM)
    q_grad = wqg[:, :, : LH * HEAD_DIM].reshape(SP, slim, LH, 1, HEAD_DIM)
    qkv_grad = jnp.concatenate((q_grad, kv_grad), axis=3)
    qkv_grad = jnp.transpose(qkv_grad, (1, 3, 0, 2, 4)).reshape(slim, -1)
    qv_grad = jnp.sum(wqg[:, 0:2, LH * HEAD_DIM : LH * HEAD_DIM + slim], axis=0)
    return (
        result,
        input_grad,
        qkv_grad,
        qv_grad[0],
        qv_grad[1],
        outg,
        vecg[0, :slim],
        vecg[1, :slim],
        vecg[2, :slim],
        upg,
        vecg[8, :deep],
        dng,
        vecg[3, :slim],
        vecg[4, :slim],
        vecg[5, :slim],
    )


def solution(mesh):
    placed = (
        P(("fsdp", "sp"), None),
        P("fsdp", None),
        P("fsdp"),
        P("fsdp"),
        P("fsdp", None),
        P("fsdp"),
        P("fsdp"),
        P("fsdp"),
        P("fsdp", None),
        P("fsdp"),
        P("fsdp", None),
        P("fsdp"),
        P("fsdp"),
        P("fsdp"),
        P(),
        P(("fsdp", "sp"), None),
    )
    return jax.shard_map(
        on_device,
        mesh=mesh,
        in_specs=placed,
        out_specs=(
            P(("fsdp", "sp"), None),
            P(("fsdp", "sp"), None),
            P("fsdp", None),
            P("fsdp"),
            P("fsdp"),
            P("fsdp", None),
            P("fsdp"),
            P("fsdp"),
            P("fsdp"),
            P("fsdp", None),
            P("fsdp"),
            P("fsdp", None),
            P("fsdp"),
            P("fsdp"),
            P("fsdp"),
        ),
        check_vma=False,
    )
```

```python
import functools

import jax
import jax.numpy as jnp
from jax import lax
from jax.experimental import pallas as pl
from jax.experimental.pallas import tpu as pltpu
from jax.sharding import PartitionSpec as P

HEADS = 12
HEAD_DIM = 64
SP = 4
FS = 32
YG = 4
XG = 8
LH = HEADS // SP

KEY_STEPS = ((0, 1), (0, 3), (1, 0), (0, 2), (1, 1), (1, 3), (1, 2))
PASSES = ((0, 1, 2), (3, 4, 5, 6))
UP_STEP = 1

BF = jnp.bfloat16
F32 = jnp.float32
MESH = pl.DeviceIdType.MESH
epsilon = 1e-05
masked = -1e30
VMEM_LIMIT = 56 * 1024 * 1024


def dot_nn(a, b):
    return lax.dot_general(a, b, (((1,), (0,)), ((), ())), preferred_element_type=F32)


def dot_nt(a, b):
    return lax.dot_general(a, b, (((1,), (1,)), ((), ())), preferred_element_type=F32)


def dot_tn(a, b):
    return lax.dot_general(a, b, (((0,), (0,)), ((), ())), preferred_element_type=F32)


def norm_forward(incoming, norm_gain, norm_shift):
    row_mean = jnp.mean(incoming, axis=-1, keepdims=True)
    centered = incoming - row_mean
    inverse = lax.rsqrt(jnp.mean(centered * centered, axis=-1, keepdims=True) + epsilon)
    normed = centered * inverse
    return (normed * norm_gain + norm_shift, normed, inverse)


def norm_backward(incoming, normed, inverse, norm_gain):
    scaled = incoming * norm_gain
    adjusted = (
        scaled
        - jnp.mean(scaled, axis=-1, keepdims=True)
        - normed * jnp.mean(scaled * normed, axis=-1, keepdims=True)
    )
    return (
        adjusted * inverse,
        jnp.sum(incoming * normed, axis=0, keepdims=True),
        jnp.sum(incoming, axis=0, keepdims=True),
    )


def loop(low, high, body):
    def step(d, carried):
        body(d)
        return carried

    lax.fori_loop(low, high, step, 0)


def remote(src, dst, send, recv, **device):
    return pltpu.make_async_remote_copy(
        src_ref=src,
        dst_ref=dst,
        send_sem=send,
        recv_sem=recv,
        device_id=device,
        device_id_type=MESH,
    )


def greet(barrier, **device):
    pl.semaphore_signal(barrier, inc=1, device_id=device, device_id_type=MESH)


def greet_all(f, s):
    barrier = pltpu.get_barrier_semaphore()
    loop(1, FS, lambda d: greet(barrier, fsdp=lax.rem(f + d, FS)))
    loop(1, SP, lambda d: greet(barrier, sp=lax.rem(s + d, SP)))

    @pl.when(s != f // 8)
    def _():
        loop(0, 8, lambda t: greet(barrier, fsdp=8 * s + t, sp=f // 8))

    pl.semaphore_wait(barrier, FS - 1 + SP - 1 + jnp.where(s != f // 8, 8, 0))


def forward_kernel(
    valid, hid, wq, out, up, down,
    hid_all, wqkv, q_all, kv_all, o_all, out_g, up_g, wdn, vecs,
    wq_g, wf, q_st, kv_st, qvb, state, o_st,
    hid_s, hid_r, wq_s, wq_r, ou_s, ou_r,
    q_s, q_r, kv_s, kv_r, o_s, o_r, loc,
    ua_s, ua_r, ub_s, ub_r, dn_s, dn_r,
):
    s = lax.axis_index("sp")
    f = lax.axis_index("fsdp")
    i, j = f // YG, lax.rem(f, YG)
    greet_all(f, s)
    rows = hid.shape[0]

    def hid_copy(d):
        dst = hid_all.at[pl.ds(s * rows, rows)]
        return remote(hid, dst, hid_s.at[d - 1], hid_r.at[d - 1], sp=lax.rem(s + d, SP))

    def fs_copy(src, buf, send, recv):
        return lambda d: remote(
            src, buf.at[f], send.at[d - 1], recv.at[d - 1], fsdp=lax.rem(f + d, FS)
        )

    wq_copy = fs_copy(wq, wq_g, wq_s, wq_r)

    def out_copy(t):
        k = lax.rem(f, 8)
        return remote(out, out_g.at[k], ou_s.at[t], ou_r.at[k], fsdp=8 * s + t, sp=f // 8)

    def out_arrival(k):
        return remote(out, out_g.at[k], ou_s.at[k], ou_r.at[k], fsdp=8 * s + k, sp=f // 8)

    z, x = f // 16, lax.rem(i, YG)

    def zy_copy(n):
        to = (lax.rem(z + (n + 1) // YG, 2) * YG + x) * YG + lax.rem(j + n + 1, YG)
        return remote(up, up_g.at[f], ua_s.at[n], ua_r.at[n], fsdp=to)

    def x_copy(d):
        to = (z * YG + lax.rem(x + d, YG)) * YG + j
        copies = []
        for n in range(2):
            at = up_g.at[pl.ds((n * YG + x) * YG, YG)]
            copies.append(remote(at, at, ub_s.at[d - 1, n], ub_r.at[d - 1, n], fsdp=to))
        return copies

    def down_copy(t):
        k = lax.rem(f, 8)
        dst = wdn.at[pl.ds(k * 96, 96)]
        return remote(down, dst, dn_s.at[t], dn_r.at[k], fsdp=8 * s + t, sp=f // 8)

    def down_arrival(k):
        dst = wdn.at[pl.ds(k * 96, 96)]
        return remote(down, dst, dn_s.at[k], dn_r.at[k], fsdp=8 * s + k, sp=f // 8)

    def is_self(t):
        return (s == f // 8) & (8 * s + t == f)

    def unless_self(work):
        def step(t):
            @pl.when(jnp.logical_not(is_self(t)))
            def _():
                work(t)

        loop(0, 8, step)

    loop(1, SP, lambda d: hid_copy(d).start())

    loop(1, FS, lambda d: wq_copy(d).start())
    hid_all[pl.ds(pl.multiple_of(s * rows, rows), rows), :] = hid[...]
    wq_g[f] = wq[...]
    loop(1, SP, lambda d: hid_copy(d).wait())

    loop(1, FS, lambda d: wq_copy(d).wait())

    width = vecs.shape[1]
    pad = jnp.zeros((8, width - 64), F32)

    def riders(n, low):
        block = wq_g[n, low : low + 8, 512:640].astype(F32)
        wide = jnp.concatenate((block[:, 64:128], pad), axis=1)
        return wide

    def shifted(wide, amount):
        return wide if amount == 0 else pltpu.roll(wide, amount, 1)

    qv = jnp.zeros((8, width), F32)
    for n in range(8):
        qv = qv + shifted(riders(8 * s + n, 0), 24 * n)
    qvb[...] = qv
    lane = lax.broadcasted_iota(jnp.int32, (1, width), 1)
    qrow = qvb[0:1, :]
    vrow = qvb[1:2, :]
    bias = jnp.zeros((1, width), F32)
    wide_q = jnp.broadcast_to(qrow, (8, width))
    wide_v = jnp.broadcast_to(vrow, (8, width))
    bias = jnp.where((lane >= 384) & (lane < 576), pltpu.roll(wide_q, 384, 1)[0:1], 0.0)
    for h in range(LH):
        here = (lane >= 128 * h + 64) & (lane < 128 * h + 128)
        bias = bias + jnp.where(here, pltpu.roll(wide_v, 64 * h + 64, 1)[0:1], 0.0)

    def assemble(n):
        wf[pl.ds(pl.multiple_of(24 * n, 8), 24), :] = wq_g[n, :, 0:576].astype(F32)

    loop(0, FS, assemble)
    wqkv[...] = wf[...].astype(BF)

    low_lane = lax.broadcasted_iota(jnp.int32, (rows, 128), 1) < HEAD_DIM

    def project(b):
        at = pl.ds(pl.multiple_of(b * rows, rows), rows)
        p = dot_nn(hid_all[at, :], wqkv[...]) + bias[:, :576]
        for h in range(LH):
            kv_st[h, at, :] = p[:, 128 * h : 128 * h + 128].astype(BF)
        q01 = p[:, 384:512] * 0.125
        q2 = jnp.concatenate((p[:, 512:576], jnp.zeros((rows, 64), F32)), axis=1) * 0.125
        q_st[0, at, :] = jnp.where(low_lane, q01, 0.0).astype(BF)
        q_st[1, at, :] = jnp.where(low_lane, pltpu.roll(q01, 64, 1), 0.0).astype(BF)
        q_st[2, at, :] = q2.astype(BF)

    loop(0, SP, project)

    def kv_copy(n):
        dz, dx = KEY_STEPS[n]
        to = lax.rem(i // YG + dz, 2) * YG + lax.rem(i + dx, YG)
        return remote(kv_st, kv_all.at[i], kv_s.at[n], kv_r.at[n], fsdp=to * YG + j)

    def kv_from(n):
        dz, dx = KEY_STEPS[n]
        return lax.rem(i // YG + dz, 2) * YG + lax.rem(i + YG - dx, YG)

    def q_copy(d):
        to = i * YG + lax.rem(j + d, YG)
        return remote(q_st, q_all.at[j], q_s.at[d - 1], q_r.at[d - 1], fsdp=to)

    loop(1, YG, lambda d: q_copy(d).start())
    for n in range(XG - 1):
        kv_copy(n).start()
    kv_all[i] = kv_st[...]
    q_all[j] = q_st[...]

    total = jnp.zeros((8, width), F32)
    for n in range(FS):
        total = total + shifted(riders(n, 0), 24 * n)
    vecs[0:8, :] = total
    ub = jnp.zeros((8, width), F32)
    for n in range(8):
        rider = riders(8 * s + n, 8)
        for c in range(4):
            row = jnp.broadcast_to(rider[c : c + 1], (8, width))
            ub = ub + shifted(row, 96 * n + 24 * c)
    vecs[8:16, :] = ub

    def send_out(t):
        @pl.when(jnp.logical_not(is_self(t)))
        def _():
            out_copy(t).start()

    loop(0, 8, send_out)

    @pl.when(s == f // 8)
    def _():
        out_own = pltpu.make_async_copy(out, out_g.at[lax.rem(f, 8)], loc.at[0])
        out_own.start()
        out_own.wait()

    for n in range(XG - 1):
        zy_copy(n).start()
    unless_self(lambda t: down_copy(t).start())
    up_g[f] = up[...]

    @pl.when(s == f // 8)
    def _():
        wdn[pl.ds(pl.multiple_of(lax.rem(f, 8) * 96, 32), 96), :] = down[...]

    tall = SP * rows
    key_place = lax.broadcasted_iota(jnp.int32, (1, tall), 1)
    half = tall // 2
    lanes = lax.broadcasted_iota(jnp.int32, (half, 128), 1)

    def o_copy(d, h):
        to = lax.rem(j + YG - d, YG)
        src = o_st.at[to, h]
        return remote(src, o_all.at[j, h], o_s.at[d - 1, h], o_r.at[d - 1, h], fsdp=i * YG + to)

    def attend(places, is_first, is_last):
        limits = [
            jnp.where((at * YG + j) * tall + key_place < valid[0], 0.0, masked) for at in places
        ]

        def tile(t):
            d = t // LH
            h = lax.rem(t, LH)
            n = lax.rem(j + YG - d, YG)
            if is_first:

                @pl.when((d > 0) & (h == 0))
                def _():
                    q_copy(d).wait_recv()

            for r in range(2):
                part_at = pl.ds(r * half, half)
                query = q_all[n, h, part_at, :]
                blocks = [kv_all[at, h] for at in places]
                scores = [dot_nt(query, block) + limit for block, limit in zip(blocks, limits)]
                tops = [jnp.max(score, axis=1, keepdims=True) for score in scores]
                top = functools.reduce(jnp.maximum, tops)
                if not is_first:
                    old = state[n, h, part_at, :]
                    before = old[:, 0:1]
                    top = jnp.maximum(top, before)
                probs = [jnp.exp(score - top) for score in scores]
                total = functools.reduce(
                    jnp.add, [jnp.sum(p, axis=1, keepdims=True) for p in probs]
                )
                weighted = functools.reduce(
                    jnp.add, [dot_nn(p.astype(BF), block) for p, block in zip(probs, blocks)]
                )
                if not is_first:
                    decay = jnp.exp(before - top)
                    total = total + decay * old[:, 32:33]
                    weighted = weighted + decay * old
                if is_last:
                    log_sum = top + jnp.log(total)
                    high = log_sum.astype(BF).astype(F32)
                    logs = jnp.where(lanes < 32, high, log_sum - high)
                    merged = jnp.where(lanes >= 64, weighted / total, logs)
                    o_st[n, h, part_at, :] = merged.astype(BF)
                else:
                    logs = jnp.where(lanes < 32, top, total)
                    state[n, h, part_at, :] = jnp.where(lanes >= 64, weighted, logs)
            if is_last:

                @pl.when(d > 0)
                def _():
                    o_copy(d, h).start()

                @pl.when(d == 0)
                def _():
                    o_all[j, h] = o_st[j, h]

        if is_last:
            loop(LH, LH * YG, tile)
            loop(0, LH, tile)
        else:
            loop(0, LH * YG, tile)

    attend([i], True, False)
    for step, members in enumerate(PASSES):
        for n in members:
            kv_copy(n).wait_recv()
        if step == UP_STEP:
            for n in range(XG - 1):
                zy_copy(n).wait()
            for d in range(1, YG):
                for copy in x_copy(d):
                    copy.start()
        places = [kv_from(n) for n in members]
        attend(places, False, step == len(PASSES) - 1)

    for d in range(1, YG):
        for copy in x_copy(d):
            copy.wait()
    unless_self(lambda t: (down_copy(t).wait_send(), down_arrival(t).wait_recv()))
    for n in range(XG - 1):
        kv_copy(n).wait_send()
    loop(1, YG, lambda d: q_copy(d).wait_send())

    def owned_wait(t):
        @pl.when(jnp.logical_not(is_self(t)))
        def _():
            out_copy(t).wait_send()
            out_arrival(t).wait_recv()

    loop(0, 8, owned_wait)
    loop(1, YG, lambda d: loop(0, LH, lambda h: o_copy(d, h).wait()))


def middle_kernel(
    o_all, out_g, up_g, wdn, vecs, hid, cot,
    result, gfs, d_all, ld_all, dup, ddn, dwo, vp,
    wf, wo, wup,
    att, ld, st, own, first, n1, inv1, x_all, act, deriv, gd, gp, gb, gsec, rb, dbuf, ldrow, vg,
    ag_s, ag_r, rs_s, rs_r, d_s, d_r, l_s, l_r, loc,
):
    s = lax.axis_index("sp")
    f = lax.axis_index("fsdp")
    i, j = f // YG, lax.rem(f, YG)
    rows = hid.shape[0]
    tall = SP * rows
    barrier = pltpu.get_barrier_semaphore()
    loop(1, YG, lambda d: greet(barrier, fsdp=i * YG + lax.rem(j + d, YG)))
    loop(1, SP, lambda d: greet(barrier, sp=lax.rem(s + d, SP)))
    pl.semaphore_wait(barrier, YG - 1 + SP - 1)

    wf[0:192, :] = out_g[...].astype(F32).reshape(192, wf.shape[1])
    for h in range(LH):
        wo[128 * h : 128 * h + 64, :] = jnp.zeros((64, wo.shape[1]), BF)
        wo[128 * h + 64 : 128 * h + 128, :] = wf[64 * h : 64 * h + 64, :].astype(BF)

    def y_peer(d):
        return i * YG + lax.rem(j + d, YG)

    def span(b):
        return pl.ds(pl.multiple_of(b * rows, rows), rows)

    lane = lax.broadcasted_iota(jnp.int32, (rows, 128), 1)

    def merge(b):
        at = span(b)
        sums = jnp.zeros((rows, 128), F32)
        for h in range(LH):
            parts = [o_all[d, h, at, :].astype(F32) for d in range(YG)]
            logs = [p[:, 0:1] + p[:, 32:33] for p in parts]
            top = functools.reduce(jnp.maximum, logs)
            weights = [jnp.exp(g - top) for g in logs]
            total = functools.reduce(jnp.add, weights)
            merged = functools.reduce(jnp.add, [p * w for p, w in zip(parts, weights)]) / total
            att[at, 128 * h : 128 * h + 128] = jnp.where(lane >= 64, merged, 0.0).astype(BF)
            sums = jnp.where(lane == 2 * h, top + jnp.log(total), sums)
        ld[at, :] = sums

    loop(0, SP, merge)

    def gather(e, buf):
        def copy(d):
            at = buf.at[pl.ds(s * rows, rows)]
            return remote(at, at, ag_s.at[e, d - 1], ag_r.at[e, d - 1], sp=lax.rem(s + d, SP))

        return copy

    def scatter(e):
        def copy(d):
            src = st.at[e, pl.ds(lax.rem(s + d, SP) * rows, rows)]
            sems = (rs_s.at[e, d - 1], rs_r.at[e, d - 1])
            return remote(src, rb.at[e, d - 1], *sems, sp=lax.rem(s + d, SP))

        return copy

    def collect(e):
        loop(1, SP, lambda d: scatter(e)(d).wait())
        total = own[...]
        for d in range(SP - 1):
            total = total + rb[e, d].astype(F32)
        return total

    def out_part(d):
        b = lax.rem(s + d, SP)
        value = dot_nn(att[span(b), :], wo[...])

        @pl.when(d < SP)
        def _():
            st[0, span(b), :] = value.astype(BF)
            scatter(0)(d).start()

        @pl.when(d == SP)
        def _():
            own[...] = value

    loop(1, SP + 1, out_part)
    summed = hid[...].astype(F32) + collect(0) + vecs[2:3, :]
    value, normed, inverse = norm_forward(summed, vecs[3:4, :], vecs[4:5, :])
    first[...] = value
    n1[...] = normed
    inv1[...] = jnp.broadcast_to(inverse, inv1.shape)
    x_all[span(s), :] = value.astype(BF)
    loop(1, SP, lambda d: gather(0, x_all)(d).start())

    def assemble(n):
        wf[pl.ds(pl.multiple_of(24 * n, 8), 24), :] = up_g[n].astype(F32)

    loop(0, FS, assemble)
    wup[...] = wf[...].astype(BF)

    def pipeline(e, buf, work):
        def step(d):
            b = lax.rem(s + SP - d, SP)

            @pl.when(d > 0)
            def _():
                gather(e, buf)(d).wait_recv()

            value = work(b)

            @pl.when(d > 0)
            def _():
                st[e + 1, span(b), :] = value.astype(BF)
                scatter(e + 1)(SP - d).start()

            @pl.when(d == 0)
            def _():
                own[...] = value

        loop(0, SP, step)
        loop(1, SP, lambda d: gather(e, buf)(d).wait_send())

    def feed(b):
        at = span(b)
        pre = dot_nn(x_all[at, :], wup[...]) + vecs[8:9, :]
        cdf = 0.5 * (1.0 + lax.erf(pre * 0.7071067811865476))
        density = jnp.exp(-0.5 * pre * pre) * 0.3989422804014327
        active = (pre * cdf).astype(BF)
        act[at, :] = active
        deriv[at, :] = cdf + pre * density
        return dot_nn(active, wdn[...])

    pipeline(0, x_all, feed)
    summed = first[...] + collect(1) + vecs[5:6, :]
    value, normed, inverse = norm_forward(summed, vecs[6:7, :], vecs[7:8, :])
    result[...] = value.astype(BF)
    grad, ggain, gshift = norm_backward(cot[...].astype(F32), normed, inverse, vecs[6:7, :])
    gsec[...] = grad
    low = grad.astype(BF)
    gd[span(s), :] = low
    loop(1, SP, lambda d: gather(1, gd)(d).start())
    vg[...] = jnp.zeros(vg.shape, F32)
    vg[3:4, :] = jnp.sum(low.astype(F32), axis=0, keepdims=True)
    vg[4:5, :] = ggain
    vg[5:6, :] = gshift

    def back(b):
        at = span(b)
        grad_pre = (dot_nt(gd[at, :], wdn[...]) * deriv[at, :]).astype(BF)
        gp[at, :] = grad_pre
        return dot_nt(grad_pre, wup[...])

    pipeline(1, gd, back)

    def weight_terms(c):
        at = pl.ds(pl.multiple_of(128 * c, 128), 128)
        wf[at, :] = dot_tn(x_all[:, at], gp[...])
        ddn[at, :] = dot_tn(act[:, at], gd[...]).astype(BF)

    loop(0, act.shape[1] // 128, weight_terms)

    def cut(n):
        dup[n] = wf[pl.ds(pl.multiple_of(24 * n, 8), 24), :].astype(BF)

    loop(0, FS, cut)

    ub = jnp.sum(gp[...].astype(F32), axis=0, keepdims=True)
    grad_first = gsec[...] + collect(2)
    grad, ggain, gshift = norm_backward(grad_first, n1[...], inv1[:, 0:1], vecs[3:4, :])
    gfs[...] = grad
    low = grad.astype(BF)
    gb[span(s), :] = low
    loop(1, SP, lambda d: gather(2, gb)(d).start())
    vg[0:1, :] = jnp.sum(low.astype(F32), axis=0, keepdims=True)
    vg[1:2, :] = ggain
    vg[2:3, :] = gshift

    def branch(d):
        b = lax.rem(s + SP - d, SP)
        at = span(b)

        @pl.when(d > 0)
        def _():
            gather(2, gb)(d).wait_recv()

        value = dot_nt(gb[at, :], wo[...]).astype(BF)
        sums = ld[at, :]
        for h in range(LH):
            part = value[:, 128 * h : 128 * h + 128]
            dbuf[h, at, :] = part
            product = part.astype(F32) * att[at, 128 * h : 128 * h + 128].astype(F32)
            sums = jnp.where(lane == 2 * h + 1, jnp.sum(product, axis=1, keepdims=True), sums)
        ld[at, :] = sums
        loop(1, YG, lambda n: d_copy(n, d).start())

    def d_copy(n, d):
        at = span(lax.rem(s + SP - d, SP))
        sems = (d_s.at[n - 1, d], d_r.at[n - 1, d])
        return remote(dbuf.at[:, at], d_all.at[j, :, at], *sems, fsdp=y_peer(n))

    loop(0, SP, branch)
    loop(1, SP, lambda d: gather(2, gb)(d).wait_send())
    ldrow[...] = jnp.transpose(ld[...], (1, 0))[0:8, :]

    def l_copy(d):
        return remote(ldrow, ld_all.at[j], l_s.at[d - 1], l_r.at[d - 1], fsdp=y_peer(d))

    loop(1, YG, lambda d: l_copy(d).start())
    d_own = pltpu.make_async_copy(dbuf, d_all.at[j], loc.at[0])
    l_own = pltpu.make_async_copy(ldrow, ld_all.at[j], loc.at[1])
    d_own.start()
    l_own.start()
    for h in range(LH):
        value = dot_tn(att[:, 128 * h : 128 * h + 128], gb[...])
        dwo[64 * h : 64 * h + 64, :] = value[64:128].astype(BF)
    lane8 = lax.broadcasted_iota(jnp.int32, (8, 128), 1)
    wide = vg[...]
    width = wide.shape[1]
    ub_wide = jnp.broadcast_to(ub, (8, width))
    for n in range(FS):
        piece = wide if n == 0 else pltpu.roll(wide, width - 24 * n, 1)
        vp[n, 0:8, :] = jnp.where(lane8 < 24, piece[:, 0:128], 0.0)
        vp[n, 8:16, :] = jnp.zeros((8, 128), F32)
    for k in range(8):
        piece = ub_wide if k == 0 else pltpu.roll(ub_wide, width - 96 * k, 1)
        vp[8 * s + k, 8:16, :] = jnp.where(lane8 < 96, piece[:, 0:128], 0.0)
    d_own.wait()
    l_own.wait()
    loop(1, YG, lambda n: loop(0, SP, lambda d: d_copy(n, d).wait()))
    loop(1, YG, lambda d: l_copy(d).wait())


def backward_kernel(
    valid, q_all, d_all, ld, kv_all, hid_all, wqkv, gfs, dup, ddn, dwo, vp,
    input_grad, wkg, wqg, upg, dng, outg, vecg,
    acc, dq, dkv, kv_rb, q_rb, g, wf, wk, wp, st, own, rb, wk_rb, wq_rb, up_rb, dn_rb, up_st, up_rc, ou_rb, vp_rb,
    up_fin, dn_fin, ou_fin, v_fin, wk_fin, wq_fin,
    kv_s, kv_r, q_s, q_r, wk_s, wk_r, wq_s, wq_r, up_s, up_r, ou_s, ou_r, vp_s, vp_r,
    rs_s, rs_r, fin_s, fin_r, us_s, us_r, ds_s, ds_r,
):
    s = lax.axis_index("sp")
    f = lax.axis_index("fsdp")
    i, j = f // YG, lax.rem(f, YG)
    rows = gfs.shape[0]
    tall = SP * rows
    greet_all(f, s)

    def kv_copy(d, h):
        to = lax.rem(i + d, XG)
        sems = (kv_s.at[d - 1, h], kv_r.at[d - 1, h])
        return remote(dkv.at[d - 1, h], kv_rb.at[d - 1, h], *sems, fsdp=to * YG + j)

    def q_copy(d, h):
        to = lax.rem(j + d, YG)
        at = pl.ds(pl.multiple_of(64 * h, 64), 64)
        sems = (q_s.at[d - 1, h], q_r.at[d - 1, h])
        return remote(dq.at[to, at], q_rb.at[d - 1, at], *sems, fsdp=i * YG + to)

    def fs_copy(src, buf, send, recv):
        def copy(d):
            to = lax.rem(f + d, FS)
            return remote(src.at[to], buf.at[d - 1], send.at[d - 1], recv.at[d - 1], fsdp=to)

        return copy

    vp_copy = fs_copy(vp, vp_rb, vp_s, vp_r)
    wq_copy = fs_copy(wp, wq_rb, wq_s, wq_r)
    wk_copy = fs_copy(wk, wk_rb, wk_s, wk_r)
    z, x = f // 16, lax.rem(i, YG)

    def up_copy(n):
        zn, yn = lax.rem(z + (n + 1) // YG, 2), lax.rem(j + n + 1, YG)
        to = (zn * YG + x) * YG + yn
        return remote(up_st.at[zn * YG + yn], up_rc.at[n], up_s.at[n], up_r.at[n], fsdp=to)

    def out_copy(k):
        n = lax.rem(f, 8)
        return remote(dwo.at[k], ou_rb.at[n], ou_s.at[k], ou_r.at[n], fsdp=8 * s + k, sp=f // 8)

    def out_arrival(n):
        return remote(dwo.at[n], ou_rb.at[n], ou_s.at[n], ou_r.at[n], fsdp=8 * s + n, sp=f // 8)

    def is_self(t):
        return (s == f // 8) & (8 * s + t == f)

    def unless_self(work):
        def step(t):
            @pl.when(jnp.logical_not(is_self(t)))
            def _():
                work(t)

        loop(0, 8, step)

    def up_sum(d):
        to = lax.rem(x + d, YG)
        copies = []
        for n in range(2):
            src = dup.at[pl.ds((n * YG + to) * YG, YG)]
            sems = (us_s.at[d - 1, n], us_r.at[d - 1, n])
            copies.append(remote(src, up_rb.at[d - 1, n], *sems, fsdp=(z * YG + to) * YG + j))
        return copies

    def down_sum(t):
        k = lax.rem(f, 8)
        src = ddn.at[pl.ds(t * 96, 96)]
        return remote(src, dn_rb.at[k], ds_s.at[t], ds_r.at[k], fsdp=8 * s + t, sp=f // 8)

    def down_sum_arrival(k):
        src = ddn.at[pl.ds(k * 96, 96)]
        return remote(src, dn_rb.at[k], ds_s.at[k], ds_r.at[k], fsdp=8 * s + k, sp=f // 8)

    for d in range(1, YG):
        for copy in up_sum(d):
            copy.start()
    unless_self(lambda t: down_sum(t).start())
    @pl.when(s == f // 8)
    def _():
        k = lax.rem(f, 8)
        dn_rb[k] = ddn[pl.ds(pl.multiple_of(k * 96, 32), 96), :]

    loop(1, FS, lambda d: vp_copy(d).start())

    def to_owner(k):
        @pl.when(jnp.logical_not(is_self(k)))
        def _():
            out_copy(k).start()

        @pl.when(is_self(k))
        def _():
            ou_rb[k] = dwo[k]

    loop(0, 8, to_owner)

    acc[...] = jnp.zeros(acc.shape, F32)

    def key_step(d, h):
        at = lax.rem(i + d, XG)
        first_key = (at * YG + j) * tall

        def work(last):
            block = kv_all[at, h]
            flipped = jnp.transpose(block.astype(F32), (1, 0))[0:HEAD_DIM].astype(BF)
            total = None
            for n in range(YG):
                query = q_all[n, h]
                grad = d_all[n, h]
                log_sum = ld[n, pl.ds(2 * h, 1), :]
                delta = ld[n, pl.ds(2 * h + 1, 1), :]
                scores = dot_nt(block, query)
                if last:
                    place = first_key + lax.broadcasted_iota(jnp.int32, (tall, 1), 0)
                    scores = jnp.where(place < valid[0], scores, masked)
                p = jnp.exp(scores - log_sum)
                grad_p = dot_nt(block, grad)
                grad_s = (p * (grad_p - delta)).astype(BF)
                terms = dot_nn(grad_s, query) + dot_nn(p.astype(BF), grad)
                total = terms if n == 0 else total + terms
                acc[n, h] = acc[n, h] + dot_nn(flipped, grad_s)
            dkv[d - 1, h] = total.astype(BF)

        @pl.when(at < XG - 1)
        def _():
            work(False)

        @pl.when(at == XG - 1)
        def _():
            work(True)

        @pl.when(d < XG)
        def _():
            kv_copy(d, h).start()

    def second_stage():
        for d in range(1, YG):
            for copy in up_sum(d):
                copy.wait()
        for n in range(2):
            for c in range(YG):
                total = dup[(n * YG + x) * YG + c].astype(F32)
                for d in range(YG - 1):
                    total = total + up_rb[d, n, c].astype(F32)
                up_st[n * YG + c] = total.astype(BF)
        for n in range(XG - 1):
            up_copy(n).start()

    def head(h):
        loop(1, XG + 1, lambda d: key_step(d, h))
        for n in range(YG):
            dq[n, pl.ds(pl.multiple_of(64 * h, 64), 64), :] = acc[n, h].astype(BF)
        loop(1, YG, lambda d: q_copy(d, h).start())

        @pl.when(h == 0)
        def _():
            second_stage()

    loop(0, LH, head)

    def span(b):
        return pl.ds(pl.multiple_of(b * rows, rows), rows)

    def sum_keys(b):
        at = span(b)
        for h in range(LH):
            total = dkv[XG - 1, h, at, :].astype(F32)
            for d in range(XG - 1):
                total = total + kv_rb[d, h, at, :].astype(F32)
            g[at, 128 * h : 128 * h + 128] = total.astype(BF)

    loop(1, XG, lambda d: loop(0, LH, lambda h: kv_copy(d, h).wait()))
    loop(0, SP, sum_keys)

    def key_terms(c):
        at = pl.ds(pl.multiple_of(128 * c, 128), 128)
        wf[at, 0:384] = dot_tn(hid_all[:, at], g[:, 0:384])

    loop(0, wf.shape[0] // 128, key_terms)

    def cut_keys(n):
        wk[n] = wf[pl.ds(pl.multiple_of(24 * n, 8), 24), 0:384].astype(BF)

    loop(0, FS, cut_keys)
    loop(1, FS, lambda d: wk_copy(d).start())

    def add_up(buf, start):
        def step(d, total):
            return total + buf[d].astype(F32)

        return lax.fori_loop(0, buf.shape[0], step, start)

    for n in range(XG - 1):
        up_copy(n).wait()
    loop(1, FS, lambda d: vp_copy(d).wait())
    up_fin[s] = add_up(up_rc, up_st[z * YG + j].astype(F32)).astype(BF)
    v_fin[s] = add_up(vp_rb, vp[f])

    def owner_wait(t):
        @pl.when(jnp.logical_not(is_self(t)))
        def _():
            out_copy(t).wait_send()
            out_arrival(t).wait_recv()

    loop(0, 8, owner_wait)
    unless_self(lambda t: (down_sum(t).wait_send(), down_sum_arrival(t).wait_recv()))

    def down_rows(c):
        at = pl.ds(pl.multiple_of(c * 32, 32), 32)
        total = dn_rb[0, at, :].astype(F32)
        for n in range(1, 8):
            total = total + dn_rb[n, at, :].astype(F32)
        dn_fin[s, at, :] = total.astype(BF)

    loop(0, dn_fin.shape[1] // 32, down_rows)

    ou_fin[s] = add_up(ou_rb, jnp.zeros(ou_fin.shape[1:], F32)).astype(BF)

    def sp_copy(e, buf):
        def copy(d):
            at = buf.at[s]
            return remote(at, at, fin_s.at[e, d - 1], fin_r.at[e, d - 1], sp=lax.rem(s + d, SP))

        return copy

    early_bufs = ((0, up_fin), (1, v_fin), (4, dn_fin), (5, ou_fin))
    for e, buf in early_bufs:
        loop(1, SP, lambda d: sp_copy(e, buf)(d).start())

    for h in range(LH):
        for d in range(1, YG):
            q_copy(d, h).wait()
    total = dq[j].astype(F32)
    for d in range(YG - 1):
        total = total + q_rb[d].astype(F32)
    g[:, 384:576] = (jnp.transpose(total, (1, 0)) * 0.125).astype(BF)

    def query_terms(c):
        at = pl.ds(pl.multiple_of(128 * c, 128), 128)
        value = dot_tn(hid_all[:, at], g[:, 384:576])
        wf[at, 384:640] = jnp.concatenate((value, jnp.zeros((128, 64), F32)), axis=1)

    loop(0, wf.shape[0] // 128, query_terms)

    sums = jnp.sum(g[...].astype(F32), axis=0, keepdims=True)
    row = lax.broadcasted_iota(jnp.int32, (8, 256), 0)
    low = lax.broadcasted_iota(jnp.int32, (8, 128), 1) < 64
    wide = jnp.broadcast_to(jnp.concatenate((sums, jnp.zeros((1, 64), F32)), axis=1), (8, 640))
    heads = [pltpu.roll(wide[:, 128 * h : 128 * h + 128], 64, 1) for h in range(LH)]
    vrow = jnp.concatenate(
        (jnp.where(low, heads[0], wide[:, 128:256]), jnp.where(low, heads[2], 0.0)), axis=1
    )
    both = jnp.where(row == 0, wide[:, 384:640], jnp.where(row == 1, vrow, 0.0))

    def cut_queries(n):
        wp[n] = wf[pl.ds(pl.multiple_of(24 * n, 8), 24), 384:640].astype(BF)

    loop(0, FS, cut_queries)
    lane = lax.broadcasted_iota(jnp.int32, (8, 128), 1)
    for n in range(8):
        piece = both if n == 0 else pltpu.roll(both, 256 - 24 * n, 1)
        piece = pltpu.roll(piece[:, 0:128], 64, 1)
        piece = jnp.where((lane >= 64) & (lane < 88), piece, 0.0)
        rest = jnp.concatenate((piece, jnp.zeros((16, 128), F32)), axis=0)
        kept = wp[8 * s + n, :, 128:256].astype(F32)
        lanes = lax.broadcasted_iota(jnp.int32, (24, 128), 1)
        wp[8 * s + n, :, 128:256] = jnp.where(lanes < 64, kept, rest).astype(BF)
    loop(1, FS, lambda d: wq_copy(d).start())

    def input_part(d):
        b = lax.rem(s + d, SP)
        value = dot_nt(g[span(b), :], wqkv[...])

        @pl.when(d < SP)
        def _():
            st[span(b), :] = value.astype(BF)
            rs_copy(d).start()

        @pl.when(d == SP)
        def _():
            own[...] = value

    def rs_copy(d):
        to = lax.rem(s + d, SP)
        src = st.at[pl.ds(to * rows, rows)]
        return remote(src, rb.at[d - 1], rs_s.at[d - 1], rs_r.at[d - 1], sp=to)

    loop(1, SP + 1, input_part)

    loop(1, FS, lambda d: wk_copy(d).wait())
    wk_fin[s] = add_up(wk_rb, wk[f].astype(F32)).astype(BF)
    loop(1, SP, lambda d: sp_copy(2, wk_fin)(d).start())
    for e, buf in early_bufs:
        loop(1, SP, lambda d: sp_copy(e, buf)(d).wait())
    for n in range(SP):
        upg[:, 768 * n : 768 * n + 768] = up_fin[n].astype(F32)
    vecg[...] = v_fin[0] + v_fin[1] + v_fin[2] + v_fin[3]
    down_total = dn_fin[0].astype(F32)
    out_total = ou_fin[0].astype(F32)
    for n in range(1, SP):
        down_total = down_total + dn_fin[n].astype(F32)
        out_total = out_total + ou_fin[n].astype(F32)
    dng[...] = down_total
    outg[...] = out_total

    loop(1, SP, lambda d: rs_copy(d).wait())
    total = gfs[...] + own[...]
    for d in range(SP - 1):
        total = total + rb[d].astype(F32)
    input_grad[...] = total

    loop(1, FS, lambda d: wq_copy(d).wait())
    wq_fin[s] = add_up(wq_rb, wp[f].astype(F32)).astype(BF)
    loop(1, SP, lambda d: sp_copy(3, wq_fin)(d).start())
    loop(1, SP, lambda d: sp_copy(2, wk_fin)(d).wait())
    wkg[...] = wk_fin[...].astype(F32)
    loop(1, SP, lambda d: sp_copy(3, wq_fin)(d).wait())
    wqg[...] = wq_fin[...].astype(F32)


def on_device(
    hidden_in,
    qkv_weight,
    query_bias,
    value_bias,
    output_weight,
    output_bias,
    first_gain,
    first_shift,
    up_weight,
    up_bias,
    down_weight,
    down_bias,
    second_gain,
    second_shift,
    valid_length,
    out_cotangent,
):
    s = lax.axis_index("sp")
    rows, width = hidden_in.shape
    tall = SP * rows
    slim = qkv_weight.shape[0]
    deep = down_weight.shape[0]
    share = up_weight.shape[1] // SP
    cols = LH * HEAD_DIM * 3
    vmem = pl.BlockSpec(memory_space=pltpu.VMEM)
    hbm = pl.BlockSpec(memory_space=pl.ANY)
    dma = pltpu.SemaphoreType.DMA
    shape = jax.ShapeDtypeStruct

    parts = qkv_weight.reshape(slim, 3, SP, LH, HEAD_DIM)
    parts = lax.dynamic_index_in_dim(parts, s, 2, keepdims=False)
    kv_cols = jnp.stack((parts[:, 1], parts[:, 2]), axis=2).reshape(slim, -1)
    wq = jnp.concatenate((kv_cols, parts[:, 0].reshape(slim, -1)), axis=1)
    up = lax.dynamic_slice_in_dim(up_weight, s * share, share, 1)
    riders = jnp.stack(
        (
            query_bias, value_bias, output_bias, first_gain, first_shift, down_bias,
            second_gain, second_shift,
        )
    )
    riders = jnp.pad(riders, ((0, slim - 8), (0, 64 - slim)))
    riders = lax.dynamic_update_slice(riders, up_bias.reshape(4, slim), (8, 0))
    wq = jnp.concatenate((wq, riders), axis=1)
    smem = pl.BlockSpec(memory_space=pltpu.SMEM)
    hid_all, wqkv, q_all, kv_all, o_all, out_g, up_g, wdn, vecs = pl.pallas_call(
        forward_kernel,
        out_shape=(
            shape((tall, width), BF),
            shape((width, cols), BF),
            shape((YG, LH, tall, 128), BF),
            shape((XG, LH, tall, 128), BF),
            shape((YG, LH, tall, 128), BF),
            shape((8, slim, width), BF),
            shape((FS, slim, share), BF),
            shape((share, width), BF),
            shape((16, width), F32),
        ),
        in_specs=[smem] + [vmem] * 5,
        out_specs=(vmem, vmem, vmem, vmem, vmem, hbm, vmem, vmem, vmem),
        scratch_shapes=[
            pltpu.VMEM((FS, slim, cols + 64), BF),
            pltpu.VMEM((width, cols), F32),
            pltpu.VMEM((LH, tall, 128), BF),
            pltpu.VMEM((LH, tall, 128), BF),
            pltpu.VMEM((8, width), F32),
            pltpu.VMEM((YG, LH, tall, 128), F32),
            pltpu.VMEM((YG, LH, tall, 128), BF),
        ]
        + [dma((n,)) for n in (3, 3, 31, 31, 8, 8, 3, 3, 7, 7)]
        + [dma((3, 3)), dma((3, 3)), dma((1,))]
        + [dma((7,)), dma((7,)), dma((3, 2)), dma((3, 2)), dma((8,)), dma((8,))],
        compiler_params=pltpu.CompilerParams(
            collective_id=0, has_side_effects=True, vmem_limit_bytes=VMEM_LIMIT
        ),
        name="forward",
    )(valid_length, hidden_in, wq, output_weight, up, down_weight)

    result, gfs, d_all, ld_all, dup, ddn, dwo, vp = pl.pallas_call(
        middle_kernel,
        out_shape=(
            shape((rows, width), BF),
            shape((rows, width), F32),
            shape((YG, LH, tall, 128), BF),
            shape((YG, 8, tall), F32),
            shape((FS, slim, share), BF),
            shape((share, width), BF),
            shape((LH * HEAD_DIM, width), BF),
            shape((FS, 16, 128), F32),
        ),
        in_specs=[vmem] * 7,
        out_specs=(vmem, vmem, hbm, hbm, vmem, vmem, vmem, vmem),
        scratch_shapes=[
            pltpu.VMEM((width, share), F32),
            pltpu.VMEM((LH * 128, width), BF),
            pltpu.VMEM((width, share), BF),
            pltpu.VMEM((tall, LH * 128), BF),
            pltpu.VMEM((tall, 128), F32),
            pltpu.VMEM((3, tall, width), BF),
            pltpu.VMEM((rows, width), F32),
            pltpu.VMEM((rows, width), F32),
            pltpu.VMEM((rows, width), F32),
            pltpu.VMEM((rows, 128), F32),
            pltpu.VMEM((tall, width), BF),
            pltpu.VMEM((tall, share), BF),
            pltpu.VMEM((tall, share), F32),
            pltpu.VMEM((tall, width), BF),
            pltpu.VMEM((tall, share), BF),
            pltpu.VMEM((tall, width), BF),
            pltpu.VMEM((rows, width), F32),
            pltpu.VMEM((3, SP - 1, rows, width), BF),
            pltpu.VMEM((LH, tall, 128), BF),
            pltpu.VMEM((8, tall), F32),
            pltpu.VMEM((8, width), F32),
        ]
        + [dma((3, 3)) for _ in range(4)]
        + [dma((3, 4)), dma((3, 4)), dma((3,)), dma((3,)), dma((2,))],
        compiler_params=pltpu.CompilerParams(
            collective_id=1, has_side_effects=True, vmem_limit_bytes=VMEM_LIMIT
        ),
        name="middle",
    )(
        o_all, out_g, up_g, wdn, vecs,
        hidden_in, out_cotangent,
    )

    input_grad, wkg, wqg, upg, dng, outg, vecg = pl.pallas_call(
        backward_kernel,
        out_shape=(
            shape((rows, width), F32),
            shape((SP, slim, 2 * LH * HEAD_DIM), F32),
            shape((SP, slim, 256), F32),
            shape((slim, SP * share), F32),
            shape((deep, width), F32),
            shape((slim, width), F32),
            shape((16, 128), F32),
        ),
        in_specs=[smem] + [vmem] * 11,
        out_specs=(vmem,) * 7,
        scratch_shapes=[
            pltpu.VMEM((YG, LH, HEAD_DIM, tall), F32),
            pltpu.VMEM((YG, LH * HEAD_DIM, tall), BF),
            pltpu.VMEM((XG, LH, tall, 128), BF),
            pltpu.VMEM((XG - 1, LH, tall, 128), BF),
            pltpu.VMEM((YG - 1, LH * HEAD_DIM, tall), BF),
            pltpu.VMEM((tall, cols), BF),
            pltpu.VMEM((width, 640), F32),
            pltpu.VMEM((FS, slim, 384), BF),
            pltpu.VMEM((FS, slim, 256), BF),
            pltpu.VMEM((tall, width), BF),
            pltpu.VMEM((rows, width), F32),
            pltpu.VMEM((SP - 1, rows, width), BF),
            pltpu.VMEM((FS - 1, slim, 384), BF),
            pltpu.VMEM((FS - 1, slim, 256), BF),
            pltpu.VMEM((YG - 1, 2, YG, slim, share), BF),
            pltpu.VMEM((8, deep, width), BF),
            pltpu.VMEM((8, slim, share), BF),
            pltpu.VMEM((XG - 1, slim, share), BF),
            pltpu.VMEM((8, slim, width), BF),
            pltpu.VMEM((FS - 1, 16, 128), F32),
            pltpu.VMEM((SP, slim, share), BF),
            pltpu.VMEM((SP, deep, width), BF),
            pltpu.VMEM((SP, slim, width), BF),
            pltpu.VMEM((SP, 16, 128), F32),
            pltpu.VMEM((SP, slim, 384), BF),
            pltpu.VMEM((SP, slim, 256), BF),
        ]
        + [dma((7, LH)), dma((7, LH)), dma((YG - 1, LH)), dma((YG - 1, LH))]
        + [dma((n,)) for n in (31, 31, 31, 31, 7, 7, 8, 8, 31, 31, 3, 3)]
        + [dma((6, 3)), dma((6, 3)), dma((3, 2)), dma((3, 2)), dma((8,)), dma((8,))],
        compiler_params=pltpu.CompilerParams(
            collective_id=2, has_side_effects=True, vmem_limit_bytes=VMEM_LIMIT
        ),
        name="backward",
    )(
        valid_length, q_all, d_all, ld_all, kv_all, hid_all, wqkv, gfs,
        dup, ddn, dwo.reshape(8, slim, width), vp,
    )

    kv_grad = wkg.reshape(SP, slim, LH, 2, HEAD_DIM)
    q_grad = wqg[:, :, : LH * HEAD_DIM].reshape(SP, slim, LH, 1, HEAD_DIM)
    qkv_grad = jnp.concatenate((q_grad, kv_grad), axis=3)
    qkv_grad = jnp.transpose(qkv_grad, (1, 3, 0, 2, 4)).reshape(slim, -1)
    qv_grad = jnp.sum(wqg[:, 0:2, LH * HEAD_DIM : LH * HEAD_DIM + slim], axis=0)
    return (
        result,
        input_grad,
        qkv_grad,
        qv_grad[0],
        qv_grad[1],
        outg,
        vecg[0, :slim],
        vecg[1, :slim],
        vecg[2, :slim],
        upg,
        vecg[8, :deep],
        dng,
        vecg[3, :slim],
        vecg[4, :slim],
        vecg[5, :slim],
    )


def solution(mesh):
    placed = (
        P(("fsdp", "sp"), None),
        P("fsdp", None),
        P("fsdp"),
        P("fsdp"),
        P("fsdp", None),
        P("fsdp"),
        P("fsdp"),
        P("fsdp"),
        P("fsdp", None),
        P("fsdp"),
        P("fsdp", None),
        P("fsdp"),
        P("fsdp"),
        P("fsdp"),
        P(),
        P(("fsdp", "sp"), None),
    )
    return jax.shard_map(
        on_device,
        mesh=mesh,
        in_specs=placed,
        out_specs=(
            P(("fsdp", "sp"), None),
            P(("fsdp", "sp"), None),
            P("fsdp", None),
            P("fsdp"),
            P("fsdp"),
            P("fsdp", None),
            P("fsdp"),
            P("fsdp"),
            P("fsdp"),
            P("fsdp", None),
            P("fsdp"),
            P("fsdp", None),
            P("fsdp"),
            P("fsdp"),
            P("fsdp"),
        ),
        check_vma=False,
    )
```
